128 devices in a mesh: ti: 16 (over z, x), kz: 8 (over y, core).
Axes of the slice: x: 4, y: 4, z: 4, core: 2. Of those that a mesh axis runs over, the one named last changes fastest.
Arguments:
- point_maps: float32 [3, 8, 160, 256], P(None, None, 'kz'), may hold values from 0.3 to 3, as said below
- point_coils: float32 [2, 8, 8, 160, 256], P(None, None, None, 'kz'), may hold values from -2 to 2
- direction_maps: float32 [3, 8, 160, 256], P(None, None, 'kz', 'ti'), may hold values from -12 to 12
- direction_coils: float32 [2, 8, 8, 160, 256], P(None, None, None, 'kz', 'ti'), may hold values from -12 to 12
- residual_maps: float32 [3, 8, 160, 256], P(None, None, 'kz', 'ti'), may hold values from -12 to 12
- residual_coils: float32 [2, 8, 8, 160, 256], P(None, None, None, 'kz', 'ti'), may hold values from -12 to 12
- inversion_times: float32 [32], P('ti'), may hold values from 0.05 to 3
- sampling_mask: int32 [32, 160, 256], P('ti'), may hold values 0 or 1
Outputs:
- new_residual_maps: float32 [3, 8, 160, 256], P(None, None, 'kz', 'ti')
- new_residual_coils: float32 [2, 8, 8, 160, 256], P(None, None, None, 'kz', 'ti')
- new_direction_maps: float32 [3, 8, 160, 256], P(None, None, 'kz', 'ti')
- new_direction_coils: float32 [2, 8, 8, 160, 256], P(None, None, None, 'kz', 'ti')
The draws below stay inside these ranges and needn't reach their ends.
Inputs may be any that keep to these rules, and one draw needn't show every extreme that they name: `sampling_mask`: 1 where the sample of that bin was acquired. `point_maps`: component 1 lies between 1.4 and 2 times component 0.
All inputs are finite; a program needn't handle non-finite values. No bound on the sum of `sampling_mask` on one device may be relied on, other than what follows from the above.
Results may differ from the reference program's by a relative error of at most 0.0003.
Values sent between devices are 32-bit elements; how exact they have to be, the bound alone decides.
No kernel may reach another device: no remote copies, remote signals or barrier semaphores. Data moves between devices by JAX's collectives and lax.ppermute only.
A program may use at most 128 MiB of HBM per device.

```python
import math
import jax
import jax.numpy as jnp
from jax import lax

COILS = 8
NY = 256
NZ = 160
BINS = 32
XS = 8


def ramp_scale(shape, power):
    zcoord = lax.broadcasted_iota(jnp.float32, shape, len(shape) - 2) / shape[-2]
    ycoord = lax.broadcasted_iota(jnp.float32, shape, len(shape) - 1) / shape[-1]
    return 10.0 ** (power * (zcoord + ycoord))


def drawn_field(key, shape):
    noise = jax.random.truncated_normal(key, -4.0, 4.0, shape, jnp.float32)
    return noise * ramp_scale(shape, 0.5) * 0.3


def draw_point_maps(key, part):
    key = jax.random.fold_in(key, 21)
    first_key, second_key, third_key = jax.random.split(key, 3)
    shape = (XS, NZ, NY)
    density = jax.random.uniform(first_key, shape, jnp.float32, 0.5, 1.5)
    amplitude = density * jax.random.uniform(second_key, shape, jnp.float32, 1.4, 2.0)
    relax_rate = jnp.exp(jax.random.uniform(third_key, shape, jnp.float32, jnp.log(0.3), jnp.log(3.0)))
    return jnp.stack([density, amplitude, relax_rate])


def draw_direction_maps(key, part):
    key = jax.random.fold_in(key, 31)
    return drawn_field(key, (3, XS, NZ, NY))


def draw_direction_coils(key, part):
    key = jax.random.fold_in(key, 41)
    return drawn_field(key, (2, COILS, XS, NZ, NY))


def draw_residual_maps(key, part):
    key = jax.random.fold_in(key, 51)
    return drawn_field(key, (3, XS, NZ, NY))


def draw_residual_coils(key, part):
    key = jax.random.fold_in(key, 61)
    return drawn_field(key, (2, COILS, XS, NZ, NY))


def with_ends(values, key, low, largest):
    longest = values.shape.index(max(values.shape))
    spots = []
    for shift in (0, 1):
        where = [jax.random.randint(jax.random.fold_in(key, axis), (), 0, length) for axis, length in enumerate(values.shape)]
        where[longest] = (where[longest] + shift) % values.shape[longest]
        spots.append(tuple(where))
    return values.at[spots[0]].set(low).at[spots[1]].set(largest)


def level_of(stream_key, extent, cuts, low, top_value):
    level, own = 1.0, jax.random.fold_in(stream_key, 6)
    for position, parts in cuts:
        draws = jnp.exp(jax.random.uniform(jax.random.fold_in(own, position), (parts,), jnp.float32, low / len(cuts), top_value / len(cuts)))
        level = level * jnp.repeat(draws, extent[position] // parts).reshape([-1 if axis == position else 1 for axis in range(len(extent))])
    return level


def normal_values(key, dims, width, limit, pieces=(), dtype=jnp.bfloat16):
    values = width * jax.random.normal(key, dims, jnp.float32)
    if pieces:
        values = values * level_of(key, dims, pieces, -0.22, 0.18)
    return jnp.clip(values, -limit, limit).astype(dtype)


def setup_inputs(seed: int = 0) -> dict:
    streams_of = jax.random.split(jax.random.key(seed), 9)
    point_maps = draw_point_maps(jax.random.fold_in(streams_of[8], 71), 0)
    point_coils = normal_values(streams_of[1], (2, COILS, XS, NZ, NY), 0.35, 2.0, ((3, 8),), jnp.float32)
    direction_maps = draw_direction_maps(jax.random.fold_in(streams_of[8], 71), 0)
    direction_coils = draw_direction_coils(jax.random.fold_in(streams_of[8], 71), 0)
    residual_maps = draw_residual_maps(jax.random.fold_in(streams_of[8], 71), 0)
    residual_coils = draw_residual_coils(jax.random.fold_in(streams_of[8], 71), 0)
    inversion_times = jnp.clip(jnp.exp(math.log(3.0) - 4.0943445 * jax.random.uniform(streams_of[6], (BINS,), jnp.float32) ** level_of(streams_of[6], (BINS,), ((0, 16),), -0.2, 0.2)), 0.05, 3.0)
    sampling_mask = with_ends((jax.random.randint(streams_of[7], (BINS, NZ, NY), 0, 3) < 1).astype(jnp.int32), jax.random.fold_in(streams_of[7], 1), 0, 1)
    return {"point_maps": point_maps, "point_coils": point_coils, "direction_maps": direction_maps, "direction_coils": direction_coils, "residual_maps": residual_maps, "residual_coils": residual_coils, "inversion_times": inversion_times, "sampling_mask": sampling_mask}


regular_weight = 2.0


def reference(point_maps, point_coils, direction_maps, direction_coils, residual_maps, residual_coils, inversion_times, sampling_mask):
    density = point_maps[0]
    amplitude = point_maps[1]
    relax_rate = point_maps[2]
    coil_map = point_coils[0] + 1j * point_coils[1]
    coil_step = direction_coils[0] + 1j * direction_coils[1]

    def per_bin(totals, inputs):
        bin_time, bin_mask = inputs
        decays = jnp.exp(-bin_time * relax_rate)
        signal = density - amplitude * decays
        signal_step = direction_maps[0] - direction_maps[1] * decays + amplitude * bin_time * decays * direction_maps[2]
        images = coil_map * signal_step[None] + coil_step * signal[None]
        kspace = jnp.fft.fft2(images, axes=(-2, -1), norm="ortho") * bin_mask.astype(jnp.float32)[None, None]
        returned = jnp.fft.ifft2(kspace, axes=(-2, -1), norm="ortho")
        back_re = jnp.real(returned)
        back_im = jnp.imag(returned)
        projected = jnp.sum(point_coils[0] * back_re + point_coils[1] * back_im, axis=0)
        g_density, g_amplitude, g_rate, g_real, g_imag = totals
        return (g_density + projected,
                g_amplitude - decays * projected,
                g_rate + amplitude * bin_time * decays * projected,
                g_real + signal[None] * back_re,
                g_imag + signal[None] * back_im), None

    zero_map = jnp.zeros(density.shape, jnp.float32)
    zero_coil = jnp.zeros(point_coils.shape[1:], jnp.float32)
    totals, unused = lax.scan(per_bin, (zero_map, zero_map, zero_map, zero_coil, zero_coil), (inversion_times, sampling_mask))
    applied_maps = jnp.stack([totals[0], totals[1], totals[2]]) + regular_weight * direction_maps
    applied_coils = jnp.stack([totals[3], totals[4]]) + regular_weight * direction_coils
    old_norm = jnp.sum(residual_maps * residual_maps) + jnp.sum(residual_coils * residual_coils)
    curvature = jnp.sum(direction_maps * applied_maps) + jnp.sum(direction_coils * applied_coils)
    step_size = old_norm / curvature
    new_residual_maps = residual_maps - step_size * applied_maps
    new_residual_coils = residual_coils - step_size * applied_coils
    new_norm = jnp.sum(new_residual_maps * new_residual_maps) + jnp.sum(new_residual_coils * new_residual_coils)
    conjugacy = new_norm / old_norm
    new_direction_maps = new_residual_maps + conjugacy * direction_maps
    new_direction_coils = new_residual_coils + conjugacy * direction_coils
    return new_residual_maps, new_residual_coils, new_direction_maps, new_direction_coils
```

```python
import math

import jax
import jax.numpy as jnp
import numpy as np
from jax import lax
from jax.experimental import pallas as pl
from jax.experimental.pallas import tpu as pltpu
from jax.sharding import PartitionSpec as P

regular_weight = 2.0
AXES = ("ti", "kz")
NZ, NY, ZB, YB, XS = 160, 256, 20, 16, 8
HALF_Z, HALF_Y = NZ // 2, NY // 2
LANES = 128
TILES = 18
MSG = TILES * LANES
HALF_MSG = MSG // 2
POINT_ROWS = 9
FEATURES = 7
VMEM_LIMIT = 50 * 1024 * 1024
f32 = jnp.float32
bf16 = jnp.bfloat16


def split_pair(table):
    high = table.astype(np.float32).astype(jnp.bfloat16)
    low = (table - high.astype(np.float64)).astype(np.float32).astype(jnp.bfloat16)
    return high, low


def real_form(matrix):
    return np.block([[matrix.real, matrix.imag], [-matrix.imag, matrix.real]])


def right_table(table):
    high, low = split_pair(table)
    return np.concatenate([high, high, low], axis=0)


def left_table(table):
    high, low = split_pair(table)
    pad = np.zeros((table.shape[0], 32), dtype=jnp.bfloat16)
    return np.concatenate([high, high, low, pad], axis=1)


def z_of_rows():
    rows = np.arange(HALF_Z)
    return (rows % 8) * ZB + 2 * (rows // 8)


def make_tables():
    n, m = np.arange(HALF_Y)[:, None], np.arange(HALF_Y)[None, :]
    y_even = real_form(np.exp(-2j * np.pi * (n * (2 * m) % NY) / NY) / math.sqrt(NY))
    y_odd = real_form(np.exp(-2j * np.pi * (n * (2 * m + 1) % NY) / NY) / math.sqrt(NY))
    spots, freq = z_of_rows()[None, :], np.arange(HALF_Z)[:, None]
    z_even = real_form((np.exp(-2j * np.pi * (freq * spots % NZ) / NZ) / math.sqrt(NZ)).T).T
    z_odd = real_form((np.exp(-2j * np.pi * (freq * (spots + 1) % NZ) / NZ) / math.sqrt(NZ)).T).T
    forward_y = np.stack([right_table(y_even), right_table(y_odd)])
    backward_y = np.stack([right_table(y_even.T), right_table(y_odd.T)])
    forward_z = np.stack([left_table(z_even), left_table(z_odd)])
    backward_z = np.stack([left_table(z_even.T), left_table(z_odd.T)])
    order = np.zeros((NY, NY), dtype=jnp.bfloat16)
    for lane in range(NY):
        order[2 * (lane % HALF_Y) + lane // HALF_Y, lane] = 1
    return forward_y, forward_z, backward_y, backward_z, order


def iota(shape, axis):
    return lax.broadcasted_iota(jnp.int32, shape, axis)


def block_transpose(tiles):
    group = iota((8, LANES), 1) >> 4
    tiles = list(tiles)
    for bit in (1, 2, 4):
        unset = (group & bit) == 0
        for i in range(8):
            if i & bit:
                continue
            a, c = tiles[i], tiles[i | bit]
            tiles[i] = jnp.where(unset, a, pltpu.roll(c, 16 * bit, 1))
            tiles[i | bit] = jnp.where(unset, pltpu.roll(a, LANES - 16 * bit, 1), c)
    return tiles


def inner_transpose(tile):
    group, row = iota((8, LANES), 1) >> 4, iota((8, LANES), 0)
    for bit in (1, 2, 4):
        g, s = (group & bit) != 0, (row & bit) != 0
        down = pltpu.roll(pltpu.roll(tile, bit, 0), LANES - 16 * bit, 1)
        up = pltpu.roll(pltpu.roll(tile, 8 - bit, 0), 16 * bit, 1)
        tile = jnp.where(g == s, tile, jnp.where(s, down, up))
    return tile


def pair_of(tile, member):
    if tile < 2 * FEATURES:
        return tile // 2, 8 * (tile % 2) + member
    feature = 2 * (tile - 2 * FEATURES) + member // 4
    return (feature, 16 + member % 4) if feature < FEATURES else None


def row_of(z):
    return (z & 1) * HALF_Z + (z >> 1) * 8


def halves(values):
    high = values.astype(bf16)
    return high, (values - high.astype(f32)).astype(bf16)


def times_right(values, table):
    high, low = halves(values)
    return jnp.dot(jnp.concatenate([high, low, high], axis=1), table, preferred_element_type=f32)


def times_left(table, values):
    high, low = halves(values)
    pad = jnp.zeros((32, values.shape[1]), bf16)
    return jnp.dot(table, jnp.concatenate([high, low, high, pad], axis=0), preferred_element_type=f32)


def pack_kernel(place, times, maps, coils, point_maps, point_coils, send, dense):
    t = place[0]
    row, lane = iota((8, LANES), 0), iota((8, LANES), 1)
    even = (row & 1) == 0
    for f in range(3 + 2 * 8):
        block = maps[f] if f < 3 else coils[(f - 3) // 8, (f - 3) % 8]
        turned = jnp.swapaxes(block.reshape(8 * YB, ZB), 0, 1)
        turned = jnp.concatenate([turned, turned[:4]], axis=0)
        for a in range(3):
            dense[f, a] = inner_transpose(turned[8 * a : 8 * a + 8])
    own_times = jnp.where(lane == 64, times[0], jnp.where(lane == 65, times[1], 0.0))
    for g in range(4):
        names = [0, 1, 2] + [3 + 8 * p + 2 * g + e for p in range(2) for e in range(2)]
        for u in range(TILES):
            if u < 2 * FEATURES:
                direction = dense[names[u // 2], u % 2]
            else:
                f = 2 * (u - 2 * FEATURES)
                upper = own_times if f + 1 == FEATURES else pltpu.roll(dense[names[f + 1], 2], 64, 1)
                direction = jnp.where(lane < 64, dense[names[f], 2], upper)
            item = jnp.minimum(t * POINT_ROWS + u // 2, FEATURES * ZB - 1)
            f = item // ZB
            z = item - f * ZB
            side = slice((u % 2) * LANES, (u % 2 + 1) * LANES)
            q = jnp.maximum(f - 3, 0)
            of_maps = point_maps[jnp.minimum(f, 2), z, :, side]
            of_coils = point_coils[q // 2, 2 * g + q % 2, z, :, side]
            point = jnp.where(f < 3, of_maps, of_coils)
            for h in range(2):
                if h == 0:
                    tile = jnp.where(even, direction, pltpu.roll(point, 1, 0))
                else:
                    tile = jnp.where(even, pltpu.roll(direction, 7, 0), point)
                for upper_z in range(2):
                    target = (2 * upper_z + g // 2) * 4 + 2 * (g % 2) + h
                    send[8 * target : 8 * target + 8, u * LANES : (u + 1) * LANES] = tile


def forward_kernel(place, own, other, table_y, table_z, spectrum, point, taus, direction, stamps):
    step = pl.program_id(0)
    t, core = place[0], place[1]

    def unpack(of_direction, of_point):
        for half in range(2):
            for u in range(TILES):
                side = slice(u * LANES, (u + 1) * LANES)
                tiles = [of_direction[8 * (8 * half + i) : 8 * (8 * half + i) + 8, side] for i in range(8)]
                for member, tile in enumerate(block_transpose(tiles)):
                    pair = pair_of(u, member)
                    if pair is not None:
                        f, z = pair
                        direction[f, row_of(z) : row_of(z) + 8, half * LANES : (half + 1) * LANES] = tile
        for item in range(FEATURES * ZB):
            source, i = item // POINT_ROWS, item % POINT_ROWS
            f, z = item // ZB, item % ZB
            point[f, row_of(z) : row_of(z) + 8, :] = of_point[8 * source : 8 * source + 8, i * NY : (i + 1) * NY]
        stamps[...] = of_direction[:, MSG - LANES : MSG]

    @pl.when((step == 0) & (core == 0))
    def _():
        unpack(own, other)

    @pl.when((step == 0) & (core == 1))
    def _():
        unpack(other, own)

    bin_of = (((t >> 2) ^ (step >> 2)) << 2) | ((t + step) & 3)
    block = stamps[pl.ds(pl.multiple_of(bin_of * 8, 8), 8), :]
    chosen = (iota((8, LANES), 0) == 0) & (iota((8, LANES), 1) == 64 + core)
    tau = jnp.sum(jnp.where(chosen, block, 0.0), axis=(0, 1), keepdims=True)
    taus[0] = jnp.broadcast_to(tau, (8, LANES))

    decays = jnp.exp(-tau * point[2])
    signal = point[0] - point[1] * decays
    change = direction[0] - direction[1] * decays + point[1] * tau * decays * direction[2]
    evens, odds = [], []
    for c in range(2):
        re = point[3 + c] * change + direction[3 + c] * signal
        im = point[5 + c] * change + direction[5 + c] * signal
        re_low, re_high, im_low, im_high = re[:, :HALF_Y], re[:, HALF_Y:], im[:, :HALF_Y], im[:, HALF_Y:]
        evens.append(jnp.concatenate([re_low + re_high, im_low + im_high], axis=1))
        odds.append(jnp.concatenate([re_low - re_high, im_low - im_high], axis=1))
    along_even = times_right(jnp.concatenate(evens, axis=0), table_y[0])
    along_odd = times_right(jnp.concatenate(odds, axis=0), table_y[1])
    for c in range(2):
        parts = []
        for parity in range(2):
            rows = slice(c * NZ + parity * HALF_Z, c * NZ + (parity + 1) * HALF_Z)
            re = jnp.concatenate([along_even[rows, :HALF_Y], along_odd[rows, :HALF_Y]], axis=1)
            im = jnp.concatenate([along_even[rows, HALF_Y:], along_odd[rows, HALF_Y:]], axis=1)
            parts.append(times_left(table_z[parity], jnp.concatenate([re, im], axis=0)))
        for part in range(2):
            a = parts[0][part * HALF_Z : (part + 1) * HALF_Z]
            b = parts[1][part * HALF_Z : (part + 1) * HALF_Z]
            spectrum[0, c, part, :HALF_Z] = a + b
            spectrum[0, c, part, HALF_Z:] = a - b


def backward_kernel(place, *refs):
    masks, refs = refs[:8], refs[8:]
    spectrum, point, taus, table_y, table_z, order, mine, theirs, total, sent, weight = refs
    step = pl.program_id(0)
    core = place[1]
    for s in range(8):

        @pl.when(step == s)
        def _():
            weight[...] = jnp.dot(masks[s][...].astype(f32).astype(bf16), order[...], preferred_element_type=f32)

    @pl.when(step == 0)
    def _():
        total[...] = jnp.zeros_like(total)

    tau = taus[0, 0:1, 0:1]
    weights = weight[...]
    evens, odds = [], []
    for c in range(2):
        plus, minus = [], []
        for part in range(2):
            values = spectrum[0, c, part] * weights
            plus.append(values[:HALF_Z] + values[HALF_Z:])
            minus.append(values[:HALF_Z] - values[HALF_Z:])
        for side in (plus, minus):
            out = times_left(table_z[0 if side is plus else 1], jnp.concatenate(side, axis=0))
            re, im = out[:HALF_Z], out[HALF_Z:]
            evens.append(jnp.concatenate([re[:, :HALF_Y], im[:, :HALF_Y]], axis=1))
            odds.append(jnp.concatenate([re[:, HALF_Y:], im[:, HALF_Y:]], axis=1))
    from_even = times_right(jnp.concatenate(evens, axis=0), table_y[0])
    from_odd = times_right(jnp.concatenate(odds, axis=0), table_y[1])
    low, high = from_even + from_odd, from_even - from_odd

    decays = jnp.exp(-tau * point[2])
    signal = point[0] - point[1] * decays
    projected = None
    for c in range(2):
        rows = slice(c * NZ, (c + 1) * NZ)
        re = jnp.concatenate([low[rows, :HALF_Y], high[rows, :HALF_Y]], axis=1)
        im = jnp.concatenate([low[rows, HALF_Y:], high[rows, HALF_Y:]], axis=1)
        term = point[3 + c] * re + point[5 + c] * im
        projected = term if projected is None else projected + term
        total[3 + c] += signal * re
        total[5 + c] += signal * im
    total[0] += projected
    faded = decays * projected
    total[1] -= faded
    total[2] += point[1] * (tau * faded)

    @pl.when(step == 7)
    def _():
        for half in range(2):
            for u in range(TILES):
                tiles = []
                for member in range(8):
                    pair = pair_of(u, member)
                    f, z = pair if pair is not None else (0, 0)
                    tiles.append(total[f, row_of(z) : row_of(z) + 8, half * LANES : (half + 1) * LANES])
                slot = core if u < TILES // 2 else 1 - core
                lane = (u % (TILES // 2)) * LANES
                for i, tile in enumerate(block_transpose(tiles)):
                    target = 8 * (8 * half + i)
                    sent[slot, target : target + 8, lane : lane + LANES] = tile
        mine[...] = sent[0]
        theirs[...] = sent[1]


def sums_kernel(received, dir_maps, dir_coils, res_maps, res_coils, out_maps, out_coils, out_sums):
    row, lane = iota((8, LANES), 0), iota((8, LANES), 1)
    even = (row & 1) == 0
    half_tiles = TILES // 2

    def piece(h, g, u):
        total = None
        for upper_z in range(2):
            source = (2 * upper_z + g // 2) * 4 + 2 * (g % 2) + h
            tile = received[8 * source : 8 * source + 8, u * LANES : (u + 1) * LANES]
            total = tile if total is None else total + tile
        return total

    def whole(groups, tile):
        u = tile % half_tiles
        sides = []
        for h in range(2):
            total = None
            for g in groups:
                term = piece(h, g, u)
                total = term if total is None else total + term
            sides.append(total)
        if tile < half_tiles:
            return jnp.where(even, sides[0], pltpu.roll(sides[1], 1, 0))
        return jnp.where(even, pltpu.roll(sides[0], 7, 0), sides[1])

    def feature(groups, f):
        last = whole(groups, 2 * FEATURES + f // 2)
        if f % 2:
            last = pltpu.roll(last, 64, 1)
        stack = [inner_transpose(tile) for tile in (whole(groups, 2 * f), whole(groups, 2 * f + 1), last)]
        turned = jnp.swapaxes(jnp.concatenate(stack, axis=0), 0, 1)
        return turned[:, :ZB].reshape(XS, YB, ZB)

    sums = [jnp.zeros((XS, YB, ZB), f32) for _ in range(4)]
    for f in range(3 + 16):
        if f < 3:
            gradient = feature(range(4), f)
            direction, residual = dir_maps[f], res_maps[f]
        else:
            part, coil = (f - 3) // 8, (f - 3) % 8
            gradient = feature([coil // 2], 3 + 2 * part + coil % 2)
            direction, residual = dir_coils[part, coil], res_coils[part, coil]
        applied = gradient + regular_weight * direction
        if f < 3:
            out_maps[f] = applied
        else:
            out_coils[part, coil] = applied
        for i, (a, b) in enumerate(
            ((residual, residual), (direction, applied), (residual, applied), (applied, applied))
        ):
            sums[i] = sums[i] + a * b
    line = jnp.zeros((1, LANES), f32)
    for i in range(4):
        value = jnp.sum(jnp.sum(sums[i], axis=0), axis=(0, 1), keepdims=True)
        line = jnp.where(iota((1, LANES), 1) == i, value, line)
    out_sums[...] = jnp.broadcast_to(line, (LANES, LANES))


def step_kernel(sums, app_maps, app_coils, dir_maps, dir_coils, res_maps, res_coils, *outs):
    line = jnp.sum(sums[...], axis=0, keepdims=True)
    lane = iota((1, LANES), 1)
    old, curve, cross, square = (
        jnp.sum(jnp.where(lane == i, line, 0.0), axis=1, keepdims=True) for i in range(4)
    )
    size = old / curve
    new = old - 2.0 * size * cross + size * size * square
    ratio = (new / old).reshape(1, 1, 1)
    size = size.reshape(1, 1, 1)
    for f in range(3):
        fresh = res_maps[f] - size * app_maps[f]
        outs[0][f] = fresh
        outs[2][f] = fresh + ratio * dir_maps[f]
    for part in range(2):
        for coil in range(8):
            fresh = res_coils[part, coil] - size * app_coils[part, coil]
            outs[1][part, coil] = fresh
            outs[3][part, coil] = fresh + ratio * dir_coils[part, coil]


def struct(*shape):
    return jax.ShapeDtypeStruct(shape, f32)


SMEM = pl.BlockSpec(memory_space=pltpu.SMEM)
VMEM = pl.BlockSpec(memory_space=pltpu.VMEM)


def params():
    return pltpu.CompilerParams(vmem_limit_bytes=VMEM_LIMIT)


def constant_block(shape):
    return pl.BlockSpec(shape, lambda s: (0,) * len(shape))


def stepping_block(shape):
    return pl.BlockSpec((1,) + shape, lambda s: (s,) + (0,) * len(shape))


def core_swap(values):
    return lax.ppermute(values, "kz", [(i, i ^ 1) for i in range(8)])


def shards(
    point_maps,
    point_coils,
    direction_maps,
    direction_coils,
    residual_maps,
    residual_coils,
    inversion_times,
    sampling_mask,
):
    forward_y, forward_z, backward_y, backward_z, order = make_tables()
    t, k = lax.axis_index("ti"), lax.axis_index("kz")
    core = k & 1
    place = jnp.stack([t, core]).astype(jnp.int32)

    own_mask = lax.dynamic_index_in_dim(sampling_mask, core, 0, keepdims=False)
    masks = [own_mask]
    for s in range(1, 8):
        pairs = [((((i >> 2) ^ (s >> 2)) << 2) | ((i + s) & 3), i) for i in range(16)]
        masks.append(lax.ppermute(own_mask, "ti", pairs))

    dir_maps, dir_coils = jnp.swapaxes(direction_maps, 2, 3), jnp.swapaxes(direction_coils, 3, 4)
    res_maps, res_coils = jnp.swapaxes(residual_maps, 2, 3), jnp.swapaxes(residual_coils, 3, 4)
    pnt_maps, pnt_coils = jnp.swapaxes(point_maps, 1, 2), jnp.swapaxes(point_coils, 2, 3)

    send = pl.pallas_call(
        pack_kernel,
        out_shape=struct(128, MSG),
        in_specs=[SMEM, SMEM] + [VMEM] * 4,
        out_specs=VMEM,
        scratch_shapes=[pltpu.VMEM((19, 3, 8, LANES), f32)],
        compiler_params=params(),
        name="pack",
    )(place, inversion_times, dir_maps, dir_coils, pnt_maps, pnt_coils)
    own = lax.all_to_all(send, AXES, 0, 0, tiled=True)
    other = core_swap(own)

    spectrum, point, taus = pl.pallas_call(
        forward_kernel,
        grid=(8,),
        out_shape=(struct(8, 2, 2, NZ, NY), struct(FEATURES, NZ, NY), struct(8, 8, LANES)),
        in_specs=[SMEM]
        + [constant_block(a.shape) for a in (own, other, forward_y, forward_z)],
        out_specs=(stepping_block((2, 2, NZ, NY)), constant_block((FEATURES, NZ, NY)), stepping_block((8, LANES))),
        scratch_shapes=[pltpu.VMEM((FEATURES, NZ, NY), f32), pltpu.VMEM((LANES, LANES), f32)],
        compiler_params=params(),
        name="forward",
    )(place, own, other, jnp.asarray(forward_y), jnp.asarray(forward_z))

    mine, theirs = pl.pallas_call(
        backward_kernel,
        grid=(8,),
        out_shape=(struct(128, HALF_MSG), struct(128, HALF_MSG)),
        in_specs=[SMEM]
        + [constant_block((NZ, NY))] * 8
        + [stepping_block((2, 2, NZ, NY)), constant_block((FEATURES, NZ, NY)), stepping_block((8, LANES))]
        + [constant_block(a.shape) for a in (backward_y, backward_z, order)],
        out_specs=(constant_block((128, HALF_MSG)),) * 2,
        scratch_shapes=[
            pltpu.VMEM((FEATURES, NZ, NY), f32),
            pltpu.VMEM((2, 128, HALF_MSG), f32),
            pltpu.VMEM((NZ, NY), f32),
        ],
        compiler_params=params(),
        name="backward",
    )(place, *masks, spectrum, point, taus, jnp.asarray(backward_y), jnp.asarray(backward_z), jnp.asarray(order))

    summed = mine + core_swap(theirs)
    received = lax.all_to_all(summed, AXES, 0, 0, tiled=True)

    maps_shape, coils_shape = struct(*dir_maps.shape), struct(*dir_coils.shape)
    app_maps, app_coils, sums = pl.pallas_call(
        sums_kernel,
        out_shape=(maps_shape, coils_shape, struct(128, LANES)),
        in_specs=[VMEM] * 5,
        out_specs=(VMEM,) * 3,
        compiler_params=params(),
        name="sums",
    )(received, dir_maps, dir_coils, res_maps, res_coils)
    all_sums = lax.all_to_all(sums.reshape(128, 1, LANES), AXES, 0, 0).reshape(128, LANES)

    outs = pl.pallas_call(
        step_kernel,
        out_shape=(maps_shape, coils_shape, maps_shape, coils_shape),
        in_specs=[VMEM] * 7,
        out_specs=(VMEM,) * 4,
        compiler_params=params(),
        name="step",
    )(all_sums, app_maps, app_coils, dir_maps, dir_coils, res_maps, res_coils)
    return tuple(jnp.swapaxes(out, -2, -1) for out in outs)


def solution(mesh):
    in_specs = (
        P(None, None, "kz", None),
        P(None, None, None, "kz", None),
        P(None, None, "kz", "ti"),
        P(None, None, None, "kz", "ti"),
        P(None, None, "kz", "ti"),
        P(None, None, None, "kz", "ti"),
        P("ti"),
        P("ti", None, None),
    )
    out_specs = (
        P(None, None, "kz", "ti"),
        P(None, None, None, "kz", "ti"),
        P(None, None, "kz", "ti"),
        P(None, None, None, "kz", "ti"),
    )
    return jax.shard_map(shards, mesh=mesh, in_specs=in_specs, out_specs=out_specs, check_vma=False)
```

```python
import math

import jax
import jax.numpy as jnp
import numpy as np
from jax import lax
from jax.experimental import pallas as pl
from jax.experimental.pallas import tpu as pltpu
from jax.sharding import PartitionSpec as P

regular_weight = 2.0
AXES = ("ti", "kz")
NZ, NY, ZB, YB, XS = 160, 256, 20, 16, 8
HALF_Z, HALF_Y = NZ // 2, NY // 2
LANES = 128
FEATURES = 7
PAIRS = FEATURES * ZB
MAIN = 16
TILES = 18
MSG = TILES * LANES
ITEMS = 9
VMEM_LIMIT = 32 * 1024 * 1024
f32 = jnp.float32
bf16 = jnp.bfloat16


def split_pair(table):
    high = table.astype(np.float32).astype(jnp.bfloat16)
    low = (table - high.astype(np.float64)).astype(np.float32).astype(jnp.bfloat16)
    return high, low


def real_form(matrix):
    return np.block([[matrix.real, matrix.imag], [-matrix.imag, matrix.real]])


def right_table(table):
    high, low = split_pair(table)
    return np.concatenate([high, high, low], axis=0)


def left_table(table):
    high, low = split_pair(table)
    pad = np.zeros((table.shape[0], 32), dtype=jnp.bfloat16)
    return np.concatenate([high, high, low, pad], axis=1)


def z_of_rows():
    rows = np.arange(HALF_Z)
    return (rows % 8) * ZB + 2 * (rows // 8)


def make_tables():
    n, m = np.arange(HALF_Y)[:, None], np.arange(HALF_Y)[None, :]
    y_even = real_form(np.exp(-2j * np.pi * (n * (2 * m) % NY) / NY) / math.sqrt(NY))
    y_odd = real_form(np.exp(-2j * np.pi * (n * (2 * m + 1) % NY) / NY) / math.sqrt(NY))
    spots, freq = z_of_rows()[None, :], np.arange(HALF_Z)[:, None]
    z_even = real_form((np.exp(-2j * np.pi * (freq * spots % NZ) / NZ) / math.sqrt(NZ)).T).T
    z_odd = real_form((np.exp(-2j * np.pi * (freq * (spots + 1) % NZ) / NZ) / math.sqrt(NZ)).T).T
    forward_y = np.stack([right_table(y_even), right_table(y_odd)])
    backward_y = np.stack([right_table(y_even.T), right_table(y_odd.T)])
    forward_z = np.stack([left_table(z_even), left_table(z_odd)])
    backward_z = np.stack([left_table(z_even.T), left_table(z_odd.T)])
    order = np.zeros((NY, NY), dtype=jnp.bfloat16)
    for lane in range(NY):
        order[2 * (lane % HALF_Y) + lane // HALF_Y, lane] = 1
    return forward_y, forward_z, backward_y, backward_z, order


def iota(shape, axis):
    return lax.broadcasted_iota(jnp.int32, shape, axis)


def block_transpose(tiles):
    group = iota((8, LANES), 1) >> 4
    tiles = list(tiles)
    for bit in (1, 2, 4):
        unset = (group & bit) == 0
        for i in range(8):
            if i & bit:
                continue
            a, c = tiles[i], tiles[i | bit]
            tiles[i] = jnp.where(unset, a, pltpu.roll(c, 16 * bit, 1))
            tiles[i | bit] = jnp.where(unset, pltpu.roll(a, LANES - 16 * bit, 1), c)
    return tiles


def inner_transpose(tile):
    group, row = iota((8, LANES), 1) >> 4, iota((8, LANES), 0)
    for bit in (1, 2, 4):
        g, s = (group & bit) != 0, (row & bit) != 0
        down = pltpu.roll(pltpu.roll(tile, bit, 0), LANES - 16 * bit, 1)
        up = pltpu.roll(pltpu.roll(tile, 8 - bit, 0), 16 * bit, 1)
        tile = jnp.where(g == s, tile, jnp.where(s, down, up))
    return tile


def halves(values):
    high = values.astype(bf16)
    return high, (values - high.astype(f32)).astype(bf16)


def times_right(values, table):
    high, low = halves(values)
    return jnp.dot(jnp.concatenate([high, low, high], axis=1), table, preferred_element_type=f32)


def times_left(table, values):
    high, low = halves(values)
    pad = jnp.zeros((32, values.shape[1]), bf16)
    return jnp.dot(table, jnp.concatenate([high, low, high, pad], axis=0), preferred_element_type=f32)


def split_rows(values):
    grouped = values.reshape(ZB // 2, 2, 8, values.shape[1])
    return [grouped[:, parity].reshape(HALF_Z, values.shape[1]) for parity in range(2)]


def join_rows(even, odd):
    parts = [side.reshape(ZB // 2, 1, 8, side.shape[1]) for side in (even, odd)]
    return jnp.concatenate(parts, axis=1).reshape(NZ, even.shape[1])


def plane(ref, f):
    return jnp.concatenate([ref[0, f * NZ : (f + 1) * NZ], ref[1, f * NZ : (f + 1) * NZ]], axis=1)


def names_of(g):
    return [0, 1, 2] + [3 + 8 * p + 2 * g + e for p in range(2) for e in range(2)]


def dense_tiles(maps, coils, stacked, turned, emit):
    blank = jnp.zeros((8, LANES), f32)
    for g in range(4):
        stacked[g, 136:144] = blank
        for i, name in enumerate(names_of(g)):
            if name < 3:
                if g == 0:
                    rows = jnp.swapaxes(maps[name].reshape(8 * YB, ZB), 0, 1)
                    for other in range(4):
                        stacked[other, i * ZB : (i + 1) * ZB] = rows
            else:
                block = coils[(name - 3) // 8, (name - 3) % 8]
                stacked[g, i * ZB : (i + 1) * ZB] = jnp.swapaxes(block.reshape(8 * YB, ZB), 0, 1)
        turned[g] = jnp.swapaxes(stacked[g, :LANES], 0, 1)
        for j in range(MAIN):
            emit(g, j, turned[g, pl.ds(j, 8, stride=YB), :])
        for v in range(2):
            emit(g, MAIN + v, inner_transpose(stacked[g, LANES + 8 * v : LANES + 8 * v + 8]))


def pack_kernel(
    times, mask, maps_in, coils_in, point_maps, point_coils,
    send, dense, mask_send,
    maps, coils, of_maps, of_coils, stamp, stacked, turned, sems,
):
    t, core = lax.axis_index("ti"), lax.axis_index("kz") & 1
    copies = [
        pltpu.make_async_copy(maps_in, maps, sems.at[0]),
        pltpu.make_async_copy(coils_in, coils, sems.at[1]),
        pltpu.make_async_copy(times, stamp, sems.at[2]),
    ]
    mask_copies = [pltpu.make_async_copy(mask.at[core], mask_send.at[s], sems.at[3 + s]) for s in range(8)]
    point_copies = []
    items = []
    for i in range(ITEMS):
        item = jnp.minimum((t >> 1) * 18 + 2 * i + (t & 1), PAIRS - 1)
        f = item // ZB
        z = item - f * ZB
        q = jnp.maximum(f - 3, 0)
        items.append(f)
        point_copies.append(
            pltpu.make_async_copy(point_maps.at[jnp.minimum(f, 2), z], of_maps.at[i], sems.at[11 + i])
        )
        point_copies.append(
            pltpu.make_async_copy(point_coils.at[q >> 1, :, q & 1, z], of_coils.at[i], sems.at[20 + i])
        )
    for copy in copies + point_copies + mask_copies:
        copy.start()
    for copy in copies:
        copy.wait()
    lane = iota((8, LANES), 1)
    spare = jnp.where(lane == 64, stamp[0], jnp.where(lane == 65, stamp[1], 0.0))

    def emit(g, u, tile):
        dense[g, u] = tile
        if u == TILES - 1:
            tile = jnp.where(lane < 64, tile, spare)
        for m in (g, g + 4):
            send[8 * m : 8 * m + 8, u * LANES : (u + 1) * LANES] = tile

    dense_tiles(maps, coils, stacked, turned, emit)
    for copy in point_copies:
        copy.wait()
    for i in range(ITEMS):
        for g in range(4):
            tile = jnp.where(items[i] < 3, of_maps[i], of_coils[i, g])
            for m in (g, g + 4):
                send[8 * m : 8 * m + 8, MSG + i * NY : MSG + (i + 1) * NY] = tile
    for copy in mask_copies:
        copy.wait()


def dense_kernel(maps, coils, dense, stacked, turned):
    def emit(g, u, tile):
        dense[g, u] = tile

    dense_tiles(maps, coils, stacked, turned, emit)


def forward_kernel(own, other, table_y, table_z, spectrum, point, taus, direction, main, rest):
    step = pl.program_id(0)
    t, core = lax.axis_index("ti"), lax.axis_index("kz") & 1

    @pl.when(step == 0)
    def _():
        for part, c in ((own, core), (other, 1 - core)):
            for j in range(MAIN):
                main[j * 64 : (j + 1) * 64, :] = part[:, j * LANES : (j + 1) * LANES]
            for y in range(4):
                for half in range(2):
                    rows = [
                        main[pl.ds(8 * 64 * side + 4 * (8 * half + i) + y, 8, stride=64), :]
                        for i in range(8)
                        for side in range(2)
                    ]
                    pairs = jnp.swapaxes(jnp.concatenate(rows, axis=0), 0, 1)
                    direction[half, pl.ds(2 * y + c, LANES, stride=8), :] = pairs
            for v in range(2):
                rest[v, pl.ds(c, 64, stride=2), :] = part[:, (MAIN + v) * LANES : (MAIN + v + 1) * LANES]
            for i in range(ITEMS):
                for half in range(2):
                    side = slice(MSG + i * NY + half * LANES, MSG + i * NY + (half + 1) * LANES)
                    for m in range(8):
                        n = 18 * m + 2 * i
                        if n < PAIRS:
                            point[half, pl.ds(8 * n + c, 8, stride=2), :] = part[8 * m : 8 * m + 8, side]
        for v in range(2):
            for half in range(2):
                tiles = [rest[v, 8 * (8 * half + i) : 8 * (8 * half + i) + 8] for i in range(8)]
                for member, tile in enumerate(block_transpose(tiles)):
                    n = LANES + 8 * v + member
                    if n < PAIRS:
                        direction[half, 8 * n : 8 * n + 8] = tile

    block = rest[1, pl.ds(pl.multiple_of(((t & 8) + step) * 8, 8), 8), :]
    chosen = (iota((8, LANES), 0) == 0) & (iota((8, LANES), 1) == 64 + core)
    tau = jnp.sum(jnp.where(chosen, block, 0.0), axis=(0, 1), keepdims=True)
    taus[0] = jnp.broadcast_to(tau, (8, LANES))

    amplitude = plane(point, 1)
    decays = jnp.exp(-tau * plane(point, 2))
    signal = plane(point, 0) - amplitude * decays
    change = plane(direction, 0) - plane(direction, 1) * decays + amplitude * tau * decays * plane(direction, 2)
    evens, odds = [], []
    for c in range(2):
        re = plane(point, 3 + c) * change + plane(direction, 3 + c) * signal
        im = plane(point, 5 + c) * change + plane(direction, 5 + c) * signal
        re_low, re_high, im_low, im_high = re[:, :HALF_Y], re[:, HALF_Y:], im[:, :HALF_Y], im[:, HALF_Y:]
        evens.append(jnp.concatenate([re_low + re_high, im_low + im_high], axis=1))
        odds.append(jnp.concatenate([re_low - re_high, im_low - im_high], axis=1))
    along_even = times_right(jnp.concatenate(evens, axis=0), table_y[0])
    along_odd = times_right(jnp.concatenate(odds, axis=0), table_y[1])
    for c in range(2):
        rows = slice(c * NZ, (c + 1) * NZ)
        re = jnp.concatenate([along_even[rows, :HALF_Y], along_odd[rows, :HALF_Y]], axis=1)
        im = jnp.concatenate([along_even[rows, HALF_Y:], along_odd[rows, HALF_Y:]], axis=1)
        parts = [
            times_left(table_z[parity], jnp.concatenate(pair, axis=0))
            for parity, pair in enumerate(zip(split_rows(re), split_rows(im)))
        ]
        for part in range(2):
            a, b = (side[part * HALF_Z : (part + 1) * HALF_Z] for side in parts)
            spectrum[0, c, part, :HALF_Z] = a + b
            spectrum[0, c, part, HALF_Z:] = a - b


def backward_kernel(mask, spectrum, point, taus, table_y, table_z, order, mine, theirs, total, sent, rest):
    step = pl.program_id(0)
    core = lax.axis_index("kz") & 1

    @pl.when(step == 0)
    def _():
        total[...] = jnp.zeros_like(total)

    tau = taus[0, 0:1, 0:1]
    weights = jnp.dot(mask[0].astype(f32).astype(bf16), order[...], preferred_element_type=f32)
    evens, odds = [], []
    for c in range(2):
        plus, minus = [], []
        for part in range(2):
            values = spectrum[0, c, part] * weights
            plus.append(values[:HALF_Z] + values[HALF_Z:])
            minus.append(values[:HALF_Z] - values[HALF_Z:])
        for parity, side in enumerate((plus, minus)):
            out = times_left(table_z[parity], jnp.concatenate(side, axis=0))
            re, im = out[:HALF_Z], out[HALF_Z:]
            evens.append(jnp.concatenate([re[:, :HALF_Y], im[:, :HALF_Y]], axis=1))
            odds.append(jnp.concatenate([re[:, HALF_Y:], im[:, HALF_Y:]], axis=1))
    from_even = times_right(jnp.concatenate(evens, axis=0), table_y[0])
    from_odd = times_right(jnp.concatenate(odds, axis=0), table_y[1])
    low, high = from_even + from_odd, from_even - from_odd

    def add(f, values):
        for half in range(2):
            total[half, f * NZ : (f + 1) * NZ] += values[:, half * LANES : (half + 1) * LANES]

    amplitude = plane(point, 1)
    decays = jnp.exp(-tau * plane(point, 2))
    signal = plane(point, 0) - amplitude * decays
    projected = None
    for c in range(2):
        sides = []
        for lanes in (slice(0, HALF_Y), slice(HALF_Y, NY)):
            value = jnp.concatenate([low[:, lanes], high[:, lanes]], axis=1)
            first = 2 * c * HALF_Z
            sides.append(join_rows(value[first : first + HALF_Z], value[first + HALF_Z : first + NZ]))
        re, im = sides
        term = plane(point, 3 + c) * re + plane(point, 5 + c) * im
        projected = term if projected is None else projected + term
        add(3 + c, signal * re)
        add(5 + c, signal * im)
    add(0, projected)
    faded = decays * projected
    add(1, -faded)
    add(2, amplitude * (tau * faded))

    @pl.when(step == 7)
    def _():
        for k in range(8):
            slot = (k & 1) ^ core
            for half in range(2):
                pairs = jnp.swapaxes(total[half, pl.ds(k, LANES, stride=8), :], 0, 1)
                for i in range(8):
                    for side in range(2):
                        first = 8 * 64 * side + 4 * (8 * half + i) + (k >> 1)
                        rows = slice(16 * i + 8 * side, 16 * i + 8 * side + 8)
                        sent[slot, pl.ds(first, 8, stride=64), :] = pairs[rows]
        for v in range(2):
            for half in range(2):
                tiles = []
                for member in range(8):
                    n = min(LANES + 8 * v + member, PAIRS - 1)
                    tiles.append(total[half, 8 * n : 8 * n + 8])
                for i, tile in enumerate(block_transpose(tiles)):
                    rest[v, 8 * (8 * half + i) : 8 * (8 * half + i) + 8] = tile
            for c in range(2):
                rows = pl.ds((MAIN + v) * 64, 64)
                sent[c ^ core, rows, :] = rest[v, pl.ds(c, 64, stride=2), :]
        for u in range(TILES):
            mine[:, u * LANES : (u + 1) * LANES] = sent[0, u * 64 : (u + 1) * 64]
            theirs[:, u * LANES : (u + 1) * LANES] = sent[1, u * 64 : (u + 1) * 64]


def sums_kernel(received, direction, residual, applied, out_sums):
    lane = iota((8, LANES), 1)
    sums = [jnp.zeros((8, LANES), f32) for _ in range(4)]
    for u in range(TILES):
        sides = []
        for g in range(4):
            upper, lower = (received[8 * m : 8 * m + 8, u * LANES : (u + 1) * LANES] for m in (g, g + 4))
            sides.append(upper + lower)
        if u < MAIN:
            maps = sides[0] + sides[1] + sides[2] + sides[3]
        for g in range(4):
            d, r, value = direction[g, u], residual[g, u], sides[g]
            if u < MAIN:
                of_maps = lane < 3 * ZB
                if g == 0:
                    value = jnp.where(of_maps, maps, value)
                else:
                    d, r, value = (jnp.where(of_maps, 0.0, a) for a in (d, r, value))
            elif u == TILES - 1:
                d, r, value = (jnp.where(lane < 64, a, 0.0) for a in (d, r, value))
            q = value + regular_weight * d
            applied[g, u] = q
            for i, (a, b) in enumerate(((r, r), (d, q), (r, q), (q, q))):
                sums[i] = sums[i] + a * b
    line = jnp.zeros((1, LANES), f32)
    for i in range(4):
        value = jnp.sum(sums[i], axis=(0, 1), keepdims=True)
        line = jnp.where(iota((1, LANES), 1) == i, value, line)
    out_sums[...] = jnp.broadcast_to(line, (LANES, LANES))


def native_kernel(dense, maps, coils, stacked, turned):
    for g in range(4):
        for j in range(MAIN):
            turned[g, pl.ds(j, 8, stride=YB), :] = dense[g, j]
        stacked[g, :LANES] = jnp.swapaxes(turned[g], 0, 1)
        for v in range(2):
            stacked[g, LANES + 8 * v : LANES + 8 * v + 8] = inner_transpose(dense[g, MAIN + v])
        for i, name in enumerate(names_of(g)):
            if name < 3 and g:
                continue
            block = jnp.swapaxes(stacked[g, i * ZB : (i + 1) * ZB], 0, 1).reshape(XS, YB, ZB)
            if name < 3:
                maps[name] = block
            else:
                coils[(name - 3) // 8, (name - 3) % 8] = block


def step_kernel(sums, app_maps, app_coils, dir_maps, dir_coils, res_maps, res_coils, *outs):
    line = jnp.sum(sums[...], axis=0, keepdims=True)
    lane = iota((1, LANES), 1)
    old, curve, cross, square = (
        jnp.sum(jnp.where(lane == i, line, 0.0), axis=1, keepdims=True) for i in range(4)
    )
    size = old / curve
    new = old - 2.0 * size * cross + size * size * square
    ratio = (new / old).reshape(1, 1, 1)
    size = size.reshape(1, 1, 1)
    for f in range(3):
        fresh = res_maps[f] - size * app_maps[f]
        outs[0][f] = fresh
        outs[2][f] = fresh + ratio * dir_maps[f]
    for part in range(2):
        for coil in range(8):
            fresh = res_coils[part, coil] - size * app_coils[part, coil]
            outs[1][part, coil] = fresh
            outs[3][part, coil] = fresh + ratio * dir_coils[part, coil]


def struct(*shape):
    return jax.ShapeDtypeStruct(shape, f32)


ANY = pl.BlockSpec(memory_space=pl.ANY)
VMEM = pl.BlockSpec(memory_space=pltpu.VMEM)
SCRATCH_STACKED = pltpu.VMEM((4, 144, LANES), f32)
SCRATCH_TURNED = pltpu.VMEM((4, LANES, LANES), f32)


def params():
    return pltpu.CompilerParams(vmem_limit_bytes=VMEM_LIMIT)


def cost(micros):
    return pl.CostEstimate(flops=int(micros * 4e8), bytes_accessed=int(micros * 2e6), transcendentals=0)


def constant_block(shape):
    return pl.BlockSpec(shape, lambda s: (0,) * len(shape))


def stepping_block(shape):
    return pl.BlockSpec((1,) + shape, lambda s: (s,) + (0,) * len(shape))


def core_swap(values):
    return lax.ppermute(values, "kz", [(i, i ^ 1) for i in range(8)])


def by_parity(values):
    groups = [[i for i in range(128) if i & 1 == c] for c in range(2)]
    return lax.all_to_all(values, AXES, 0, 0, axis_index_groups=groups, tiled=True)


def shards(
    point_maps,
    point_coils,
    direction_maps,
    direction_coils,
    residual_maps,
    residual_coils,
    inversion_times,
    sampling_mask,
):
    forward_y, forward_z, backward_y, backward_z, order = (jnp.asarray(table) for table in make_tables())
    dir_maps, dir_coils = jnp.swapaxes(direction_maps, 2, 3), jnp.swapaxes(direction_coils, 3, 4)
    res_maps, res_coils = jnp.swapaxes(residual_maps, 2, 3), jnp.swapaxes(residual_coils, 3, 4)
    pnt_maps = jnp.swapaxes(point_maps, 1, 2)
    pnt_coils = jnp.swapaxes(point_coils, 2, 3).reshape(2, 4, 2, ZB, XS, NY)

    send, dir_dense, mask_send = pl.pallas_call(
        pack_kernel,
        out_shape=(
            struct(64, 2 * MSG),
            struct(4, TILES, 8, LANES),
            jax.ShapeDtypeStruct((8, NZ, NY), jnp.int32),
        ),
        in_specs=[ANY] * 6,
        out_specs=(VMEM, VMEM, ANY),
        scratch_shapes=[
            pltpu.VMEM(dir_maps.shape, f32),
            pltpu.VMEM(dir_coils.shape, f32),
            pltpu.VMEM((ITEMS, 8, NY), f32),
            pltpu.VMEM((ITEMS, 4, 8, NY), f32),
            pltpu.SMEM((2,), f32),
            SCRATCH_STACKED,
            SCRATCH_TURNED,
            pltpu.SemaphoreType.DMA((29,)),
        ],
        compiler_params=params(),
        cost_estimate=cost(4),
        name="pack",
    )(inversion_times, sampling_mask, dir_maps, dir_coils, pnt_maps, pnt_coils)

    def densify(maps, coils):
        return pl.pallas_call(
            dense_kernel,
            out_shape=struct(4, TILES, 8, LANES),
            in_specs=[VMEM] * 2,
            out_specs=VMEM,
            scratch_shapes=[SCRATCH_STACKED, SCRATCH_TURNED],
            compiler_params=params(),
            cost_estimate=cost(3),
            name="dense",
        )(maps, coils)

    res_dense = densify(res_maps, res_coils)
    own = by_parity(send)
    other = core_swap(own)
    mask_send, own = lax.optimization_barrier((mask_send, own))
    groups = [[8 * b + i for i in range(8)] for b in range(2)]
    masks = lax.all_to_all(mask_send, "ti", 0, 0, axis_index_groups=groups, tiled=True)

    spectrum, point, taus = pl.pallas_call(
        forward_kernel,
        grid=(8,),
        out_shape=(struct(8, 2, 2, NZ, NY), struct(2, FEATURES * NZ, LANES), struct(8, 8, LANES)),
        in_specs=[constant_block(a.shape) for a in (own, other, forward_y, forward_z)],
        out_specs=(
            stepping_block((2, 2, NZ, NY)),
            constant_block((2, FEATURES * NZ, LANES)),
            stepping_block((8, LANES)),
        ),
        scratch_shapes=[
            pltpu.VMEM((2, FEATURES * NZ, LANES), f32),
            pltpu.VMEM((MAIN * 64, LANES), f32),
            pltpu.VMEM((2, LANES, LANES), f32),
        ],
        compiler_params=params(),
        cost_estimate=cost(12),
        name="forward",
    )(own, other, forward_y, forward_z)

    mine, theirs = pl.pallas_call(
        backward_kernel,
        grid=(8,),
        out_shape=(struct(64, MSG), struct(64, MSG)),
        in_specs=[
            stepping_block((NZ, NY)),
            stepping_block((2, 2, NZ, NY)),
            constant_block((2, FEATURES * NZ, LANES)),
            stepping_block((8, LANES)),
        ]
        + [constant_block(a.shape) for a in (backward_y, backward_z, order)],
        out_specs=(constant_block((64, MSG)),) * 2,
        scratch_shapes=[
            pltpu.VMEM((2, FEATURES * NZ, LANES), f32),
            pltpu.VMEM((2, TILES * 64, LANES), f32),
            pltpu.VMEM((2, LANES, LANES), f32),
        ],
        compiler_params=params(),
        cost_estimate=cost(12),
        name="backward",
    )(masks, spectrum, point, taus, backward_y, backward_z, order)

    received = by_parity(mine + core_swap(theirs))
    app_dense, sums = pl.pallas_call(
        sums_kernel,
        out_shape=(struct(4, TILES, 8, LANES), struct(128, LANES)),
        in_specs=[VMEM] * 3,
        out_specs=(VMEM,) * 2,
        compiler_params=params(),
        cost_estimate=cost(1),
        name="sums",
    )(received, dir_dense, res_dense)
    all_sums = lax.all_to_all(sums.reshape(128, 1, LANES), AXES, 0, 0).reshape(128, LANES)

    maps_shape, coils_shape = struct(*dir_maps.shape), struct(*dir_coils.shape)
    app_maps, app_coils = pl.pallas_call(
        native_kernel,
        out_shape=(maps_shape, coils_shape),
        in_specs=[VMEM],
        out_specs=(VMEM,) * 2,
        scratch_shapes=[SCRATCH_STACKED, SCRATCH_TURNED],
        compiler_params=params(),
        cost_estimate=cost(3),
        name="native",
    )(app_dense)

    outs = pl.pallas_call(
        step_kernel,
        out_shape=(maps_shape, coils_shape, maps_shape, coils_shape),
        in_specs=[VMEM] * 7,
        out_specs=(VMEM,) * 4,
        compiler_params=params(),
        cost_estimate=cost(2),
        name="step",
    )(all_sums, app_maps, app_coils, dir_maps, dir_coils, res_maps, res_coils)
    return tuple(jnp.swapaxes(out, -2, -1) for out in outs)


def solution(mesh):
    in_specs = (
        P(None, None, "kz", None),
        P(None, None, None, "kz", None),
        P(None, None, "kz", "ti"),
        P(None, None, None, "kz", "ti"),
        P(None, None, "kz", "ti"),
        P(None, None, None, "kz", "ti"),
        P("ti"),
        P("ti", None, None),
    )
    out_specs = (
        P(None, None, "kz", "ti"),
        P(None, None, None, "kz", "ti"),
        P(None, None, "kz", "ti"),
        P(None, None, None, "kz", "ti"),
    )
    return jax.shard_map(shards, mesh=mesh, in_specs=in_specs, out_specs=out_specs, check_vma=False)
```

```python
import math

import jax
import jax.numpy as jnp
import numpy as np
from jax import lax
from jax.experimental import pallas as pl
from jax.experimental.pallas import tpu as pltpu
from jax.sharding import PartitionSpec as P

regular_weight = 2.0
AXES = ("ti", "kz")
NZ, NY, ZB, YB, XS = 160, 256, 20, 16, 8
HALF_Z, HALF_Y = NZ // 2, NY // 2
LANES = 128
FEATURES = 7
PAIRS = FEATURES * ZB
MAIN = 16
TILES = 18
MSG = TILES * LANES
ITEMS = 9
WHOLE = 2 * TILES
VMEM_LIMIT = 32 * 1024 * 1024
f32 = jnp.float32
bf16 = jnp.bfloat16


def split_pair(table):
    high = table.astype(np.float32).astype(jnp.bfloat16)
    low = (table - high.astype(np.float64)).astype(np.float32).astype(jnp.bfloat16)
    return high, low


def real_form(matrix):
    return np.block([[matrix.real, matrix.imag], [-matrix.imag, matrix.real]])


def right_table(table):
    high, low = split_pair(table)
    return np.concatenate([high, high, low], axis=0)


def left_table(table):
    high, low = split_pair(table)
    pad = np.zeros((table.shape[0], 32), dtype=jnp.bfloat16)
    return np.concatenate([high, high, low, pad], axis=1)


def z_of_rows():
    rows = np.arange(HALF_Z)
    return (rows % 8) * ZB + 2 * (rows // 8)


def make_tables():
    n, m = np.arange(HALF_Y)[:, None], np.arange(HALF_Y)[None, :]
    y_even = real_form(np.exp(-2j * np.pi * (n * (2 * m) % NY) / NY) / math.sqrt(NY))
    y_odd = real_form(np.exp(-2j * np.pi * (n * (2 * m + 1) % NY) / NY) / math.sqrt(NY))
    spots, freq = z_of_rows()[None, :], np.arange(HALF_Z)[:, None]
    z_even = real_form((np.exp(-2j * np.pi * (freq * spots % NZ) / NZ) / math.sqrt(NZ)).T).T
    z_odd = real_form((np.exp(-2j * np.pi * (freq * (spots + 1) % NZ) / NZ) / math.sqrt(NZ)).T).T
    forward_y = np.stack([right_table(y_even), right_table(y_odd)])
    backward_y = np.stack([right_table(y_even.T), right_table(y_odd.T)])
    forward_z = np.stack([left_table(z_even), left_table(z_odd)])
    backward_z = np.stack([left_table(z_even.T), left_table(z_odd.T)])
    order = np.zeros((NY, NY), dtype=jnp.bfloat16)
    for lane in range(NY):
        order[2 * (lane % HALF_Y) + lane // HALF_Y, lane] = 1
    return forward_y, forward_z, backward_y, backward_z, order


def iota(shape, axis):
    return lax.broadcasted_iota(jnp.int32, shape, axis)


def block_transpose(tiles):
    group = iota((8, LANES), 1) >> 4
    tiles = list(tiles)
    for bit in (1, 2, 4):
        unset = (group & bit) == 0
        for i in range(8):
            if i & bit:
                continue
            a, c = tiles[i], tiles[i | bit]
            tiles[i] = jnp.where(unset, a, pltpu.roll(c, 16 * bit, 1))
            tiles[i | bit] = jnp.where(unset, pltpu.roll(a, LANES - 16 * bit, 1), c)
    return tiles


def inner_transpose(tile):
    group, row = iota((8, LANES), 1) >> 4, iota((8, LANES), 0)
    for bit in (1, 2, 4):
        g, s = (group & bit) != 0, (row & bit) != 0
        down = pltpu.roll(pltpu.roll(tile, bit, 0), LANES - 16 * bit, 1)
        up = pltpu.roll(pltpu.roll(tile, 8 - bit, 0), 16 * bit, 1)
        tile = jnp.where(g == s, tile, jnp.where(s, down, up))
    return tile


def halves(values):
    high = values.astype(bf16)
    return high, (values - high.astype(f32)).astype(bf16)


def times_right(values, table):
    high, low = halves(values)
    return jnp.dot(jnp.concatenate([high, low, high], axis=1), table, preferred_element_type=f32)


def times_left(table, values):
    high, low = halves(values)
    pad = jnp.zeros((32, values.shape[1]), bf16)
    return jnp.dot(table, jnp.concatenate([high, low, high, pad], axis=0), preferred_element_type=f32)


def split_rows(values):
    grouped = values.reshape(ZB // 2, 2, 8, values.shape[1])
    return [grouped[:, parity].reshape(HALF_Z, values.shape[1]) for parity in range(2)]


def join_rows(even, odd):
    parts = [side.reshape(ZB // 2, 1, 8, side.shape[1]) for side in (even, odd)]
    return jnp.concatenate(parts, axis=1).reshape(NZ, even.shape[1])


def plane(ref, f):
    return jnp.concatenate([ref[0, f * NZ : (f + 1) * NZ], ref[1, f * NZ : (f + 1) * NZ]], axis=1)


def names_of(g):
    return [0, 1, 2] + [3 + 8 * p + 2 * g + e for p in range(2) for e in range(2)]


def dense_tiles(maps, coils, stacked, turned, emit, arrive=None):
    blank = jnp.zeros((8, LANES), f32)
    for g in range(4):
        if arrive is not None:
            arrive(g)
        stacked[g, 136:144] = blank
        for i, name in enumerate(names_of(g)):
            if name < 3:
                if g == 0:
                    rows = jnp.swapaxes(maps[name].reshape(8 * YB, ZB), 0, 1)
                    for other in range(4):
                        stacked[other, i * ZB : (i + 1) * ZB] = rows
            else:
                block = coils[(name - 3) // 8, (name - 3) % 8]
                stacked[g, i * ZB : (i + 1) * ZB] = jnp.swapaxes(block.reshape(8 * YB, ZB), 0, 1)
        turned[g] = jnp.swapaxes(stacked[g, :LANES], 0, 1)
        for j in range(MAIN):
            emit(g, j, turned[g, pl.ds(j, 8, stride=YB), :])
        for v in range(2):
            emit(g, MAIN + v, inner_transpose(stacked[g, LANES + 8 * v : LANES + 8 * v + 8]))


def pack_kernel(
    times, mask, maps_in, coils_in, point_maps, point_coils,
    send, dense, mask_send,
    maps, coils, of_maps, of_coils, stamp, own_mask, stacked, turned, sems,
):
    t, core = lax.axis_index("ti"), lax.axis_index("kz") & 1
    mask_copy = pltpu.make_async_copy(mask.at[core], own_mask, sems.at[0])
    mask_copies = [pltpu.make_async_copy(own_mask, mask_send.at[s], sems.at[1 + s]) for s in range(8)]
    maps_copies = [
        pltpu.make_async_copy(maps_in, maps, sems.at[9]),
        pltpu.make_async_copy(times, stamp, sems.at[10]),
    ]
    coils_copies = [
        pltpu.make_async_copy(
            coils_in.at[p, pl.ds(2 * g, 2)], coils.at[p, pl.ds(2 * g, 2)], sems.at[11 + 2 * g + p]
        )
        for g in range(4)
        for p in range(2)
    ]
    point_copies = []
    items = []
    for i in range(ITEMS):
        item = jnp.minimum((t >> 1) * 18 + 2 * i + (t & 1), PAIRS - 1)
        f = item // ZB
        z = item - f * ZB
        q = jnp.maximum(f - 3, 0)
        items.append(f)
        point_copies.append(
            pltpu.make_async_copy(point_maps.at[jnp.minimum(f, 2), z], of_maps.at[i], sems.at[19 + i])
        )
        point_copies.append(
            pltpu.make_async_copy(point_coils.at[q >> 1, :, q & 1, z], of_coils.at[i], sems.at[28 + i])
        )
    for copy in point_copies + maps_copies + coils_copies + [mask_copy]:
        copy.start()
    for copy in point_copies:
        copy.wait()
    for i in range(ITEMS):
        for g in range(4):
            tile = jnp.where(items[i] < 3, of_maps[i], of_coils[i, g])
            for m in (g, g + 4):
                for half in range(2):
                    first = 8 * m * WHOLE + TILES + 2 * i + half
                    send[pl.ds(first, 8, stride=WHOLE), :] = tile[:, half * LANES : (half + 1) * LANES]
    for copy in maps_copies:
        copy.wait()
    lane = iota((8, LANES), 1)
    spare = jnp.where(lane == 64, stamp[0], jnp.where(lane == 65, stamp[1], 0.0))

    def emit(g, u, tile):
        dense[g, u] = tile
        if u == TILES - 1:
            tile = jnp.where(lane < 64, tile, spare)
        for m in (g, g + 4):
            send[pl.ds(8 * m * WHOLE + u, 8, stride=WHOLE), :] = tile

    def arrive(g):
        if g == 1:
            mask_copy.wait()
            for copy in mask_copies:
                copy.start()
        for copy in coils_copies[2 * g : 2 * g + 2]:
            copy.wait()

    dense_tiles(maps, coils, stacked, turned, emit, arrive)
    for copy in mask_copies:
        copy.wait()


def dense_kernel(maps_in, coils_in, dense, maps, coils, stacked, turned, sems):
    copies = [
        pltpu.make_async_copy(maps_in, maps, sems.at[0]),
        pltpu.make_async_copy(coils_in, coils, sems.at[1]),
    ]
    for copy in copies:
        copy.start()
    for copy in copies:
        copy.wait()

    def emit(g, u, tile):
        dense[g, u] = tile

    dense_tiles(maps, coils, stacked, turned, emit)


def forward_kernel(
    own, other, table_y_in, table_z_in,
    spectrum, point, taus,
    direction, rest, table_y, table_z, kept, sems,
):
    step = pl.program_id(0)
    t, core = lax.axis_index("ti"), lax.axis_index("kz") & 1
    slot = step & 1
    tables = [
        pltpu.make_async_copy(table_y_in, table_y, sems.at[2]),
        pltpu.make_async_copy(table_z_in, table_z, sems.at[3]),
    ]

    def store(at, side):
        return pltpu.make_async_copy(kept.at[side], spectrum.at[at], sems.at[side])

    @pl.when(step == 0)
    def _():
        for copy in tables:
            copy.start()
        for part, c in ((own, core), (other, 1 - core)):
            for y in range(4):
                for half in range(2):
                    firsts = [WHOLE * (4 * (8 * half + i) + y) for i in range(8)]
                    rows = [part[first : first + MAIN, :] for first in firsts]
                    pairs = jnp.swapaxes(jnp.concatenate(rows, axis=0), 0, 1)
                    direction[half, pl.ds(2 * y + c, LANES, stride=8), :] = pairs
            for v in range(2):
                rest[v, pl.ds(c, 64, stride=2), :] = part[pl.ds(MAIN + v, 64, stride=WHOLE), :]
            for i in range(ITEMS):
                for half in range(2):
                    for m in range(8):
                        n = 18 * m + 2 * i
                        if n < PAIRS:
                            first = 8 * m * WHOLE + TILES + 2 * i + half
                            point[half, pl.ds(8 * n + c, 8, stride=2), :] = part[pl.ds(first, 8, stride=WHOLE), :]
        for v in range(2):
            for half in range(2):
                tiles = [rest[v, 8 * (8 * half + i) : 8 * (8 * half + i) + 8] for i in range(8)]
                for member, tile in enumerate(block_transpose(tiles)):
                    n = LANES + 8 * v + member
                    if n < PAIRS:
                        direction[half, 8 * n : 8 * n + 8] = tile
        for copy in tables:
            copy.wait()

    @pl.when(step >= 2)
    def _():
        store(step - 2, slot).wait()

    block = rest[1, pl.ds(pl.multiple_of(((t & 8) + step) * 8, 8), 8), :]
    chosen = (iota((8, LANES), 0) == 0) & (iota((8, LANES), 1) == 64 + core)
    tau = jnp.sum(jnp.where(chosen, block, 0.0), axis=(0, 1), keepdims=True)
    taus[0] = jnp.broadcast_to(tau, (8, LANES))

    amplitude = plane(point, 1)
    decays = jnp.exp(-tau * plane(point, 2))
    signal = plane(point, 0) - amplitude * decays
    change = plane(direction, 0) - plane(direction, 1) * decays + amplitude * tau * decays * plane(direction, 2)
    evens, odds = [], []
    for c in range(2):
        re = plane(point, 3 + c) * change + plane(direction, 3 + c) * signal
        im = plane(point, 5 + c) * change + plane(direction, 5 + c) * signal
        re_low, re_high, im_low, im_high = re[:, :HALF_Y], re[:, HALF_Y:], im[:, :HALF_Y], im[:, HALF_Y:]
        evens.append(jnp.concatenate([re_low + re_high, im_low + im_high], axis=1))
        odds.append(jnp.concatenate([re_low - re_high, im_low - im_high], axis=1))
    along_even = times_right(jnp.concatenate(evens, axis=0), table_y[0])
    along_odd = times_right(jnp.concatenate(odds, axis=0), table_y[1])
    for c in range(2):
        rows = slice(c * NZ, (c + 1) * NZ)
        re = jnp.concatenate([along_even[rows, :HALF_Y], along_odd[rows, :HALF_Y]], axis=1)
        im = jnp.concatenate([along_even[rows, HALF_Y:], along_odd[rows, HALF_Y:]], axis=1)
        parts = [
            times_left(table_z[parity], jnp.concatenate(pair, axis=0))
            for parity, pair in enumerate(zip(split_rows(re), split_rows(im)))
        ]
        for part in range(2):
            a, b = (side[part * HALF_Z : (part + 1) * HALF_Z] for side in parts)
            kept[slot, c, part, :HALF_Z] = a + b
            kept[slot, c, part, HALF_Z:] = a - b
    store(step, slot).start()

    @pl.when(step == 7)
    def _():
        store(6, 0).wait()
        store(7, 1).wait()


def backward_kernel(
    mask, spectrum, point, taus, table_y_in, table_z_in, order_in,
    mine, theirs,
    total, sent, rest, table_y, table_z, order, kept, sems,
):
    step = pl.program_id(0)
    core = lax.axis_index("kz") & 1
    slot = step & 1
    tables = [
        pltpu.make_async_copy(order_in, order, sems.at[4]),
        pltpu.make_async_copy(table_z_in, table_z, sems.at[3]),
        pltpu.make_async_copy(table_y_in, table_y, sems.at[2]),
    ]

    def load(at, side):
        return pltpu.make_async_copy(spectrum.at[at], kept.at[side], sems.at[side])

    @pl.when(step == 0)
    def _():
        load(0, 0).start()
        for copy in tables:
            copy.start()
        total[...] = jnp.zeros_like(total)
        for copy in tables:
            copy.wait()

    @pl.when(step < 7)
    def _():
        load(step + 1, 1 - slot).start()

    load(step, slot).wait()

    tau = taus[0, 0:1, 0:1]
    weights = jnp.dot(mask[0].astype(f32).astype(bf16), order[...], preferred_element_type=f32)
    evens, odds = [], []
    for c in range(2):
        plus, minus = [], []
        for part in range(2):
            values = kept[slot, c, part] * weights
            plus.append(values[:HALF_Z] + values[HALF_Z:])
            minus.append(values[:HALF_Z] - values[HALF_Z:])
        for parity, side in enumerate((plus, minus)):
            out = times_left(table_z[parity], jnp.concatenate(side, axis=0))
            re, im = out[:HALF_Z], out[HALF_Z:]
            evens.append(jnp.concatenate([re[:, :HALF_Y], im[:, :HALF_Y]], axis=1))
            odds.append(jnp.concatenate([re[:, HALF_Y:], im[:, HALF_Y:]], axis=1))
    from_even = times_right(jnp.concatenate(evens, axis=0), table_y[0])
    from_odd = times_right(jnp.concatenate(odds, axis=0), table_y[1])
    low, high = from_even + from_odd, from_even - from_odd

    def add(f, values):
        for half in range(2):
            total[half, f * NZ : (f + 1) * NZ] += values[:, half * LANES : (half + 1) * LANES]

    amplitude = plane(point, 1)
    decays = jnp.exp(-tau * plane(point, 2))
    signal = plane(point, 0) - amplitude * decays
    projected = None
    for c in range(2):
        sides = []
        for lanes in (slice(0, HALF_Y), slice(HALF_Y, NY)):
            value = jnp.concatenate([low[:, lanes], high[:, lanes]], axis=1)
            first = 2 * c * HALF_Z
            sides.append(join_rows(value[first : first + HALF_Z], value[first + HALF_Z : first + NZ]))
        re, im = sides
        term = plane(point, 3 + c) * re + plane(point, 5 + c) * im
        projected = term if projected is None else projected + term
        add(3 + c, signal * re)
        add(5 + c, signal * im)
    add(0, projected)
    faded = decays * projected
    add(1, -faded)
    add(2, amplitude * (tau * faded))

    @pl.when(step == 7)
    def _():
        for k in range(8):
            place = (k & 1) ^ core
            for half in range(2):
                pairs = jnp.swapaxes(total[half, pl.ds(k, LANES, stride=8), :], 0, 1)
                for i in range(8):
                    first = TILES * (4 * (8 * half + i) + (k >> 1))
                    sent[place, first : first + MAIN, :] = pairs[YB * i : YB * (i + 1)]
        for v in range(2):
            for half in range(2):
                tiles = []
                for member in range(8):
                    n = min(LANES + 8 * v + member, PAIRS - 1)
                    tiles.append(total[half, 8 * n : 8 * n + 8])
                for i, tile in enumerate(block_transpose(tiles)):
                    rest[v, 8 * (8 * half + i) : 8 * (8 * half + i) + 8] = tile
            for c in range(2):
                rows = pl.ds(MAIN + v, 64, stride=TILES)
                sent[c ^ core, rows, :] = rest[v, pl.ds(c, 64, stride=2), :]
        mine[...] = sent[0]
        theirs[...] = sent[1]


def sums_kernel(received, direction, residual, applied, out_sums):
    lane = iota((8, LANES), 1)
    sums = [jnp.zeros((8, LANES), f32) for _ in range(4)]
    for u in range(TILES):
        sides = []
        for g in range(4):
            upper, lower = (received[pl.ds(8 * m * TILES + u, 8, stride=TILES), :] for m in (g, g + 4))
            sides.append(upper + lower)
        if u < MAIN:
            maps = sides[0] + sides[1] + sides[2] + sides[3]
        for g in range(4):
            d, r, value = direction[g, u], residual[g, u], sides[g]
            if u < MAIN:
                of_maps = lane < 3 * ZB
                if g == 0:
                    value = jnp.where(of_maps, maps, value)
                else:
                    d, r, value = (jnp.where(of_maps, 0.0, a) for a in (d, r, value))
            elif u == TILES - 1:
                d, r, value = (jnp.where(lane < 64, a, 0.0) for a in (d, r, value))
            q = value + regular_weight * d
            applied[g, u] = q
            for i, (a, b) in enumerate(((r, r), (d, q), (r, q), (q, q))):
                sums[i] = sums[i] + a * b
    line = jnp.zeros((1, LANES), f32)
    for i in range(4):
        value = jnp.sum(sums[i], axis=(0, 1), keepdims=True)
        line = jnp.where(iota((1, LANES), 1) == i, value, line)
    out_sums[...] = jnp.broadcast_to(line, (LANES, LANES))


def native_kernel(
    dense, dir_coils, res_coils, maps_out, fields, maps, stacked, turned, sems
):
    copies = [
        pltpu.make_async_copy(source.at[p], fields.at[pl.ds(first + 8 * p, 8)], sems.at[2 * i + p])
        for i, (source, first) in enumerate(((dir_coils, 16), (res_coils, 32)))
        for p in range(2)
    ]
    for copy in copies:
        copy.start()
    for g in range(4):
        for j in range(MAIN):
            turned[g, pl.ds(j, 8, stride=YB), :] = dense[g, j]
        stacked[g, :LANES] = jnp.swapaxes(turned[g], 0, 1)
        for v in range(2):
            stacked[g, LANES + 8 * v : LANES + 8 * v + 8] = inner_transpose(dense[g, MAIN + v])
        for i, name in enumerate(names_of(g)):
            if name < 3 and g:
                continue
            block = jnp.swapaxes(stacked[g, i * ZB : (i + 1) * ZB], 0, 1).reshape(XS, YB, ZB)
            if name < 3:
                maps[name] = block
            else:
                fields[name - 3] = block
    copies.append(pltpu.make_async_copy(maps, maps_out, sems.at[4]))
    copies[-1].start()
    for copy in copies:
        copy.wait()


def step_kernel(sums, fields, app_maps, dir_maps, res_maps, *refs):
    outs, (maps, sems) = refs[:4], refs[4:]
    copies = [
        pltpu.make_async_copy(source, maps.at[i], sems.at[i])
        for i, source in enumerate((app_maps, dir_maps, res_maps))
    ]
    for copy in copies:
        copy.start()
    line = jnp.sum(sums[...], axis=0, keepdims=True)
    lane = iota((1, LANES), 1)
    old, curve, cross, square = (
        jnp.sum(jnp.where(lane == i, line, 0.0), axis=1, keepdims=True) for i in range(4)
    )
    size = old / curve
    new = old - 2.0 * size * cross + size * size * square
    ratio = (new / old).reshape(1, 1, 1)
    size = size.reshape(1, 1, 1)
    for coil in range(16):
        fresh = fields[32 + coil] - size * fields[coil]
        outs[1][coil // 8, coil % 8] = fresh
        outs[3][coil // 8, coil % 8] = fresh + ratio * fields[16 + coil]
    for copy in copies:
        copy.wait()
    for f in range(3):
        fresh = maps[2, f] - size * maps[0, f]
        outs[0][f] = fresh
        outs[2][f] = fresh + ratio * maps[1, f]


def struct(*shape):
    return jax.ShapeDtypeStruct(shape, f32)


HBM = pl.BlockSpec(memory_space=pltpu.HBM)
VMEM = pl.BlockSpec(memory_space=pltpu.VMEM)
SCRATCH_STACKED = pltpu.VMEM((4, 144, LANES), f32)
SCRATCH_TURNED = pltpu.VMEM((4, LANES, LANES), f32)


def params():
    return pltpu.CompilerParams(vmem_limit_bytes=VMEM_LIMIT)


def cost(micros):
    return pl.CostEstimate(flops=int(micros * 4e8), bytes_accessed=int(micros * 2e6), transcendentals=0)


def constant_block(shape):
    return pl.BlockSpec(shape, lambda s: (0,) * len(shape))


def stepping_block(shape):
    return pl.BlockSpec((1,) + shape, lambda s: (s,) + (0,) * len(shape))


def in_hbm(*values):
    return tuple(pltpu.with_memory_space_constraint(value, pltpu.HBM) for value in values)


def in_vmem(*values):
    return tuple(pltpu.with_memory_space_constraint(value, pltpu.VMEM) for value in values)


def far(*shape):
    return pltpu.HBM(shape, f32)


def near(*shape):
    return pltpu.VMEM(shape, f32)


def core_swap(values):
    return lax.ppermute(values, "kz", [(i, i ^ 1) for i in range(8)])


def by_parity(values):
    groups = [[i for i in range(128) if i & 1 == c] for c in range(2)]
    messages = values.reshape(64, 1, values.shape[0] // 64 * LANES)
    return lax.all_to_all(messages, AXES, 0, 0, axis_index_groups=groups).reshape(values.shape)


def shards(
    point_maps,
    point_coils,
    direction_maps,
    direction_coils,
    residual_maps,
    residual_coils,
    inversion_times,
    sampling_mask,
):
    forward_y, forward_z, backward_y, backward_z, order = (jnp.asarray(table) for table in make_tables())
    dir_maps, dir_coils = jnp.swapaxes(direction_maps, 2, 3), jnp.swapaxes(direction_coils, 3, 4)
    res_maps, res_coils = jnp.swapaxes(residual_maps, 2, 3), jnp.swapaxes(residual_coils, 3, 4)
    pnt_maps = jnp.swapaxes(point_maps, 1, 2)
    pnt_coils = jnp.swapaxes(point_coils, 2, 3).reshape(2, 4, 2, ZB, XS, NY)

    send, dir_dense, mask_send = pl.pallas_call(
        pack_kernel,
        out_shape=(
            struct(64 * WHOLE, LANES),
            near(4, TILES, 8, LANES),
            pltpu.HBM((8, NZ, NY), jnp.int32),
        ),
        in_specs=[HBM] * 6,
        out_specs=(VMEM, VMEM, HBM),
        scratch_shapes=[
            pltpu.VMEM(dir_maps.shape, f32),
            pltpu.VMEM(dir_coils.shape, f32),
            pltpu.VMEM((ITEMS, 8, NY), f32),
            pltpu.VMEM((ITEMS, 4, 8, NY), f32),
            pltpu.SMEM((2,), f32),
            pltpu.VMEM((NZ, NY), jnp.int32),
            SCRATCH_STACKED,
            SCRATCH_TURNED,
            pltpu.SemaphoreType.DMA((37,)),
        ],
        compiler_params=params(),
        cost_estimate=cost(4),
        name="pack",
    )(*in_hbm(inversion_times, sampling_mask, dir_maps, dir_coils, pnt_maps, pnt_coils))

    def densify(maps, coils):
        return pl.pallas_call(
            dense_kernel,
            out_shape=near(4, TILES, 8, LANES),
            in_specs=[HBM] * 2,
            out_specs=VMEM,
            scratch_shapes=[
                pltpu.VMEM(maps.shape, f32),
                pltpu.VMEM(coils.shape, f32),
                SCRATCH_STACKED,
                SCRATCH_TURNED,
                pltpu.SemaphoreType.DMA((2,)),
            ],
            compiler_params=params(),
            cost_estimate=cost(3),
            name="dense",
        )(*in_hbm(maps, coils))

    own = by_parity(send)
    other = core_swap(own)
    groups = [[8 * b + i for i in range(8)] for b in range(2)]
    masks = lax.all_to_all(mask_send, "ti", 0, 0, axis_index_groups=groups, tiled=True)

    spectrum, point, taus = pl.pallas_call(
        forward_kernel,
        grid=(8,),
        out_shape=(
            far(8, 2, 2, NZ, NY),
            near(2, FEATURES * NZ, LANES),
            near(8, 8, LANES),
        ),
        in_specs=[constant_block(own.shape)] * 2 + [HBM] * 2,
        out_specs=(
            HBM,
            constant_block((2, FEATURES * NZ, LANES)),
            stepping_block((8, LANES)),
        ),
        scratch_shapes=[
            pltpu.VMEM((2, FEATURES * NZ, LANES), f32),
            pltpu.VMEM((2, LANES, LANES), f32),
            pltpu.VMEM(forward_y.shape, bf16),
            pltpu.VMEM(forward_z.shape, bf16),
            pltpu.VMEM((2, 2, 2, NZ, NY), f32),
            pltpu.SemaphoreType.DMA((4,)),
        ],
        compiler_params=params(),
        cost_estimate=cost(12),
        name="forward",
    )(own, other, *in_hbm(forward_y, forward_z))

    after = lax.optimization_barrier((res_maps, res_coils, taus))
    res_dense = densify(*after[:2])
    masks, res_dense = lax.optimization_barrier((masks, res_dense))

    mine, theirs = pl.pallas_call(
        backward_kernel,
        grid=(8,),
        out_shape=(struct(64 * TILES, LANES), struct(64 * TILES, LANES)),
        in_specs=[
            stepping_block((NZ, NY)),
            HBM,
            constant_block((2, FEATURES * NZ, LANES)),
            stepping_block((8, LANES)),
        ]
        + [HBM] * 3,
        out_specs=(constant_block((64 * TILES, LANES)),) * 2,
        scratch_shapes=[
            pltpu.VMEM((2, FEATURES * NZ, LANES), f32),
            pltpu.VMEM((2, 64 * TILES, LANES), f32),
            pltpu.VMEM((2, LANES, LANES), f32),
            pltpu.VMEM(backward_y.shape, bf16),
            pltpu.VMEM(backward_z.shape, bf16),
            pltpu.VMEM(order.shape, bf16),
            pltpu.VMEM((2, 2, 2, NZ, NY), f32),
            pltpu.SemaphoreType.DMA((5,)),
        ],
        compiler_params=params(),
        cost_estimate=cost(12),
        name="backward",
    )(*in_hbm(masks, spectrum), *in_vmem(point, taus), *in_hbm(backward_y, backward_z, order))

    received = by_parity(mine + core_swap(theirs))
    app_dense, sums = pl.pallas_call(
        sums_kernel,
        out_shape=(near(4, TILES, 8, LANES), near(128, LANES)),
        in_specs=[VMEM] * 3,
        out_specs=(VMEM, VMEM),
        compiler_params=params(),
        cost_estimate=cost(1),
        name="sums",
    )(received, *in_vmem(dir_dense, res_dense))
    all_sums = lax.all_to_all(sums.reshape(128, 1, LANES), AXES, 0, 0).reshape(128, LANES)

    maps_shape, coils_shape = struct(*dir_maps.shape), struct(*dir_coils.shape)
    app_maps, fields = pl.pallas_call(
        native_kernel,
        out_shape=(far(*dir_maps.shape), near(48, XS, YB, ZB)),
        in_specs=[VMEM] + [HBM] * 2,
        out_specs=(HBM, VMEM),
        scratch_shapes=[
            pltpu.VMEM(dir_maps.shape, f32),
            SCRATCH_STACKED,
            SCRATCH_TURNED,
            pltpu.SemaphoreType.DMA((5,)),
        ],
        compiler_params=params(),
        cost_estimate=cost(3),
        name="native",
    )(*in_vmem(app_dense), *in_hbm(dir_coils, res_coils))

    outs = pl.pallas_call(
        step_kernel,
        out_shape=(maps_shape, coils_shape, maps_shape, coils_shape),
        in_specs=[VMEM] * 2 + [HBM] * 3,
        out_specs=(VMEM,) * 4,
        scratch_shapes=[pltpu.VMEM((3,) + dir_maps.shape, f32), pltpu.SemaphoreType.DMA((3,))],
        compiler_params=params(),
        cost_estimate=cost(2),
        name="step",
    )(all_sums, *in_vmem(fields), *in_hbm(app_maps, dir_maps, res_maps))
    return tuple(jnp.swapaxes(out, -2, -1) for out in outs)


def solution(mesh):
    in_specs = (
        P(None, None, "kz", None),
        P(None, None, None, "kz", None),
        P(None, None, "kz", "ti"),
        P(None, None, None, "kz", "ti"),
        P(None, None, "kz", "ti"),
        P(None, None, None, "kz", "ti"),
        P("ti"),
        P("ti", None, None),
    )
    out_specs = (
        P(None, None, "kz", "ti"),
        P(None, None, None, "kz", "ti"),
        P(None, None, "kz", "ti"),
        P(None, None, None, "kz", "ti"),
    )
    return jax.shard_map(shards, mesh=mesh, in_specs=in_specs, out_specs=out_specs, check_vma=False)
```

```python
import math

import jax
import jax.numpy as jnp
import numpy as np
from jax import lax
from jax.experimental import pallas as pl
from jax.experimental.pallas import tpu as pltpu
from jax.sharding import PartitionSpec as P

regular_weight = 2.0
AXES = ("ti", "kz")
NZ, NY, ZB, YB, XS = 160, 256, 20, 16, 8
HALF_Z, HALF_Y = NZ // 2, NY // 2
LANES = 128
FEATURES = 7
PAIRS = FEATURES * ZB
MAIN = 16
TILES = 18
MSG = TILES * LANES
ITEMS = 9
BINS = 8
FULL = 4
WHOLE = 2 * TILES
VMEM_LIMIT = 32 * 1024 * 1024
f32 = jnp.float32
bf16 = jnp.bfloat16


def split_pair(table):
    high = table.astype(np.float32).astype(jnp.bfloat16)
    low = (table - high.astype(np.float64)).astype(np.float32).astype(jnp.bfloat16)
    return high, low


def real_form(matrix):
    return np.block([[matrix.real, matrix.imag], [-matrix.imag, matrix.real]])


def right_table(table):
    high, low = split_pair(table)
    return np.concatenate([high, high, low], axis=0)


def left_table(table):
    high, low = split_pair(table)
    pad = np.zeros((table.shape[0], 32), dtype=jnp.bfloat16)
    return np.concatenate([high, high, low, pad], axis=1)


def z_of_rows():
    rows = np.arange(HALF_Z)
    return (rows % 8) * ZB + 2 * (rows // 8)


def make_tables():
    n, m = np.arange(HALF_Y)[:, None], np.arange(HALF_Y)[None, :]
    y_even = real_form(np.exp(-2j * np.pi * (n * (2 * m) % NY) / NY) / math.sqrt(NY))
    y_odd = real_form(np.exp(-2j * np.pi * (n * (2 * m + 1) % NY) / NY) / math.sqrt(NY))
    spots, freq = z_of_rows()[None, :], np.arange(HALF_Z)[:, None]
    z_even = real_form((np.exp(-2j * np.pi * (freq * spots % NZ) / NZ) / math.sqrt(NZ)).T).T
    z_odd = real_form((np.exp(-2j * np.pi * (freq * (spots + 1) % NZ) / NZ) / math.sqrt(NZ)).T).T
    forward_y = np.stack([right_table(y_even), right_table(y_odd)])
    backward_y = np.stack([right_table(y_even.T), right_table(y_odd.T)])
    forward_z = np.stack([left_table(z_even), left_table(z_odd)])
    backward_z = np.stack([left_table(z_even.T), left_table(z_odd.T)])
    order = np.zeros((NY, NY), dtype=jnp.bfloat16)
    for lane in range(NY):
        order[2 * (lane % HALF_Y) + lane // HALF_Y, lane] = 1
    return forward_y, forward_z, backward_y, backward_z, order


def iota(shape, axis):
    return lax.broadcasted_iota(jnp.int32, shape, axis)


def block_transpose(tiles):
    group = iota((8, LANES), 1) >> 4
    tiles = list(tiles)
    for bit in (1, 2, 4):
        unset = (group & bit) == 0
        for i in range(8):
            if i & bit:
                continue
            a, c = tiles[i], tiles[i | bit]
            tiles[i] = jnp.where(unset, a, pltpu.roll(c, 16 * bit, 1))
            tiles[i | bit] = jnp.where(unset, pltpu.roll(a, LANES - 16 * bit, 1), c)
    return tiles


def inner_transpose(tile):
    group, row = iota((8, LANES), 1) >> 4, iota((8, LANES), 0)
    for bit in (1, 2, 4):
        g, s = (group & bit) != 0, (row & bit) != 0
        down = pltpu.roll(pltpu.roll(tile, bit, 0), LANES - 16 * bit, 1)
        up = pltpu.roll(pltpu.roll(tile, 8 - bit, 0), 16 * bit, 1)
        tile = jnp.where(g == s, tile, jnp.where(s, down, up))
    return tile


def halves(values):
    high = values.astype(bf16)
    return high, (values - high.astype(f32)).astype(bf16)


def times_right(values, table):
    high, low = halves(values)
    return jnp.dot(jnp.concatenate([high, low, high], axis=1), table, preferred_element_type=f32)


def times_left(table, values):
    high, low = halves(values)
    pad = jnp.zeros((32, values.shape[1]), bf16)
    return jnp.dot(table, jnp.concatenate([high, low, high, pad], axis=0), preferred_element_type=f32)


def split_rows(values):
    grouped = values.reshape(ZB // 2, 2, 8, values.shape[1])
    return [grouped[:, parity].reshape(HALF_Z, values.shape[1]) for parity in range(2)]


def join_rows(even, odd):
    parts = [side.reshape(ZB // 2, 1, 8, side.shape[1]) for side in (even, odd)]
    return jnp.concatenate(parts, axis=1).reshape(NZ, even.shape[1])


def plane(ref, f):
    return jnp.concatenate([ref[0, f * NZ : (f + 1) * NZ], ref[1, f * NZ : (f + 1) * NZ]], axis=1)


def names_of(g):
    return [0, 1, 2] + [3 + 8 * p + 2 * g + e for p in range(2) for e in range(2)]


def dense_tiles(maps, coils, stacked, turned, emit, arrive=None):
    blank = jnp.zeros((8, LANES), f32)
    for g in range(4):
        if arrive is not None:
            arrive(g)
        stacked[g, 136:144] = blank
        for i, name in enumerate(names_of(g)):
            if name < 3:
                if g == 0:
                    rows = jnp.swapaxes(maps[name].reshape(8 * YB, ZB), 0, 1)
                    for other in range(4):
                        stacked[other, i * ZB : (i + 1) * ZB] = rows
            else:
                block = coils[(name - 3) // 8, (name - 3) % 8]
                stacked[g, i * ZB : (i + 1) * ZB] = jnp.swapaxes(block.reshape(8 * YB, ZB), 0, 1)
        turned[g] = jnp.swapaxes(stacked[g, :LANES], 0, 1)
        for j in range(MAIN):
            emit(g, j, turned[g, pl.ds(j, 8, stride=YB), :])
        for v in range(2):
            emit(g, MAIN + v, inner_transpose(stacked[g, LANES + 8 * v : LANES + 8 * v + 8]))


def pack_kernel(
    times, maps_in, coils_in, point_maps, point_coils,
    send, dense,
    maps, coils, of_maps, of_coils, stamp, stacked, turned, sems,
):
    t = lax.axis_index("ti")
    maps_copies = [
        pltpu.make_async_copy(maps_in, maps, sems.at[9]),
        pltpu.make_async_copy(times, stamp, sems.at[10]),
    ]
    coils_copies = [
        pltpu.make_async_copy(
            coils_in.at[p, pl.ds(2 * g, 2)], coils.at[p, pl.ds(2 * g, 2)], sems.at[11 + 2 * g + p]
        )
        for g in range(4)
        for p in range(2)
    ]
    point_copies = []
    items = []
    for i in range(ITEMS):
        item = jnp.minimum((t >> 1) * 18 + 2 * i + (t & 1), PAIRS - 1)
        f = item // ZB
        z = item - f * ZB
        q = jnp.maximum(f - 3, 0)
        items.append(f)
        point_copies.append(
            pltpu.make_async_copy(point_maps.at[jnp.minimum(f, 2), z], of_maps.at[i], sems.at[19 + i])
        )
        point_copies.append(
            pltpu.make_async_copy(point_coils.at[q >> 1, :, q & 1, z], of_coils.at[i], sems.at[28 + i])
        )
    for copy in point_copies + maps_copies + coils_copies:
        copy.start()
    for copy in point_copies:
        copy.wait()
    for i in range(ITEMS):
        for g in range(4):
            tile = jnp.where(items[i] < 3, of_maps[i], of_coils[i, g])
            for m in (g, g + 4):
                for half in range(2):
                    first = 8 * m * WHOLE + TILES + 2 * i + half
                    send[pl.ds(first, 8, stride=WHOLE), :] = tile[:, half * LANES : (half + 1) * LANES]
    for copy in maps_copies:
        copy.wait()
    lane = iota((8, LANES), 1)
    spare = jnp.where(lane == 64, stamp[0], jnp.where(lane == 65, stamp[1], 0.0))

    def emit(g, u, tile):
        dense[g, u] = tile
        if u == TILES - 1:
            tile = jnp.where(lane < 64, tile, spare)
        for m in (g, g + 4):
            send[pl.ds(8 * m * WHOLE + u, 8, stride=WHOLE), :] = tile

    def arrive(g):
        for copy in coils_copies[2 * g : 2 * g + 2]:
            copy.wait()

    dense_tiles(maps, coils, stacked, turned, emit, arrive)


def dense_kernel(maps_in, coils_in, dense, maps, coils, stacked, turned, sems):
    copies = [
        pltpu.make_async_copy(maps_in, maps, sems.at[0]),
        pltpu.make_async_copy(coils_in, coils, sems.at[1]),
    ]
    for copy in copies:
        copy.start()
    for copy in copies:
        copy.wait()

    def emit(g, u, tile):
        dense[g, u] = tile

    dense_tiles(maps, coils, stacked, turned, emit)


def unpack(part, c, point, direction, rest):
    for y in range(4):
        for half in range(2):
            firsts = [WHOLE * (4 * (8 * half + i) + y) for i in range(8)]
            rows = [part[first : first + MAIN, :] for first in firsts]
            pairs = jnp.swapaxes(jnp.concatenate(rows, axis=0), 0, 1)
            direction[half, pl.ds(2 * y + c, LANES, stride=8), :] = pairs
    for v in range(2):
        rest[v, pl.ds(c, 64, stride=2), :] = part[pl.ds(MAIN + v, 64, stride=WHOLE), :]
    for i in range(ITEMS):
        for half in range(2):
            for m in range(8):
                n = 18 * m + 2 * i
                if n < PAIRS:
                    first = 8 * m * WHOLE + TILES + 2 * i + half
                    point[half, pl.ds(8 * n + c, 8, stride=2), :] = part[pl.ds(first, 8, stride=WHOLE), :]


def unpack_rest(direction, rest):
    for v in range(2):
        for half in range(2):
            tiles = [rest[v, 8 * (8 * half + i) : 8 * (8 * half + i) + 8] for i in range(8)]
            for member, tile in enumerate(block_transpose(tiles)):
                n = LANES + 8 * v + member
                if n < PAIRS:
                    direction[half, 8 * n : 8 * n + 8] = tile


def forward_bin(tau, point, direction, table_y, table_z, spectrum):
    amplitude = plane(point, 1)
    decays = jnp.exp(-tau * plane(point, 2))
    signal = plane(point, 0) - amplitude * decays
    change = plane(direction, 0) - plane(direction, 1) * decays + amplitude * tau * decays * plane(direction, 2)
    evens, odds = [], []
    for c in range(2):
        re = plane(point, 3 + c) * change + plane(direction, 3 + c) * signal
        im = plane(point, 5 + c) * change + plane(direction, 5 + c) * signal
        re_low, re_high, im_low, im_high = re[:, :HALF_Y], re[:, HALF_Y:], im[:, :HALF_Y], im[:, HALF_Y:]
        evens.append(jnp.concatenate([re_low + re_high, im_low + im_high], axis=1))
        odds.append(jnp.concatenate([re_low - re_high, im_low - im_high], axis=1))
    along_even = times_right(jnp.concatenate(evens, axis=0), table_y[0])
    along_odd = times_right(jnp.concatenate(odds, axis=0), table_y[1])
    for c in range(2):
        rows = slice(c * NZ, (c + 1) * NZ)
        re = jnp.concatenate([along_even[rows, :HALF_Y], along_odd[rows, :HALF_Y]], axis=1)
        im = jnp.concatenate([along_even[rows, HALF_Y:], along_odd[rows, HALF_Y:]], axis=1)
        parts = [
            times_left(table_z[parity], jnp.concatenate(pair, axis=0))
            for parity, pair in enumerate(zip(split_rows(re), split_rows(im)))
        ]
        for part in range(2):
            a, b = (side[part * HALF_Z : (part + 1) * HALF_Z] for side in parts)
            spectrum[c, part, :HALF_Z] = a + b
            spectrum[c, part, HALF_Z:] = a - b


def backward_bin(tau, mask, spectrum, point, table_y, table_z, order, total):
    weights = jnp.dot(mask.astype(f32).astype(bf16), order[...], preferred_element_type=f32)
    evens, odds = [], []
    for c in range(2):
        plus, minus = [], []
        for part in range(2):
            values = spectrum[c, part] * weights
            plus.append(values[:HALF_Z] + values[HALF_Z:])
            minus.append(values[:HALF_Z] - values[HALF_Z:])
        for parity, side in enumerate((plus, minus)):
            out = times_left(table_z[parity], jnp.concatenate(side, axis=0))
            re, im = out[:HALF_Z], out[HALF_Z:]
            evens.append(jnp.concatenate([re[:, :HALF_Y], im[:, :HALF_Y]], axis=1))
            odds.append(jnp.concatenate([re[:, HALF_Y:], im[:, HALF_Y:]], axis=1))
    from_even = times_right(jnp.concatenate(evens, axis=0), table_y[0])
    from_odd = times_right(jnp.concatenate(odds, axis=0), table_y[1])
    low, high = from_even + from_odd, from_even - from_odd

    def add(f, values):
        for half in range(2):
            total[half, f * NZ : (f + 1) * NZ] += values[:, half * LANES : (half + 1) * LANES]

    amplitude = plane(point, 1)
    decays = jnp.exp(-tau * plane(point, 2))
    signal = plane(point, 0) - amplitude * decays
    projected = None
    for c in range(2):
        sides = []
        for lanes in (slice(0, HALF_Y), slice(HALF_Y, NY)):
            value = jnp.concatenate([low[:, lanes], high[:, lanes]], axis=1)
            first = 2 * c * HALF_Z
            sides.append(join_rows(value[first : first + HALF_Z], value[first + HALF_Z : first + NZ]))
        re, im = sides
        term = plane(point, 3 + c) * re + plane(point, 5 + c) * im
        projected = term if projected is None else projected + term
        add(3 + c, signal * re)
        add(5 + c, signal * im)
    add(0, projected)
    faded = decays * projected
    add(1, -faded)
    add(2, amplitude * (tau * faded))


def pack_sums(core, total, sent, rest, mine, theirs):
    for k in range(8):
        place = (k & 1) ^ core
        for half in range(2):
            pairs = jnp.swapaxes(total[half, pl.ds(k, LANES, stride=8), :], 0, 1)
            for i in range(8):
                first = TILES * (4 * (8 * half + i) + (k >> 1))
                sent[place, first : first + MAIN, :] = pairs[YB * i : YB * (i + 1)]
    for v in range(2):
        for half in range(2):
            tiles = []
            for member in range(8):
                n = min(LANES + 8 * v + member, PAIRS - 1)
                tiles.append(total[half, 8 * n : 8 * n + 8])
            for i, tile in enumerate(block_transpose(tiles)):
                rest[v, 8 * (8 * half + i) : 8 * (8 * half + i) + 8] = tile
        for c in range(2):
            rows = pl.ds(MAIN + v, 64, stride=TILES)
            sent[c ^ core, rows, :] = rest[v, pl.ds(c, 64, stride=2), :]
    mine[...] = sent[0]
    theirs[...] = sent[1]


def first_kernel(*refs):
    own, other, mask, *tables_in = refs[:8]
    spectrum, last, point, taus, total, backward_y, backward_z, order = refs[8:16]
    direction, rest, forward_y, forward_z, kept, sems = refs[16:]
    step = pl.program_id(0)
    t, core = lax.axis_index("ti"), lax.axis_index("kz") & 1
    slot = step & 1
    tables = (forward_y, forward_z, backward_y, backward_z, order)
    copies = [pltpu.make_async_copy(a, b, sems.at[2 + i]) for i, (a, b) in enumerate(zip(tables_in, tables))]

    def store(at, side):
        return pltpu.make_async_copy(kept.at[side], spectrum.at[at - FULL], sems.at[side])

    @pl.when(step == 0)
    def _():
        for copy in copies:
            copy.start()
        total[...] = jnp.zeros_like(total)
        unpack(own, core, point, direction, rest)
        unpack(other, 1 - core, point, direction, rest)
        unpack_rest(direction, rest)
        for copy in copies:
            copy.wait()

    @pl.when(step >= FULL + 2)
    def _():
        store(step - 2, slot).wait()

    spread = (step & 3) ^ ((step & 2) >> 1)
    bin_of = ((t & 12) | ((t + spread) & 3)) ^ (step & 4)
    block = rest[1, pl.ds(pl.multiple_of(bin_of * 8, 8), 8), :]
    chosen = (iota((8, LANES), 0) == 0) & (iota((8, LANES), 1) == 64 + core)
    tau = jnp.sum(jnp.where(chosen, block, 0.0), axis=(0, 1), keepdims=True)

    taus[0] = jnp.broadcast_to(tau, (8, LANES))

    @pl.when(step < BINS - 1)
    def _():
        forward_bin(tau, point, direction, forward_y, forward_z, kept.at[slot])

    @pl.when(step < FULL)
    def _():
        backward_bin(tau, mask[0], kept.at[slot], point, backward_y, backward_z, order, total)

    @pl.when((step >= FULL) & (step < BINS - 1))
    def _():
        store(step, slot).start()

    @pl.when(step == BINS - 1)
    def _():
        forward_bin(tau, point, direction, forward_y, forward_z, last)
        store(BINS - 2, BINS & 1).wait()


def second_kernel(
    mask, spectrum, last, point, taus, total_in, table_y, table_z, order,
    mine, theirs,
    total, sent, rest, kept, sems,
):
    step = pl.program_id(0)
    core = lax.axis_index("kz") & 1
    slot = step & 1

    def load(at):
        return pltpu.make_async_copy(spectrum.at[at - 1], kept.at[at & 1], sems.at[at & 1])

    @pl.when(step == 0)
    def _():
        total[...] = total_in[...]
        kept[0] = last[...]

    @pl.when(step < BINS - FULL - 1)
    def _():
        load(step + 1).start()

    @pl.when(step > 0)
    def _():
        load(step).wait()

    tau = taus[0, 0:1, 0:1]
    backward_bin(tau, mask[0], kept.at[slot], point, table_y, table_z, order, total)

    @pl.when(step == BINS - FULL - 1)
    def _():
        pack_sums(core, total, sent, rest, mine, theirs)


def sums_kernel(received, direction, residual, applied_out, out_sums, applied, sems):
    lane = iota((8, LANES), 1)
    sums = [jnp.zeros((8, LANES), f32) for _ in range(4)]
    copies = []
    for u in range(TILES):
        sides = []
        for g in range(4):
            upper, lower = (received[pl.ds(8 * m * TILES + u, 8, stride=TILES), :] for m in (g, g + 4))
            sides.append(upper + lower)
        if u < MAIN:
            maps = sides[0] + sides[1] + sides[2] + sides[3]
        for g in range(4):
            d, r, value = direction[g, u], residual[g, u], sides[g]
            if u < MAIN:
                of_maps = lane < 3 * ZB
                if g == 0:
                    value = jnp.where(of_maps, maps, value)
                else:
                    d, r, value = (jnp.where(of_maps, 0.0, a) for a in (d, r, value))
            elif u == TILES - 1:
                d, r, value = (jnp.where(lane < 64, a, 0.0) for a in (d, r, value))
            q = value + regular_weight * d
            applied[u, g] = q
            for i, (a, b) in enumerate(((r, r), (d, q), (r, q), (q, q))):
                sums[i] = sums[i] + a * b
        if u % 6 == 5:
            part = pl.ds(u - 5, 6)
            copies.append(pltpu.make_async_copy(applied.at[part], applied_out.at[part], sems.at[u // 6]))
            copies[-1].start()
    line = jnp.zeros((1, LANES), f32)
    for i in range(4):
        value = jnp.sum(sums[i], axis=(0, 1), keepdims=True)
        line = jnp.where(iota((1, LANES), 1) == i, value, line)
    out_sums[...] = jnp.broadcast_to(line, (LANES, LANES))
    for copy in copies:
        copy.wait()


def native_kernel(
    dense_in, dir_coils, res_coils, maps_out, fields, dense, maps, stacked, turned, sems
):
    copies = [
        pltpu.make_async_copy(source.at[p], fields.at[pl.ds(first + 8 * p, 8)], sems.at[2 * i + p])
        for i, (source, first) in enumerate(((dir_coils, 16), (res_coils, 32)))
        for p in range(2)
    ]
    copies.append(pltpu.make_async_copy(dense_in, dense, sems.at[5]))
    copies[-1].start()
    for copy in copies[:-1]:
        copy.start()
    copies.pop().wait()
    for g in range(4):
        for j in range(MAIN):
            turned[g, pl.ds(j, 8, stride=YB), :] = dense[j, g]
        stacked[g, :LANES] = jnp.swapaxes(turned[g], 0, 1)
        for v in range(2):
            stacked[g, LANES + 8 * v : LANES + 8 * v + 8] = inner_transpose(dense[MAIN + v, g])
        for i, name in enumerate(names_of(g)):
            if name < 3 and g:
                continue
            block = jnp.swapaxes(stacked[g, i * ZB : (i + 1) * ZB], 0, 1).reshape(XS, YB, ZB)
            if name < 3:
                maps[name] = block
            else:
                fields[name - 3] = block
    copies.append(pltpu.make_async_copy(maps, maps_out, sems.at[4]))
    copies[-1].start()
    for copy in copies:
        copy.wait()


def step_kernel(sums, fields, app_maps, dir_maps, res_maps, *refs):
    outs, (maps, made_maps, made_coils, sems) = refs[:4], refs[4:]
    copies = [
        pltpu.make_async_copy(source, maps.at[i], sems.at[i])
        for i, source in enumerate((app_maps, dir_maps, res_maps))
    ]
    for copy in copies:
        copy.start()
    line = jnp.sum(sums[...], axis=0, keepdims=True)
    lane = iota((1, LANES), 1)
    old, curve, cross, square = (
        jnp.sum(jnp.where(lane == i, line, 0.0), axis=1, keepdims=True) for i in range(4)
    )
    size = old / curve
    new = old - 2.0 * size * cross + size * size * square
    ratio = (new / old).reshape(1, 1, 1)
    size = size.reshape(1, 1, 1)
    stores = []
    for first in range(0, 16, 4):
        for coil in range(first, first + 4):
            fresh = fields[32 + coil] - size * fields[coil]
            made_coils[0, coil] = fresh
            made_coils[1, coil] = fresh + ratio * fields[16 + coil]
        part, rows = first // 8, pl.ds(first % 8, 4)
        for i in range(2):
            stores.append(
                pltpu.make_async_copy(
                    made_coils.at[i, pl.ds(first, 4)], outs[1 + 2 * i].at[part, rows], sems.at[3 + len(stores)]
                )
            )
            stores[-1].start()
    for copy in copies:
        copy.wait()
    for f in range(3):
        fresh = maps[2, f] - size * maps[0, f]
        made_maps[0, f] = fresh
        made_maps[1, f] = fresh + ratio * maps[1, f]
    for i in range(2):
        stores.append(pltpu.make_async_copy(made_maps.at[i], outs[2 * i], sems.at[3 + len(stores)]))
        stores[-1].start()
    for copy in stores:
        copy.wait()


def struct(*shape):
    return jax.ShapeDtypeStruct(shape, f32)


HBM = pl.BlockSpec(memory_space=pltpu.HBM)
VMEM = pl.BlockSpec(memory_space=pltpu.VMEM)
SCRATCH_STACKED = pltpu.VMEM((4, 144, LANES), f32)
SCRATCH_TURNED = pltpu.VMEM((4, LANES, LANES), f32)


def params():
    return pltpu.CompilerParams(vmem_limit_bytes=VMEM_LIMIT)


def cost(micros):
    return pl.CostEstimate(flops=int(micros * 4e8), bytes_accessed=int(micros * 2e6), transcendentals=0)


def constant_block(shape):
    return pl.BlockSpec(shape, lambda s: (0,) * len(shape))


def stepping_block(shape):
    return pl.BlockSpec((1,) + shape, lambda s: (s,) + (0,) * len(shape))


def in_hbm(*values):
    return tuple(pltpu.with_memory_space_constraint(value, pltpu.HBM) for value in values)


def in_vmem(*values):
    return tuple(pltpu.with_memory_space_constraint(value, pltpu.VMEM) for value in values)


def far(*shape):
    return pltpu.HBM(shape, f32)


def near(*shape):
    return pltpu.VMEM(shape, f32)


def core_swap(values):
    return lax.ppermute(values, "kz", [(i, i ^ 1) for i in range(8)])


def by_parity(values):
    groups = [[i for i in range(128) if i & 1 == c] for c in range(2)]
    messages = values.reshape(64, 1, values.shape[0] // 64 * LANES)
    return lax.all_to_all(messages, AXES, 0, 0, axis_index_groups=groups).reshape(values.shape)


def shards(
    point_maps,
    point_coils,
    direction_maps,
    direction_coils,
    residual_maps,
    residual_coils,
    inversion_times,
    sampling_mask,
):
    forward_y, forward_z, backward_y, backward_z, order = (jnp.asarray(table) for table in make_tables())
    dir_maps, dir_coils = jnp.swapaxes(direction_maps, 2, 3), jnp.swapaxes(direction_coils, 3, 4)
    res_maps, res_coils = jnp.swapaxes(residual_maps, 2, 3), jnp.swapaxes(residual_coils, 3, 4)
    pnt_maps = jnp.swapaxes(point_maps, 1, 2)
    pnt_coils = jnp.swapaxes(point_coils, 2, 3).reshape(2, 4, 2, ZB, XS, NY)

    send, dir_dense = pl.pallas_call(
        pack_kernel,
        out_shape=(
            struct(64 * WHOLE, LANES),
            near(4, TILES, 8, LANES),
        ),
        in_specs=[HBM] * 5,
        out_specs=(VMEM, VMEM),
        scratch_shapes=[
            pltpu.VMEM(dir_maps.shape, f32),
            pltpu.VMEM(dir_coils.shape, f32),
            pltpu.VMEM((ITEMS, 8, NY), f32),
            pltpu.VMEM((ITEMS, 4, 8, NY), f32),
            pltpu.SMEM((2,), f32),
            SCRATCH_STACKED,
            SCRATCH_TURNED,
            pltpu.SemaphoreType.DMA((37,)),
        ],
        compiler_params=params(),
        cost_estimate=cost(4),
        name="pack",
    )(*in_hbm(inversion_times, dir_maps, dir_coils, pnt_maps, pnt_coils))

    def densify(maps, coils):
        return pl.pallas_call(
            dense_kernel,
            out_shape=near(4, TILES, 8, LANES),
            in_specs=[HBM] * 2,
            out_specs=VMEM,
            scratch_shapes=[
                pltpu.VMEM(maps.shape, f32),
                pltpu.VMEM(coils.shape, f32),
                SCRATCH_STACKED,
                SCRATCH_TURNED,
                pltpu.SemaphoreType.DMA((2,)),
            ],
            compiler_params=params(),
            cost_estimate=cost(3),
            name="dense",
        )(*in_hbm(maps, coils))

    own = by_parity(send)
    res_dense = densify(res_maps, res_coils)
    own_mask = lax.dynamic_index_in_dim(sampling_mask, lax.axis_index("kz") & 1, 0, keepdims=False)
    own_mask, res_dense = lax.optimization_barrier((own_mask, res_dense))

    def from_ti(values, shift, flip):
        return lax.ppermute(values, "ti", [(((i & 12) | ((i + shift) & 3)) ^ flip, i) for i in range(16)])

    near_masks = jnp.stack([own_mask] + [from_ti(own_mask, shift, 0) for shift in (1, 3, 2)])
    own, near_masks = lax.optimization_barrier((own, near_masks))
    other = core_swap(own)
    far_masks = from_ti(near_masks, 0, 4)
    planes = (2, FEATURES * NZ, LANES)
    tables = (forward_y, forward_z, backward_y, backward_z, order)
    sums_shape = struct(64 * TILES, LANES)
    sent_scratch = pltpu.VMEM((2, 64 * TILES, LANES), f32)
    spectrum, last, point, taus, total, *near_tables = pl.pallas_call(
        first_kernel,
        grid=(BINS,),
        out_shape=(
            far(BINS - FULL - 1, 2, 2, NZ, NY),
            near(2, 2, NZ, NY),
            near(*planes),
            near(BINS, 8, LANES),
            near(*planes),
            *[pltpu.VMEM(table.shape, bf16) for table in tables[2:]],
        ),
        in_specs=[constant_block(own.shape)] * 2
        + [pl.BlockSpec((1, NZ, NY), lambda s: (jnp.minimum(s, FULL - 1), 0, 0))]
        + [HBM] * 5,
        out_specs=(
            HBM,
            constant_block((2, 2, NZ, NY)),
            constant_block(planes),
            stepping_block((8, LANES)),
            constant_block(planes),
            *[constant_block(table.shape) for table in tables[2:]],
        ),
        scratch_shapes=[
            pltpu.VMEM(planes, f32),
            pltpu.VMEM((2, LANES, LANES), f32),
            pltpu.VMEM(forward_y.shape, bf16),
            pltpu.VMEM(forward_z.shape, bf16),
            pltpu.VMEM((2, 2, 2, NZ, NY), f32),
            pltpu.SemaphoreType.DMA((7,)),
        ],
        compiler_params=params(),
        cost_estimate=cost(15),
        name="first",
    )(own, other, near_masks, *in_hbm(*tables))

    def bin_block(shape, first):
        return pl.BlockSpec((1,) + shape, lambda s: (jnp.where(s == 0, BINS - 1, s + FULL - 1) - first, 0, 0))

    mine, theirs = pl.pallas_call(
        second_kernel,
        grid=(BINS - FULL,),
        out_shape=(sums_shape, sums_shape),
        in_specs=[
            bin_block((NZ, NY), FULL),
            HBM,
            constant_block((2, 2, NZ, NY)),
            constant_block(planes),
            bin_block((8, LANES), 0),
            constant_block(planes),
        ]
        + [constant_block(table.shape) for table in tables[2:]],
        out_specs=(constant_block((64 * TILES, LANES)),) * 2,
        scratch_shapes=[
            pltpu.VMEM(planes, f32),
            sent_scratch,
            pltpu.VMEM((2, LANES, LANES), f32),
            pltpu.VMEM((2, 2, 2, NZ, NY), f32),
            pltpu.SemaphoreType.DMA((2,)),
        ],
        compiler_params=params(),
        cost_estimate=cost(8),
        name="second",
    )(far_masks, *in_hbm(spectrum), *in_vmem(last, point, taus, total, *near_tables))

    received = by_parity(mine + core_swap(theirs))
    app_dense, sums = pl.pallas_call(
        sums_kernel,
        out_shape=(far(TILES, 4, 8, LANES), near(128, LANES)),
        in_specs=[VMEM] * 3,
        out_specs=(HBM, VMEM),
        scratch_shapes=[pltpu.VMEM((TILES, 4, 8, LANES), f32), pltpu.SemaphoreType.DMA((3,))],
        compiler_params=params(),
        cost_estimate=cost(1),
        name="sums",
    )(received, *in_vmem(dir_dense, res_dense))
    all_sums = lax.all_to_all(sums.reshape(128, 1, LANES), AXES, 0, 0).reshape(128, LANES)

    maps_shape, coils_shape = far(*dir_maps.shape), far(*dir_coils.shape)
    app_maps, fields = pl.pallas_call(
        native_kernel,
        out_shape=(far(*dir_maps.shape), near(48, XS, YB, ZB)),
        in_specs=[HBM] * 3,
        out_specs=(HBM, VMEM),
        scratch_shapes=[
            pltpu.VMEM((TILES, 4, 8, LANES), f32),
            pltpu.VMEM(dir_maps.shape, f32),
            SCRATCH_STACKED,
            SCRATCH_TURNED,
            pltpu.SemaphoreType.DMA((6,)),
        ],
        compiler_params=params(),
        cost_estimate=cost(3),
        name="native",
    )(*in_hbm(app_dense, dir_coils, res_coils))

    outs = pl.pallas_call(
        step_kernel,
        out_shape=(maps_shape, coils_shape, maps_shape, coils_shape),
        in_specs=[VMEM] * 2 + [HBM] * 3,
        out_specs=(HBM,) * 4,
        scratch_shapes=[
            pltpu.VMEM((3,) + dir_maps.shape, f32),
            pltpu.VMEM((2,) + dir_maps.shape, f32),
            pltpu.VMEM((2, 16, XS, YB, ZB), f32),
            pltpu.SemaphoreType.DMA((13,)),
        ],
        compiler_params=params(),
        cost_estimate=cost(2),
        name="step",
    )(all_sums, *in_vmem(fields), *in_hbm(app_maps, dir_maps, res_maps))
    return tuple(jnp.swapaxes(out, -2, -1) for out in outs)


def solution(mesh):
    in_specs = (
        P(None, None, "kz", None),
        P(None, None, None, "kz", None),
        P(None, None, "kz", "ti"),
        P(None, None, None, "kz", "ti"),
        P(None, None, "kz", "ti"),
        P(None, None, None, "kz", "ti"),
        P("ti"),
        P("ti", None, None),
    )
    out_specs = (
        P(None, None, "kz", "ti"),
        P(None, None, None, "kz", "ti"),
        P(None, None, "kz", "ti"),
        P(None, None, None, "kz", "ti"),
    )
    return jax.shard_map(shards, mesh=mesh, in_specs=in_specs, out_specs=out_specs, check_vma=False)
```

```python
import math

import jax
import jax.numpy as jnp
import numpy as np
from jax import lax
from jax.experimental import pallas as pl
from jax.experimental.pallas import tpu as pltpu
from jax.sharding import PartitionSpec as P

regular_weight = 2.0
AXES = ("ti", "kz")
NZ, NY, ZB, YB, XS = 160, 256, 20, 16, 8
HALF_Z, HALF_Y = NZ // 2, NY // 2
LANES = 128
FEATURES = 7
PAIRS = FEATURES * ZB
MAIN = 16
TILES = 18
MSG = TILES * LANES
ITEMS = 9
BINS = 8
NEAR = 5
STEPS = ((0, 0), (0, 1), (0, 3), (1, 0), (3, 0), (1, 1), (1, 3), (2, 0))
WHOLE = 2 * TILES
VMEM_LIMIT = 32 * 1024 * 1024
f32 = jnp.float32
bf16 = jnp.bfloat16


def split_pair(table):
    high = table.astype(np.float32).astype(jnp.bfloat16)
    low = (table - high.astype(np.float64)).astype(np.float32).astype(jnp.bfloat16)
    return high, low


def real_form(matrix):
    return np.block([[matrix.real, matrix.imag], [-matrix.imag, matrix.real]])


def right_table(table):
    high, low = split_pair(table)
    return np.concatenate([high, high, low], axis=0)


def left_table(table):
    high, low = split_pair(table)
    pad = np.zeros((table.shape[0], 32), dtype=jnp.bfloat16)
    return np.concatenate([high, high, low, pad], axis=1)


def z_of_rows():
    rows = np.arange(HALF_Z)
    return (rows % 8) * ZB + 2 * (rows // 8)


def make_tables():
    n, m = np.arange(HALF_Y)[:, None], np.arange(HALF_Y)[None, :]
    y_even = real_form(np.exp(-2j * np.pi * (n * (2 * m) % NY) / NY) / math.sqrt(NY))
    y_odd = real_form(np.exp(-2j * np.pi * (n * (2 * m + 1) % NY) / NY) / math.sqrt(NY))
    spots, freq = z_of_rows()[None, :], np.arange(HALF_Z)[:, None]
    z_even = real_form((np.exp(-2j * np.pi * (freq * spots % NZ) / NZ) / math.sqrt(NZ)).T).T
    z_odd = real_form((np.exp(-2j * np.pi * (freq * (spots + 1) % NZ) / NZ) / math.sqrt(NZ)).T).T
    forward_y = np.stack([right_table(y_even), right_table(y_odd)])
    backward_y = np.stack([right_table(y_even.T), right_table(y_odd.T)])
    forward_z = np.stack([left_table(z_even), left_table(z_odd)])
    backward_z = np.stack([left_table(z_even.T), left_table(z_odd.T)])
    order = np.zeros((NY, NY), dtype=jnp.bfloat16)
    for lane in range(NY):
        order[2 * (lane % HALF_Y) + lane // HALF_Y, lane] = 1
    return forward_y, forward_z, backward_y, backward_z, order


def iota(shape, axis):
    return lax.broadcasted_iota(jnp.int32, shape, axis)


def block_transpose(tiles):
    group = iota((8, LANES), 1) >> 4
    tiles = list(tiles)
    for bit in (1, 2, 4):
        unset = (group & bit) == 0
        for i in range(8):
            if i & bit:
                continue
            a, c = tiles[i], tiles[i | bit]
            tiles[i] = jnp.where(unset, a, pltpu.roll(c, 16 * bit, 1))
            tiles[i | bit] = jnp.where(unset, pltpu.roll(a, LANES - 16 * bit, 1), c)
    return tiles


def inner_transpose(tile):
    group, row = iota((8, LANES), 1) >> 4, iota((8, LANES), 0)
    for bit in (1, 2, 4):
        g, s = (group & bit) != 0, (row & bit) != 0
        down = pltpu.roll(pltpu.roll(tile, bit, 0), LANES - 16 * bit, 1)
        up = pltpu.roll(pltpu.roll(tile, 8 - bit, 0), 16 * bit, 1)
        tile = jnp.where(g == s, tile, jnp.where(s, down, up))
    return tile


def halves(values):
    high = values.astype(bf16)
    return high, (values - high.astype(f32)).astype(bf16)


def times_right(values, table):
    high, low = halves(values)
    return jnp.dot(jnp.concatenate([high, low, high], axis=1), table, preferred_element_type=f32)


def times_left(table, values):
    high, low = halves(values)
    pad = jnp.zeros((32, values.shape[1]), bf16)
    return jnp.dot(table, jnp.concatenate([high, low, high, pad], axis=0), preferred_element_type=f32)


def split_rows(values):
    grouped = values.reshape(ZB // 2, 2, 8, values.shape[1])
    return [grouped[:, parity].reshape(HALF_Z, values.shape[1]) for parity in range(2)]


def join_rows(even, odd):
    parts = [side.reshape(ZB // 2, 1, 8, side.shape[1]) for side in (even, odd)]
    return jnp.concatenate(parts, axis=1).reshape(NZ, even.shape[1])


def plane(ref, f):
    return jnp.concatenate([ref[0, f * NZ : (f + 1) * NZ], ref[1, f * NZ : (f + 1) * NZ]], axis=1)


def pairs_of(g):
    return (g, 4 + (g ^ 1))


def names_of(g):
    return [0, 1, 2] + [3 + 8 * p + 2 * g + e for p in range(2) for e in range(2)]


def dense_tiles(maps, coils, stacked, turned, emit, arrive=None):
    blank = jnp.zeros((8, LANES), f32)
    for g in range(4):
        if arrive is not None:
            arrive(g)
        stacked[g, 136:144] = blank
        for i, name in enumerate(names_of(g)):
            if name < 3:
                if g == 0:
                    rows = jnp.swapaxes(maps[name].reshape(8 * YB, ZB), 0, 1)
                    for other in range(4):
                        stacked[other, i * ZB : (i + 1) * ZB] = rows
            else:
                block = coils[(name - 3) // 8, (name - 3) % 8]
                stacked[g, i * ZB : (i + 1) * ZB] = jnp.swapaxes(block.reshape(8 * YB, ZB), 0, 1)
        turned[g] = jnp.swapaxes(stacked[g, :LANES], 0, 1)
        for j in range(MAIN):
            emit(g, j, turned[g, pl.ds(j, 8, stride=YB), :])
        for v in range(2):
            emit(g, MAIN + v, inner_transpose(stacked[g, LANES + 8 * v : LANES + 8 * v + 8]))


def pack_kernel(
    times, maps_in, coils_in, point_maps, point_coils,
    send_out, dense,
    send, maps, coils, of_maps, of_coils, stamp, stacked, turned, sems,
):
    t = lax.axis_index("ti")
    maps_copies = [
        pltpu.make_async_copy(maps_in, maps, sems.at[9]),
        pltpu.make_async_copy(times, stamp, sems.at[10]),
    ]
    coils_copies = [
        pltpu.make_async_copy(
            coils_in.at[p, pl.ds(2 * g, 2)], coils.at[p, pl.ds(2 * g, 2)], sems.at[11 + 2 * g + p]
        )
        for g in range(4)
        for p in range(2)
    ]
    point_copies = []
    items = []
    for i in range(ITEMS):
        item = jnp.minimum((t >> 1) * 18 + 2 * i + (t & 1), PAIRS - 1)
        f = item // ZB
        z = item - f * ZB
        q = jnp.maximum(f - 3, 0)
        items.append(f)
        point_copies.append(
            pltpu.make_async_copy(point_maps.at[jnp.minimum(f, 2), z], of_maps.at[i], sems.at[19 + i])
        )
        point_copies.append(
            pltpu.make_async_copy(point_coils.at[q >> 1, :, q & 1, z], of_coils.at[i], sems.at[28 + i])
        )
    for copy in point_copies + maps_copies + coils_copies:
        copy.start()
    for copy in point_copies:
        copy.wait()
    for copy in maps_copies:
        copy.wait()
    lane = iota((8, LANES), 1)
    spare = jnp.where(lane == 64, stamp[0], jnp.where(lane == 65, stamp[1], 0.0))

    stores = []

    def emit(g, u, tile):
        dense[g, u] = tile
        if u == TILES - 1:
            tile = jnp.where(lane < 64, tile, spare)
        for m in pairs_of(g):
            send[pl.ds(8 * m * WHOLE + u, 8, stride=WHOLE), :] = tile
        if u == TILES - 1:
            for m in pairs_of(g):
                rows = pl.ds(8 * m * WHOLE, 8 * WHOLE)
                stores.append(pltpu.make_async_copy(send.at[rows], send_out.at[rows], sems.at[len(stores)]))
                stores[-1].start()

    def arrive(g):
        for i in range(ITEMS):
            tile = jnp.where(items[i] < 3, of_maps[i], of_coils[i, g])
            for m in pairs_of(g):
                for half in range(2):
                    first = 8 * m * WHOLE + TILES + 2 * i + half
                    send[pl.ds(first, 8, stride=WHOLE), :] = tile[:, half * LANES : (half + 1) * LANES]
        for copy in coils_copies[2 * g : 2 * g + 2]:
            copy.wait()

    dense_tiles(maps, coils, stacked, turned, emit, arrive)
    for copy in stores:
        copy.wait()


def dense_kernel(maps_in, coils_in, dense, maps, coils, stacked, turned, sems):
    copies = [
        pltpu.make_async_copy(maps_in, maps, sems.at[0]),
        pltpu.make_async_copy(coils_in, coils, sems.at[1]),
    ]
    for copy in copies:
        copy.start()
    for copy in copies:
        copy.wait()

    def emit(g, u, tile):
        dense[g, u] = tile

    dense_tiles(maps, coils, stacked, turned, emit)


def unpack(part, c, point, direction, rest):
    for y in range(4):
        for half in range(2):
            firsts = [WHOLE * (4 * (8 * half + i) + y) for i in range(8)]
            rows = [part[first : first + MAIN, :] for first in firsts]
            pairs = jnp.swapaxes(jnp.concatenate(rows, axis=0), 0, 1)
            direction[half, pl.ds(2 * y + c, LANES, stride=8), :] = pairs
    for v in range(2):
        rest[v, pl.ds(c, 64, stride=2), :] = part[pl.ds(MAIN + v, 64, stride=WHOLE), :]
    for i in range(ITEMS):
        for half in range(2):
            for m in range(8):
                n = 18 * m + 2 * i
                if n < PAIRS:
                    first = 8 * m * WHOLE + TILES + 2 * i + half
                    point[half, pl.ds(8 * n + c, 8, stride=2), :] = part[pl.ds(first, 8, stride=WHOLE), :]


def unpack_rest(direction, rest):
    for v in range(2):
        for half in range(2):
            tiles = [rest[v, 8 * (8 * half + i) : 8 * (8 * half + i) + 8] for i in range(8)]
            for member, tile in enumerate(block_transpose(tiles)):
                n = LANES + 8 * v + member
                if n < PAIRS:
                    direction[half, 8 * n : 8 * n + 8] = tile


def model_terms(tau, point):
    decays = jnp.exp(-tau * plane(point, 2))
    return decays, plane(point, 0) - plane(point, 1) * decays


def forward_bin(tau, point, direction, table_y, table_z, spectrum):
    amplitude = plane(point, 1)
    decays, signal = model_terms(tau, point)
    change = plane(direction, 0) - plane(direction, 1) * decays + amplitude * tau * decays * plane(direction, 2)
    evens, odds = [], []
    for c in range(2):
        re = plane(point, 3 + c) * change + plane(direction, 3 + c) * signal
        im = plane(point, 5 + c) * change + plane(direction, 5 + c) * signal
        re_low, re_high, im_low, im_high = re[:, :HALF_Y], re[:, HALF_Y:], im[:, :HALF_Y], im[:, HALF_Y:]
        evens.append(jnp.concatenate([re_low + re_high, im_low + im_high], axis=1))
        odds.append(jnp.concatenate([re_low - re_high, im_low - im_high], axis=1))
    along_even = times_right(jnp.concatenate(evens, axis=0), table_y[0])
    along_odd = times_right(jnp.concatenate(odds, axis=0), table_y[1])
    for c in range(2):
        rows = slice(c * NZ, (c + 1) * NZ)
        re = jnp.concatenate([along_even[rows, :HALF_Y], along_odd[rows, :HALF_Y]], axis=1)
        im = jnp.concatenate([along_even[rows, HALF_Y:], along_odd[rows, HALF_Y:]], axis=1)
        parts = [
            times_left(table_z[parity], jnp.concatenate(pair, axis=0))
            for parity, pair in enumerate(zip(split_rows(re), split_rows(im)))
        ]
        for part in range(2):
            a, b = (side[part * HALF_Z : (part + 1) * HALF_Z] for side in parts)
            spectrum[c, part, :HALF_Z] = a + b
            spectrum[c, part, HALF_Z:] = a - b
    return decays, signal


def backward_bin(tau, decays, signal, mask, spectrum, point, table_y, table_z, order, total):
    weights = jnp.dot(mask.astype(f32).astype(bf16), order[...], preferred_element_type=f32)
    evens, odds = [], []
    for c in range(2):
        plus, minus = [], []
        for part in range(2):
            values = spectrum[c, part] * weights
            plus.append(values[:HALF_Z] + values[HALF_Z:])
            minus.append(values[:HALF_Z] - values[HALF_Z:])
        for parity, side in enumerate((plus, minus)):
            out = times_left(table_z[parity], jnp.concatenate(side, axis=0))
            re, im = out[:HALF_Z], out[HALF_Z:]
            evens.append(jnp.concatenate([re[:, :HALF_Y], im[:, :HALF_Y]], axis=1))
            odds.append(jnp.concatenate([re[:, HALF_Y:], im[:, HALF_Y:]], axis=1))
    from_even = times_right(jnp.concatenate(evens, axis=0), table_y[0])
    from_odd = times_right(jnp.concatenate(odds, axis=0), table_y[1])
    low, high = from_even + from_odd, from_even - from_odd

    def add(f, values):
        for half in range(2):
            total[half, f * NZ : (f + 1) * NZ] += values[:, half * LANES : (half + 1) * LANES]

    projected = None
    for c in range(2):
        sides = []
        for lanes in (slice(0, HALF_Y), slice(HALF_Y, NY)):
            value = jnp.concatenate([low[:, lanes], high[:, lanes]], axis=1)
            first = 2 * c * HALF_Z
            sides.append(join_rows(value[first : first + HALF_Z], value[first + HALF_Z : first + NZ]))
        re, im = sides
        term = plane(point, 3 + c) * re + plane(point, 5 + c) * im
        projected = term if projected is None else projected + term
        add(3 + c, signal * re)
        add(5 + c, signal * im)
    add(0, projected)
    faded = decays * projected
    add(1, -faded)
    add(2, plane(point, 1) * (tau * faded))


def pack_sums(core, total, sent, rest, mine, theirs):
    for k in range(8):
        place = (k & 1) ^ core
        for half in range(2):
            pairs = jnp.swapaxes(total[half, pl.ds(k, LANES, stride=8), :], 0, 1)
            for i in range(8):
                first = TILES * (4 * (8 * half + i) + (k >> 1))
                sent[place, first : first + MAIN, :] = pairs[YB * i : YB * (i + 1)]
    for v in range(2):
        for half in range(2):
            tiles = []
            for member in range(8):
                n = min(LANES + 8 * v + member, PAIRS - 1)
                tiles.append(total[half, 8 * n : 8 * n + 8])
            for i, tile in enumerate(block_transpose(tiles)):
                rest[v, 8 * (8 * half + i) : 8 * (8 * half + i) + 8] = tile
        for c in range(2):
            rows = pl.ds(MAIN + v, 64, stride=TILES)
            sent[c ^ core, rows, :] = rest[v, pl.ds(c, 64, stride=2), :]
    mine[...] = sent[0]
    theirs[...] = sent[1]


def first_kernel(*refs):
    own, other, *masks = refs[: 2 + NEAR]
    tables_in, refs = refs[2 + NEAR : 7 + NEAR], refs[7 + NEAR :]
    spectrum, last, point, taus, total, backward_y, backward_z, order = refs[:8]
    direction, rest, forward_y, forward_z, kept, mask, sems = refs[8:]
    step = pl.program_id(0)
    t, core = lax.axis_index("ti"), lax.axis_index("kz") & 1
    slot = step & 1

    def store(at, side):
        return pltpu.make_async_copy(kept.at[side], spectrum.at[at - NEAR], sems.at[side])

    @pl.when(step == 0)
    def _():
        tables = (forward_y, forward_z, backward_y, backward_z, order)
        copies = [pltpu.make_async_copy(a, b, sems.at[2 + i]) for i, (a, b) in enumerate(zip(tables_in, tables))]
        for copy in copies:
            copy.start()
        total[...] = jnp.zeros_like(total)
        unpack(own, core, point, direction, rest)
        unpack(other, 1 - core, point, direction, rest)
        unpack_rest(direction, rest)
        for copy in copies:
            copy.wait()

    @pl.when(step >= NEAR + 2)
    def _():
        store(step - 2, slot).wait()

    for n in range(NEAR):

        @pl.when(step == n)
        def _():
            mask[...] = masks[n][...]

    along_z, along_x = (
        sum(jnp.where(step == n, moves[axis], 0) for n, moves in enumerate(STEPS)) for axis in range(2)
    )
    bin_of = (((t >> 2) + along_z) & 3) * 4 + ((t + along_x) & 3)
    block = rest[1, pl.ds(pl.multiple_of(bin_of * 8, 8), 8), :]
    chosen = (iota((8, LANES), 0) == 0) & (iota((8, LANES), 1) == 64 + core)
    tau = jnp.sum(jnp.where(chosen, block, 0.0), axis=(0, 1), keepdims=True)
    taus[0] = jnp.broadcast_to(tau, (8, LANES))

    @pl.when(step < NEAR)
    def _():
        decays, signal = forward_bin(tau, point, direction, forward_y, forward_z, kept.at[slot])
        backward_bin(tau, decays, signal, mask[...], kept.at[slot], point, backward_y, backward_z, order, total)

    @pl.when((step >= NEAR) & (step < BINS - 1))
    def _():
        forward_bin(tau, point, direction, forward_y, forward_z, kept.at[slot])
        store(step, slot).start()

    @pl.when(step == BINS - 1)
    def _():
        forward_bin(tau, point, direction, forward_y, forward_z, last)
        store(BINS - 2, BINS & 1).wait()


def second_kernel(
    mask, spectrum, last, point, taus, total_in, table_y, table_z, order,
    mine, theirs,
    total, sent, rest, kept, sems,
):
    step = pl.program_id(0)
    core = lax.axis_index("kz") & 1
    slot = step & 1

    def load(at):
        return pltpu.make_async_copy(spectrum.at[at - 1], kept.at[at & 1], sems.at[at & 1])

    @pl.when(step == 0)
    def _():
        total[...] = total_in[...]
        kept[0] = last[...]

    @pl.when(step < BINS - NEAR - 1)
    def _():
        load(step + 1).start()

    @pl.when(step > 0)
    def _():
        load(step).wait()

    tau = taus[0, 0:1, 0:1]
    decays, signal = model_terms(tau, point)
    backward_bin(tau, decays, signal, mask[0], kept.at[slot], point, table_y, table_z, order, total)

    @pl.when(step == BINS - NEAR - 1)
    def _():
        pack_sums(core, total, sent, rest, mine, theirs)


def sums_kernel(received, direction, residual, applied_out, out_sums, applied, sems):
    lane = iota((8, LANES), 1)
    sums = [jnp.zeros((8, LANES), f32) for _ in range(4)]
    copies = []
    for u in range(TILES):
        sides = []
        for g in range(4):
            upper, lower = (received[pl.ds(8 * m * TILES + u, 8, stride=TILES), :] for m in pairs_of(g))
            sides.append(upper + lower)
        if u < MAIN:
            maps = sides[0] + sides[1] + sides[2] + sides[3]
        for g in range(4):
            d, r, value = direction[g, u], residual[g, u], sides[g]
            if u < MAIN:
                of_maps = lane < 3 * ZB
                if g == 0:
                    value = jnp.where(of_maps, maps, value)
                else:
                    d, r, value = (jnp.where(of_maps, 0.0, a) for a in (d, r, value))
            elif u == TILES - 1:
                d, r, value = (jnp.where(lane < 64, a, 0.0) for a in (d, r, value))
            q = value + regular_weight * d
            applied[u, g] = q
            for i, (a, b) in enumerate(((r, r), (d, q), (r, q), (q, q))):
                sums[i] = sums[i] + a * b
        if u % 6 == 5:
            part = pl.ds(u - 5, 6)
            copies.append(pltpu.make_async_copy(applied.at[part], applied_out.at[part], sems.at[u // 6]))
            copies[-1].start()
    line = jnp.zeros((1, LANES), f32)
    for i in range(4):
        value = jnp.sum(sums[i], axis=(0, 1), keepdims=True)
        line = jnp.where(iota((1, LANES), 1) == i, value, line)
    out_sums[...] = jnp.broadcast_to(line, (LANES, LANES))
    for copy in copies:
        copy.wait()


def native_kernel(
    dense_in, dir_coils, res_coils, maps_out, fields, dense, maps, stacked, turned, sems
):
    copies = [
        pltpu.make_async_copy(source.at[p], fields.at[pl.ds(first + 8 * p, 8)], sems.at[2 * i + p])
        for i, (source, first) in enumerate(((dir_coils, 16), (res_coils, 32)))
        for p in range(2)
    ]
    copies.append(pltpu.make_async_copy(dense_in, dense, sems.at[5]))
    copies[-1].start()
    for copy in copies[:-1]:
        copy.start()
    copies.pop().wait()
    for g in range(4):
        for j in range(MAIN):
            turned[g, pl.ds(j, 8, stride=YB), :] = dense[j, g]
        stacked[g, :LANES] = jnp.swapaxes(turned[g], 0, 1)
        for v in range(2):
            stacked[g, LANES + 8 * v : LANES + 8 * v + 8] = inner_transpose(dense[MAIN + v, g])
        for i, name in enumerate(names_of(g)):
            if name < 3 and g:
                continue
            block = jnp.swapaxes(stacked[g, i * ZB : (i + 1) * ZB], 0, 1).reshape(XS, YB, ZB)
            if name < 3:
                maps[name] = block
            else:
                fields[name - 3] = block
    copies.append(pltpu.make_async_copy(maps, maps_out, sems.at[4]))
    copies[-1].start()
    for copy in copies:
        copy.wait()


def step_kernel(sums, fields, app_maps, dir_maps, res_maps, *refs):
    outs, (maps, made_maps, made_coils, sems) = refs[:4], refs[4:]
    copies = [
        pltpu.make_async_copy(source, maps.at[i], sems.at[i])
        for i, source in enumerate((app_maps, dir_maps, res_maps))
    ]
    for copy in copies:
        copy.start()
    line = jnp.sum(sums[...], axis=0, keepdims=True)
    lane = iota((1, LANES), 1)
    old, curve, cross, square = (
        jnp.sum(jnp.where(lane == i, line, 0.0), axis=1, keepdims=True) for i in range(4)
    )
    size = old / curve
    new = old - 2.0 * size * cross + size * size * square
    ratio = (new / old).reshape(1, 1, 1)
    size = size.reshape(1, 1, 1)
    stores = []
    for first in range(0, 16, 4):
        for coil in range(first, first + 4):
            fresh = fields[32 + coil] - size * fields[coil]
            made_coils[0, coil] = fresh
            made_coils[1, coil] = fresh + ratio * fields[16 + coil]
        part, rows = first // 8, pl.ds(first % 8, 4)
        for i in range(2):
            stores.append(
                pltpu.make_async_copy(
                    made_coils.at[i, pl.ds(first, 4)], outs[1 + 2 * i].at[part, rows], sems.at[3 + len(stores)]
                )
            )
            stores[-1].start()
    for copy in copies:
        copy.wait()
    for f in range(3):
        fresh = maps[2, f] - size * maps[0, f]
        made_maps[0, f] = fresh
        made_maps[1, f] = fresh + ratio * maps[1, f]
    for i in range(2):
        stores.append(pltpu.make_async_copy(made_maps.at[i], outs[2 * i], sems.at[3 + len(stores)]))
        stores[-1].start()
    for copy in stores:
        copy.wait()


def struct(*shape):
    return jax.ShapeDtypeStruct(shape, f32)


HBM = pl.BlockSpec(memory_space=pltpu.HBM)
VMEM = pl.BlockSpec(memory_space=pltpu.VMEM)
SCRATCH_STACKED = pltpu.VMEM((4, 144, LANES), f32)
SCRATCH_TURNED = pltpu.VMEM((4, LANES, LANES), f32)


def params():
    return pltpu.CompilerParams(vmem_limit_bytes=VMEM_LIMIT)


def cost(micros):
    return pl.CostEstimate(flops=int(micros * 4e8), bytes_accessed=int(micros * 2e6), transcendentals=0)


def constant_block(shape):
    return pl.BlockSpec(shape, lambda s: (0,) * len(shape))


def stepping_block(shape):
    return pl.BlockSpec((1,) + shape, lambda s: (s,) + (0,) * len(shape))


def in_hbm(*values):
    return tuple(pltpu.with_memory_space_constraint(value, pltpu.HBM) for value in values)


def in_vmem(*values):
    return tuple(pltpu.with_memory_space_constraint(value, pltpu.VMEM) for value in values)


def far(*shape):
    return pltpu.HBM(shape, f32)


def near(*shape):
    return pltpu.VMEM(shape, f32)


def core_swap(values):
    return lax.ppermute(values, "kz", [(i, i ^ 1) for i in range(8)])


def by_parity(values):
    groups = [[i for i in range(128) if i & 1 == c] for c in range(2)]
    messages = values.reshape(64, 1, values.shape[0] // 64 * LANES)
    return lax.all_to_all(messages, AXES, 0, 0, axis_index_groups=groups).reshape(values.shape)


def shards(
    point_maps,
    point_coils,
    direction_maps,
    direction_coils,
    residual_maps,
    residual_coils,
    inversion_times,
    sampling_mask,
):
    forward_y, forward_z, backward_y, backward_z, order = (jnp.asarray(table) for table in make_tables())
    dir_maps, dir_coils = jnp.swapaxes(direction_maps, 2, 3), jnp.swapaxes(direction_coils, 3, 4)
    res_maps, res_coils = jnp.swapaxes(residual_maps, 2, 3), jnp.swapaxes(residual_coils, 3, 4)
    pnt_maps = jnp.swapaxes(point_maps, 1, 2)
    pnt_coils = jnp.swapaxes(point_coils, 2, 3).reshape(2, 4, 2, ZB, XS, NY)

    send, dir_dense = pl.pallas_call(
        pack_kernel,
        out_shape=(
            far(64 * WHOLE, LANES),
            near(4, TILES, 8, LANES),
        ),
        in_specs=[HBM] * 5,
        out_specs=(HBM, VMEM),
        scratch_shapes=[
            pltpu.VMEM((64 * WHOLE, LANES), f32),
            pltpu.VMEM(dir_maps.shape, f32),
            pltpu.VMEM(dir_coils.shape, f32),
            pltpu.VMEM((ITEMS, 8, NY), f32),
            pltpu.VMEM((ITEMS, 4, 8, NY), f32),
            pltpu.SMEM((2,), f32),
            SCRATCH_STACKED,
            SCRATCH_TURNED,
            pltpu.SemaphoreType.DMA((37,)),
        ],
        compiler_params=params(),
        cost_estimate=cost(4),
        name="pack",
    )(*in_hbm(inversion_times, dir_maps, dir_coils, pnt_maps, pnt_coils))

    def densify(maps, coils):
        return pl.pallas_call(
            dense_kernel,
            out_shape=near(4, TILES, 8, LANES),
            in_specs=[HBM] * 2,
            out_specs=VMEM,
            scratch_shapes=[
                pltpu.VMEM(maps.shape, f32),
                pltpu.VMEM(coils.shape, f32),
                SCRATCH_STACKED,
                SCRATCH_TURNED,
                pltpu.SemaphoreType.DMA((2,)),
            ],
            compiler_params=params(),
            cost_estimate=cost(3),
            name="dense",
        )(*in_hbm(maps, coils))

    own_mask = lax.dynamic_index_in_dim(sampling_mask, lax.axis_index("kz") & 1, 0, keepdims=False)

    def from_ti(values, move):
        pairs = [((((i >> 2) + move[0]) & 3) * 4 + ((i + move[1]) & 3), i) for i in range(16)]
        return lax.ppermute(values, "ti", pairs)

    masks = [own_mask] + [from_ti(own_mask, move) for move in STEPS[1:NEAR]]
    send, *masks = lax.optimization_barrier((send, *masks))
    own = by_parity(send)
    res_dense = densify(*lax.optimization_barrier((res_maps, res_coils, dir_dense))[:2])
    stack = jnp.stack(masks[1:4])
    own, res_dense, stack = lax.optimization_barrier((own, res_dense, stack))
    other = core_swap(own)
    far_masks = from_ti(stack, STEPS[3])
    planes = (2, FEATURES * NZ, LANES)
    tables = (forward_y, forward_z, backward_y, backward_z, order)
    sums_shape = struct(64 * TILES, LANES)
    sent_scratch = pltpu.VMEM((2, 64 * TILES, LANES), f32)
    spectrum, last, point, taus, total, *near_tables = pl.pallas_call(
        first_kernel,
        grid=(BINS,),
        out_shape=(
            far(BINS - NEAR - 1, 2, 2, NZ, NY),
            near(2, 2, NZ, NY),
            near(*planes),
            near(BINS, 8, LANES),
            near(*planes),
            *[pltpu.VMEM(table.shape, bf16) for table in tables[2:]],
        ),
        in_specs=[constant_block(own.shape)] * 2
        + [constant_block((NZ, NY))] * NEAR
        + [HBM] * 5,
        out_specs=(
            HBM,
            constant_block((2, 2, NZ, NY)),
            constant_block(planes),
            stepping_block((8, LANES)),
            constant_block(planes),
            *[constant_block(table.shape) for table in tables[2:]],
        ),
        scratch_shapes=[
            pltpu.VMEM(planes, f32),
            pltpu.VMEM((2, LANES, LANES), f32),
            pltpu.VMEM(forward_y.shape, bf16),
            pltpu.VMEM(forward_z.shape, bf16),
            pltpu.VMEM((2, 2, 2, NZ, NY), f32),
            pltpu.VMEM((NZ, NY), jnp.int32),
            pltpu.SemaphoreType.DMA((7,)),
        ],
        compiler_params=params(),
        cost_estimate=cost(15),
        name="first",
    )(own, other, *masks, *in_hbm(*tables))

    def bin_block(shape, first):
        return pl.BlockSpec((1,) + shape, lambda s: (jnp.where(s == 0, BINS - 1, s + NEAR - 1) - first, 0, 0))

    mine, theirs = pl.pallas_call(
        second_kernel,
        grid=(BINS - NEAR,),
        out_shape=(sums_shape, sums_shape),
        in_specs=[
            bin_block((NZ, NY), NEAR),
            HBM,
            constant_block((2, 2, NZ, NY)),
            constant_block(planes),
            bin_block((8, LANES), 0),
            constant_block(planes),
        ]
        + [constant_block(table.shape) for table in tables[2:]],
        out_specs=(constant_block((64 * TILES, LANES)),) * 2,
        scratch_shapes=[
            pltpu.VMEM(planes, f32),
            sent_scratch,
            pltpu.VMEM((2, LANES, LANES), f32),
            pltpu.VMEM((2, 2, 2, NZ, NY), f32),
            pltpu.SemaphoreType.DMA((2,)),
        ],
        compiler_params=params(),
        cost_estimate=cost(8),
        name="second",
    )(far_masks, *in_hbm(spectrum), *in_vmem(last, point, taus, total, *near_tables))

    received = by_parity(mine + core_swap(theirs))
    app_dense, sums = pl.pallas_call(
        sums_kernel,
        out_shape=(far(TILES, 4, 8, LANES), near(128, LANES)),
        in_specs=[VMEM] * 3,
        out_specs=(HBM, VMEM),
        scratch_shapes=[pltpu.VMEM((TILES, 4, 8, LANES), f32), pltpu.SemaphoreType.DMA((3,))],
        compiler_params=params(),
        cost_estimate=cost(1),
        name="sums",
    )(received, *in_vmem(dir_dense, res_dense))
    all_sums = lax.all_to_all(sums.reshape(128, 1, LANES), AXES, 0, 0).reshape(128, LANES)

    maps_shape, coils_shape = far(*dir_maps.shape), far(*dir_coils.shape)
    app_maps, fields = pl.pallas_call(
        native_kernel,
        out_shape=(far(*dir_maps.shape), near(48, XS, YB, ZB)),
        in_specs=[HBM] * 3,
        out_specs=(HBM, VMEM),
        scratch_shapes=[
            pltpu.VMEM((TILES, 4, 8, LANES), f32),
            pltpu.VMEM(dir_maps.shape, f32),
            SCRATCH_STACKED,
            SCRATCH_TURNED,
            pltpu.SemaphoreType.DMA((6,)),
        ],
        compiler_params=params(),
        cost_estimate=cost(3),
        name="native",
    )(*in_hbm(app_dense, dir_coils, res_coils))

    outs = pl.pallas_call(
        step_kernel,
        out_shape=(maps_shape, coils_shape, maps_shape, coils_shape),
        in_specs=[VMEM] * 2 + [HBM] * 3,
        out_specs=(HBM,) * 4,
        scratch_shapes=[
            pltpu.VMEM((3,) + dir_maps.shape, f32),
            pltpu.VMEM((2,) + dir_maps.shape, f32),
            pltpu.VMEM((2, 16, XS, YB, ZB), f32),
            pltpu.SemaphoreType.DMA((13,)),
        ],
        compiler_params=params(),
        cost_estimate=cost(2),
        name="step",
    )(all_sums, *in_vmem(fields), *in_hbm(app_maps, dir_maps, res_maps))
    return tuple(jnp.swapaxes(out, -2, -1) for out in outs)


def solution(mesh):
    in_specs = (
        P(None, None, "kz", None),
        P(None, None, None, "kz", None),
        P(None, None, "kz", "ti"),
        P(None, None, None, "kz", "ti"),
        P(None, None, "kz", "ti"),
        P(None, None, None, "kz", "ti"),
        P("ti"),
        P("ti", None, None),
    )
    out_specs = (
        P(None, None, "kz", "ti"),
        P(None, None, None, "kz", "ti"),
        P(None, None, "kz", "ti"),
        P(None, None, None, "kz", "ti"),
    )
    return jax.shard_map(shards, mesh=mesh, in_specs=in_specs, out_specs=out_specs, check_vma=False)
```

```python
import math

import jax
import jax.numpy as jnp
import numpy as np
from jax import lax
from jax.experimental import pallas as pl
from jax.experimental.pallas import tpu as pltpu
from jax.sharding import PartitionSpec as P

regular_weight = 2.0
AXES = ("ti", "kz")
NZ, NY, ZB, YB, XS = 160, 256, 20, 16, 8
HALF_Z, HALF_Y = NZ // 2, NY // 2
LANES = 128
FEATURES = 7
PAIRS = FEATURES * ZB
MAIN = 16
TILES = 18
MSG = TILES * LANES
ITEMS = 9
BINS = 8
NEAR = 5
STEPS = ((0, 0), (0, 1), (0, 3), (1, 0), (3, 0), (1, 1), (1, 3), (2, 0))
WHOLE = 2 * TILES
VMEM_LIMIT = 32 * 1024 * 1024
f32 = jnp.float32
bf16 = jnp.bfloat16


def split_pair(table):
    high = table.astype(np.float32).astype(jnp.bfloat16)
    low = (table - high.astype(np.float64)).astype(np.float32).astype(jnp.bfloat16)
    return high, low


def real_form(matrix):
    return np.block([[matrix.real, matrix.imag], [-matrix.imag, matrix.real]])


def right_table(table):
    high, low = split_pair(table)
    return np.concatenate([high, high, low], axis=0)


def left_table(table):
    high, low = split_pair(table)
    pad = np.zeros((table.shape[0], 32), dtype=jnp.bfloat16)
    return np.concatenate([high, high, low, pad], axis=1)


def z_of_rows():
    rows = np.arange(HALF_Z)
    return (rows % 8) * ZB + 2 * (rows // 8)


def make_tables():
    n, m = np.arange(HALF_Y)[:, None], np.arange(HALF_Y)[None, :]
    y_even = real_form(np.exp(-2j * np.pi * (n * (2 * m) % NY) / NY) / math.sqrt(NY))
    y_odd = real_form(np.exp(-2j * np.pi * (n * (2 * m + 1) % NY) / NY) / math.sqrt(NY))
    spots, freq = z_of_rows()[None, :], np.arange(HALF_Z)[:, None]
    z_even = real_form((np.exp(-2j * np.pi * (freq * spots % NZ) / NZ) / math.sqrt(NZ)).T).T
    z_odd = real_form((np.exp(-2j * np.pi * (freq * (spots + 1) % NZ) / NZ) / math.sqrt(NZ)).T).T
    forward_y = np.stack([right_table(y_even), right_table(y_odd)])
    backward_y = np.stack([right_table(y_even.T), right_table(y_odd.T)])
    forward_z = np.stack([left_table(z_even), left_table(z_odd)])
    backward_z = np.stack([left_table(z_even.T), left_table(z_odd.T)])
    order = np.zeros((NY, NY), dtype=jnp.bfloat16)
    for lane in range(NY):
        order[2 * (lane % HALF_Y) + lane // HALF_Y, lane] = 1
    return forward_y, forward_z, backward_y, backward_z, order


def iota(shape, axis):
    return lax.broadcasted_iota(jnp.int32, shape, axis)


def block_transpose(tiles):
    group = iota((8, LANES), 1) >> 4
    tiles = list(tiles)
    for bit in (1, 2, 4):
        unset = (group & bit) == 0
        for i in range(8):
            if i & bit:
                continue
            a, c = tiles[i], tiles[i | bit]
            tiles[i] = jnp.where(unset, a, pltpu.roll(c, 16 * bit, 1))
            tiles[i | bit] = jnp.where(unset, pltpu.roll(a, LANES - 16 * bit, 1), c)
    return tiles


def inner_transpose(tile):
    group, row = iota((8, LANES), 1) >> 4, iota((8, LANES), 0)
    for bit in (1, 2, 4):
        g, s = (group & bit) != 0, (row & bit) != 0
        down = pltpu.roll(pltpu.roll(tile, bit, 0), LANES - 16 * bit, 1)
        up = pltpu.roll(pltpu.roll(tile, 8 - bit, 0), 16 * bit, 1)
        tile = jnp.where(g == s, tile, jnp.where(s, down, up))
    return tile


def halves(values):
    high = values.astype(bf16)
    return high, (values - high.astype(f32)).astype(bf16)


def times_right(values, table):
    high, low = halves(values)
    return jnp.dot(jnp.concatenate([high, low, high], axis=1), table, preferred_element_type=f32)


def times_left(table, values):
    high, low = halves(values)
    pad = jnp.zeros((32, values.shape[1]), bf16)
    return jnp.dot(table, jnp.concatenate([high, low, high, pad], axis=0), preferred_element_type=f32)


def split_rows(values):
    grouped = values.reshape(ZB // 2, 2, 8, values.shape[1])
    return [grouped[:, parity].reshape(HALF_Z, values.shape[1]) for parity in range(2)]


def join_rows(even, odd):
    parts = [side.reshape(ZB // 2, 1, 8, side.shape[1]) for side in (even, odd)]
    return jnp.concatenate(parts, axis=1).reshape(NZ, even.shape[1])


def plane(ref, f):
    return jnp.concatenate([ref[0, f * NZ : (f + 1) * NZ], ref[1, f * NZ : (f + 1) * NZ]], axis=1)


def pairs_of(g):
    return (g, 4 + (g ^ 1))


def names_of(g):
    return [0, 1, 2] + [3 + 8 * p + 2 * g + e for p in range(2) for e in range(2)]


def dense_tiles(maps, coils, stacked, turned, emit, arrive=None):
    blank = jnp.zeros((8, LANES), f32)
    for g in range(4):
        if arrive is not None:
            arrive(g)
        stacked[g, 136:144] = blank
        for i, name in enumerate(names_of(g)):
            if name < 3:
                if g == 0:
                    rows = jnp.swapaxes(maps[name].reshape(8 * YB, ZB), 0, 1)
                    for other in range(4):
                        stacked[other, i * ZB : (i + 1) * ZB] = rows
            else:
                block = coils[(name - 3) // 8, (name - 3) % 8]
                stacked[g, i * ZB : (i + 1) * ZB] = jnp.swapaxes(block.reshape(8 * YB, ZB), 0, 1)
        turned[g] = jnp.swapaxes(stacked[g, :LANES], 0, 1)
        for j in range(MAIN):
            emit(g, j, turned[g, pl.ds(j, 8, stride=YB), :])
        for v in range(2):
            emit(g, MAIN + v, inner_transpose(stacked[g, LANES + 8 * v : LANES + 8 * v + 8]))


def pack_kernel(
    times, maps_in, coils_in, point_maps, point_coils,
    send_out, dense,
    send, maps, coils, of_maps, of_coils, stamp, stacked, turned, sems,
):
    t = lax.axis_index("ti")
    maps_copies = [
        pltpu.make_async_copy(maps_in, maps, sems.at[9]),
        pltpu.make_async_copy(times, stamp, sems.at[10]),
    ]
    coils_copies = [
        pltpu.make_async_copy(
            coils_in.at[p, pl.ds(2 * g, 2)], coils.at[p, pl.ds(2 * g, 2)], sems.at[11 + 2 * g + p]
        )
        for g in range(4)
        for p in range(2)
    ]
    point_copies = []
    items = []
    for i in range(ITEMS):
        item = jnp.minimum((t >> 1) * 18 + 2 * i + (t & 1), PAIRS - 1)
        f = item // ZB
        z = item - f * ZB
        q = jnp.maximum(f - 3, 0)
        items.append(f)
        point_copies.append(
            pltpu.make_async_copy(point_maps.at[jnp.minimum(f, 2), z], of_maps.at[i], sems.at[19 + i])
        )
        point_copies.append(
            pltpu.make_async_copy(point_coils.at[q >> 1, :, q & 1, z], of_coils.at[i], sems.at[28 + i])
        )
    for copy in point_copies + maps_copies + coils_copies:
        copy.start()
    for copy in point_copies:
        copy.wait()
    for copy in maps_copies:
        copy.wait()
    lane = iota((8, LANES), 1)
    spare = jnp.where(lane == 64, stamp[0], jnp.where(lane == 65, stamp[1], 0.0))

    stores = []

    def emit(g, u, tile):
        dense[g, u] = tile
        if u == TILES - 1:
            tile = jnp.where(lane < 64, tile, spare)
        for m in pairs_of(g):
            send[pl.ds(8 * m * WHOLE + u, 8, stride=WHOLE), :] = tile
        if u == TILES - 1:
            for m in pairs_of(g):
                rows = pl.ds(8 * m * WHOLE, 8 * WHOLE)
                stores.append(pltpu.make_async_copy(send.at[rows], send_out.at[rows], sems.at[len(stores)]))
                stores[-1].start()

    def arrive(g):
        for i in range(ITEMS):
            tile = jnp.where(items[i] < 3, of_maps[i], of_coils[i, g])
            for m in pairs_of(g):
                for half in range(2):
                    first = 8 * m * WHOLE + TILES + 2 * i + half
                    send[pl.ds(first, 8, stride=WHOLE), :] = tile[:, half * LANES : (half + 1) * LANES]
        for copy in coils_copies[2 * g : 2 * g + 2]:
            copy.wait()

    dense_tiles(maps, coils, stacked, turned, emit, arrive)
    for copy in stores:
        copy.wait()


def dense_kernel(maps_in, coils_in, dense, maps, coils, stacked, turned, sems):
    copies = [
        pltpu.make_async_copy(maps_in, maps, sems.at[0]),
        pltpu.make_async_copy(coils_in, coils, sems.at[1]),
    ]
    for copy in copies:
        copy.start()
    for copy in copies:
        copy.wait()

    def emit(g, u, tile):
        dense[g, u] = tile

    dense_tiles(maps, coils, stacked, turned, emit)


def unpack(part, c, point, direction, rest):
    for y in range(4):
        for half in range(2):
            firsts = [WHOLE * (4 * (8 * half + i) + y) for i in range(8)]
            rows = [part[first : first + MAIN, :] for first in firsts]
            pairs = jnp.swapaxes(jnp.concatenate(rows, axis=0), 0, 1)
            direction[half, pl.ds(2 * y + c, LANES, stride=8), :] = pairs
    for v in range(2):
        rest[v, pl.ds(c, 64, stride=2), :] = part[pl.ds(MAIN + v, 64, stride=WHOLE), :]
    for i in range(ITEMS):
        for half in range(2):
            for m in range(8):
                n = 18 * m + 2 * i
                if n < PAIRS:
                    first = 8 * m * WHOLE + TILES + 2 * i + half
                    point[half, pl.ds(8 * n + c, 8, stride=2), :] = part[pl.ds(first, 8, stride=WHOLE), :]


def unpack_rest(direction, rest):
    for v in range(2):
        for half in range(2):
            tiles = [rest[v, 8 * (8 * half + i) : 8 * (8 * half + i) + 8] for i in range(8)]
            for member, tile in enumerate(block_transpose(tiles)):
                n = LANES + 8 * v + member
                if n < PAIRS:
                    direction[half, 8 * n : 8 * n + 8] = tile


def model_terms(tau, point):
    decays = jnp.exp(-tau * plane(point, 2))
    return decays, plane(point, 0) - plane(point, 1) * decays


def forward_bin(tau, point, direction, table_y, table_z, spectrum):
    amplitude = plane(point, 1)
    decays, signal = model_terms(tau, point)
    change = plane(direction, 0) - plane(direction, 1) * decays + amplitude * tau * decays * plane(direction, 2)
    evens, odds = [], []
    for c in range(2):
        re = plane(point, 3 + c) * change + plane(direction, 3 + c) * signal
        im = plane(point, 5 + c) * change + plane(direction, 5 + c) * signal
        re_low, re_high, im_low, im_high = re[:, :HALF_Y], re[:, HALF_Y:], im[:, :HALF_Y], im[:, HALF_Y:]
        evens.append(jnp.concatenate([re_low + re_high, im_low + im_high], axis=1))
        odds.append(jnp.concatenate([re_low - re_high, im_low - im_high], axis=1))
    along_even = times_right(jnp.concatenate(evens, axis=0), table_y[0])
    along_odd = times_right(jnp.concatenate(odds, axis=0), table_y[1])
    for c in range(2):
        rows = slice(c * NZ, (c + 1) * NZ)
        re = jnp.concatenate([along_even[rows, :HALF_Y], along_odd[rows, :HALF_Y]], axis=1)
        im = jnp.concatenate([along_even[rows, HALF_Y:], along_odd[rows, HALF_Y:]], axis=1)
        parts = [
            times_left(table_z[parity], jnp.concatenate(pair, axis=0))
            for parity, pair in enumerate(zip(split_rows(re), split_rows(im)))
        ]
        for part in range(2):
            a, b = (side[part * HALF_Z : (part + 1) * HALF_Z] for side in parts)
            spectrum[c, part, :HALF_Z] = a + b
            spectrum[c, part, HALF_Z:] = a - b
    return decays, signal


def backward_bin(tau, decays, signal, mask, spectrum, point, table_y, table_z, order, total):
    weights = jnp.dot(mask.astype(f32).astype(bf16), order[...], preferred_element_type=f32)
    evens, odds = [], []
    for c in range(2):
        plus, minus = [], []
        for part in range(2):
            values = spectrum[c, part] * weights
            plus.append(values[:HALF_Z] + values[HALF_Z:])
            minus.append(values[:HALF_Z] - values[HALF_Z:])
        for parity, side in enumerate((plus, minus)):
            out = times_left(table_z[parity], jnp.concatenate(side, axis=0))
            re, im = out[:HALF_Z], out[HALF_Z:]
            evens.append(jnp.concatenate([re[:, :HALF_Y], im[:, :HALF_Y]], axis=1))
            odds.append(jnp.concatenate([re[:, HALF_Y:], im[:, HALF_Y:]], axis=1))
    from_even = times_right(jnp.concatenate(evens, axis=0), table_y[0])
    from_odd = times_right(jnp.concatenate(odds, axis=0), table_y[1])
    low, high = from_even + from_odd, from_even - from_odd

    def add(f, values):
        for half in range(2):
            total[half, f * NZ : (f + 1) * NZ] += values[:, half * LANES : (half + 1) * LANES]

    projected = None
    for c in range(2):
        sides = []
        for lanes in (slice(0, HALF_Y), slice(HALF_Y, NY)):
            value = jnp.concatenate([low[:, lanes], high[:, lanes]], axis=1)
            first = 2 * c * HALF_Z
            sides.append(join_rows(value[first : first + HALF_Z], value[first + HALF_Z : first + NZ]))
        re, im = sides
        term = plane(point, 3 + c) * re + plane(point, 5 + c) * im
        projected = term if projected is None else projected + term
        add(3 + c, signal * re)
        add(5 + c, signal * im)
    add(0, projected)
    faded = decays * projected
    add(1, -faded)
    add(2, plane(point, 1) * (tau * faded))


def pack_sums(core, total, sent, rest, mine, theirs):
    for k in range(8):
        place = (k & 1) ^ core
        for half in range(2):
            pairs = jnp.swapaxes(total[half, pl.ds(k, LANES, stride=8), :], 0, 1)
            for i in range(8):
                first = TILES * (4 * (8 * half + i) + (k >> 1))
                sent[place, first : first + MAIN, :] = pairs[YB * i : YB * (i + 1)]
    for v in range(2):
        for half in range(2):
            tiles = []
            for member in range(8):
                n = min(LANES + 8 * v + member, PAIRS - 1)
                tiles.append(total[half, 8 * n : 8 * n + 8])
            for i, tile in enumerate(block_transpose(tiles)):
                rest[v, 8 * (8 * half + i) : 8 * (8 * half + i) + 8] = tile
        for c in range(2):
            rows = pl.ds(MAIN + v, 64, stride=TILES)
            sent[c ^ core, rows, :] = rest[v, pl.ds(c, 64, stride=2), :]
    mine[...] = sent[0]
    theirs[...] = sent[1]


def first_kernel(*refs):
    own, other, *masks = refs[: 2 + NEAR]
    tables_in, refs = refs[2 + NEAR : 7 + NEAR], refs[7 + NEAR :]
    spectra, point, taus, total, backward_y, backward_z, order = refs[:7]
    direction, rest, forward_y, forward_z, kept, sems = refs[7:]
    step = pl.program_id(0)
    t, core = lax.axis_index("ti"), lax.axis_index("kz") & 1

    @pl.when(step == 0)
    def _():
        tables = (forward_y, forward_z, backward_y, backward_z, order)
        copies = [pltpu.make_async_copy(a, b, sems.at[i]) for i, (a, b) in enumerate(zip(tables_in, tables))]
        for copy in copies:
            copy.start()
        total[...] = jnp.zeros_like(total)
        unpack(own, core, point, direction, rest)
        unpack(other, 1 - core, point, direction, rest)
        unpack_rest(direction, rest)
        for copy in copies:
            copy.wait()

    def bin_time(n):
        along_z, along_x = STEPS[n]
        bin_of = (((t >> 2) + along_z) & 3) * 4 + ((t + along_x) & 3)
        block = rest[1, pl.ds(pl.multiple_of(bin_of * 8, 8), 8), :]
        chosen = (iota((8, LANES), 0) == 0) & (iota((8, LANES), 1) == 64 + core)
        tau = jnp.sum(jnp.where(chosen, block, 0.0), axis=(0, 1), keepdims=True)
        taus[n] = jnp.broadcast_to(tau, (8, LANES))
        return tau

    for first in range(0, BINS, 2):

        @pl.when(step == first // 2)
        def _():
            done = []
            for n in (first, first + 1):
                tau = bin_time(n)
                spectrum = kept.at[n & 1] if n < NEAR else spectra.at[n - NEAR]
                done.append((n, tau, spectrum, forward_bin(tau, point, direction, forward_y, forward_z, spectrum)))
            for n, tau, spectrum, terms in done:
                if n < NEAR:
                    backward_bin(tau, *terms, masks[n][...], spectrum, point, backward_y, backward_z, order, total)


def second_kernel(mask, spectra, point, taus, total_in, table_y, table_z, order, mine, theirs, total, sent, rest):
    core = lax.axis_index("kz") & 1
    total[...] = total_in[...]
    for n in range(NEAR, BINS):
        tau = taus[n, 0:1, 0:1]
        terms = model_terms(tau, point)
        backward_bin(tau, *terms, mask[n - NEAR], spectra.at[n - NEAR], point, table_y, table_z, order, total)
    pack_sums(core, total, sent, rest, mine, theirs)


def sums_kernel(received, direction, residual, applied_out, out_sums, applied, sems):
    lane = iota((8, LANES), 1)
    sums = [jnp.zeros((8, LANES), f32) for _ in range(4)]
    copies = []
    for u in range(TILES):
        sides = []
        for g in range(4):
            upper, lower = (received[pl.ds(8 * m * TILES + u, 8, stride=TILES), :] for m in pairs_of(g))
            sides.append(upper + lower)
        if u < MAIN:
            maps = sides[0] + sides[1] + sides[2] + sides[3]
        for g in range(4):
            d, r, value = direction[g, u], residual[g, u], sides[g]
            if u < MAIN:
                of_maps = lane < 3 * ZB
                if g == 0:
                    value = jnp.where(of_maps, maps, value)
                else:
                    d, r, value = (jnp.where(of_maps, 0.0, a) for a in (d, r, value))
            elif u == TILES - 1:
                d, r, value = (jnp.where(lane < 64, a, 0.0) for a in (d, r, value))
            q = value + regular_weight * d
            applied[u, g] = q
            for i, (a, b) in enumerate(((r, r), (d, q), (r, q), (q, q))):
                sums[i] = sums[i] + a * b
        if u % 6 == 5:
            part = pl.ds(u - 5, 6)
            copies.append(pltpu.make_async_copy(applied.at[part], applied_out.at[part], sems.at[u // 6]))
            copies[-1].start()
    line = jnp.zeros((1, LANES), f32)
    for i in range(4):
        value = jnp.sum(sums[i], axis=(0, 1), keepdims=True)
        line = jnp.where(iota((1, LANES), 1) == i, value, line)
    out_sums[...] = jnp.broadcast_to(line, (LANES, LANES))
    for copy in copies:
        copy.wait()


def native_kernel(
    dense_in, dir_coils, res_coils, maps_out, fields, dense, maps, stacked, turned, sems
):
    copies = [
        pltpu.make_async_copy(source.at[p], fields.at[pl.ds(first + 8 * p, 8)], sems.at[2 * i + p])
        for i, (source, first) in enumerate(((dir_coils, 16), (res_coils, 32)))
        for p in range(2)
    ]
    copies.append(pltpu.make_async_copy(dense_in, dense, sems.at[5]))
    copies[-1].start()
    for copy in copies[:-1]:
        copy.start()
    copies.pop().wait()
    for g in range(4):
        for j in range(MAIN):
            turned[g, pl.ds(j, 8, stride=YB), :] = dense[j, g]
        stacked[g, :LANES] = jnp.swapaxes(turned[g], 0, 1)
        for v in range(2):
            stacked[g, LANES + 8 * v : LANES + 8 * v + 8] = inner_transpose(dense[MAIN + v, g])
        for i, name in enumerate(names_of(g)):
            if name < 3 and g:
                continue
            block = jnp.swapaxes(stacked[g, i * ZB : (i + 1) * ZB], 0, 1).reshape(XS, YB, ZB)
            if name < 3:
                maps[name] = block
            else:
                fields[name - 3] = block
    copies.append(pltpu.make_async_copy(maps, maps_out, sems.at[4]))
    copies[-1].start()
    for copy in copies:
        copy.wait()


def step_kernel(sums, fields, app_maps, dir_maps, res_maps, *refs):
    outs, (maps, made_maps, made_coils, sems) = refs[:4], refs[4:]
    copies = [
        pltpu.make_async_copy(source, maps.at[i], sems.at[i])
        for i, source in enumerate((app_maps, dir_maps, res_maps))
    ]
    for copy in copies:
        copy.start()
    line = jnp.sum(sums[...], axis=0, keepdims=True)
    lane = iota((1, LANES), 1)
    old, curve, cross, square = (
        jnp.sum(jnp.where(lane == i, line, 0.0), axis=1, keepdims=True) for i in range(4)
    )
    size = old / curve
    new = old - 2.0 * size * cross + size * size * square
    ratio = (new / old).reshape(1, 1, 1)
    size = size.reshape(1, 1, 1)
    stores = []
    for first in range(0, 16, 4):
        for coil in range(first, first + 4):
            fresh = fields[32 + coil] - size * fields[coil]
            made_coils[0, coil] = fresh
            made_coils[1, coil] = fresh + ratio * fields[16 + coil]
        part, rows = first // 8, pl.ds(first % 8, 4)
        for i in range(2):
            stores.append(
                pltpu.make_async_copy(
                    made_coils.at[i, pl.ds(first, 4)], outs[1 + 2 * i].at[part, rows], sems.at[3 + len(stores)]
                )
            )
            stores[-1].start()
    for copy in copies:
        copy.wait()
    for f in range(3):
        fresh = maps[2, f] - size * maps[0, f]
        made_maps[0, f] = fresh
        made_maps[1, f] = fresh + ratio * maps[1, f]
    for i in range(2):
        stores.append(pltpu.make_async_copy(made_maps.at[i], outs[2 * i], sems.at[3 + len(stores)]))
        stores[-1].start()
    for copy in stores:
        copy.wait()


def struct(*shape):
    return jax.ShapeDtypeStruct(shape, f32)


HBM = pl.BlockSpec(memory_space=pltpu.HBM)
VMEM = pl.BlockSpec(memory_space=pltpu.VMEM)
SCRATCH_STACKED = pltpu.VMEM((4, 144, LANES), f32)
SCRATCH_TURNED = pltpu.VMEM((4, LANES, LANES), f32)


def params():
    return pltpu.CompilerParams(vmem_limit_bytes=VMEM_LIMIT)


def cost(micros):
    return pl.CostEstimate(flops=int(micros * 4e8), bytes_accessed=int(micros * 2e6), transcendentals=0)


def constant_block(shape):
    return pl.BlockSpec(shape, lambda s: (0,) * len(shape))


def in_hbm(*values):
    return tuple(pltpu.with_memory_space_constraint(value, pltpu.HBM) for value in values)


def in_vmem(*values):
    return tuple(pltpu.with_memory_space_constraint(value, pltpu.VMEM) for value in values)


def far(*shape):
    return pltpu.HBM(shape, f32)


def near(*shape):
    return pltpu.VMEM(shape, f32)


def core_swap(values):
    return lax.ppermute(values, "kz", [(i, i ^ 1) for i in range(8)])


def by_parity(values):
    groups = [[i for i in range(128) if i & 1 == c] for c in range(2)]
    messages = values.reshape(64, 1, values.shape[0] // 64 * LANES)
    return lax.all_to_all(messages, AXES, 0, 0, axis_index_groups=groups).reshape(values.shape)


def shards(
    point_maps,
    point_coils,
    direction_maps,
    direction_coils,
    residual_maps,
    residual_coils,
    inversion_times,
    sampling_mask,
):
    forward_y, forward_z, backward_y, backward_z, order = (jnp.asarray(table) for table in make_tables())
    dir_maps, dir_coils = jnp.swapaxes(direction_maps, 2, 3), jnp.swapaxes(direction_coils, 3, 4)
    res_maps, res_coils = jnp.swapaxes(residual_maps, 2, 3), jnp.swapaxes(residual_coils, 3, 4)
    pnt_maps = jnp.swapaxes(point_maps, 1, 2)
    pnt_coils = jnp.swapaxes(point_coils, 2, 3).reshape(2, 4, 2, ZB, XS, NY)

    send, dir_dense = pl.pallas_call(
        pack_kernel,
        out_shape=(
            far(64 * WHOLE, LANES),
            near(4, TILES, 8, LANES),
        ),
        in_specs=[HBM] * 5,
        out_specs=(HBM, VMEM),
        scratch_shapes=[
            pltpu.VMEM((64 * WHOLE, LANES), f32),
            pltpu.VMEM(dir_maps.shape, f32),
            pltpu.VMEM(dir_coils.shape, f32),
            pltpu.VMEM((ITEMS, 8, NY), f32),
            pltpu.VMEM((ITEMS, 4, 8, NY), f32),
            pltpu.SMEM((2,), f32),
            SCRATCH_STACKED,
            SCRATCH_TURNED,
            pltpu.SemaphoreType.DMA((37,)),
        ],
        compiler_params=params(),
        cost_estimate=cost(4),
        name="pack",
    )(*in_hbm(inversion_times, dir_maps, dir_coils, pnt_maps, pnt_coils))

    def densify(maps, coils):
        return pl.pallas_call(
            dense_kernel,
            out_shape=near(4, TILES, 8, LANES),
            in_specs=[HBM] * 2,
            out_specs=VMEM,
            scratch_shapes=[
                pltpu.VMEM(maps.shape, f32),
                pltpu.VMEM(coils.shape, f32),
                SCRATCH_STACKED,
                SCRATCH_TURNED,
                pltpu.SemaphoreType.DMA((2,)),
            ],
            compiler_params=params(),
            cost_estimate=cost(3),
            name="dense",
        )(*in_hbm(maps, coils))

    own_mask = lax.dynamic_index_in_dim(sampling_mask, lax.axis_index("kz") & 1, 0, keepdims=False)

    def from_ti(values, move):
        pairs = [((((i >> 2) + move[0]) & 3) * 4 + ((i + move[1]) & 3), i) for i in range(16)]
        return lax.ppermute(values, "ti", pairs)

    masks = [own_mask] + [from_ti(own_mask, move) for move in STEPS[1:NEAR]]
    send, *masks = lax.optimization_barrier((send, *masks))
    own = by_parity(send)
    res_dense = densify(*lax.optimization_barrier((res_maps, res_coils, dir_dense))[:2])
    stack = jnp.stack(masks[1:4])
    own, res_dense, stack = lax.optimization_barrier((own, res_dense, stack))
    other = core_swap(own)
    far_masks = from_ti(stack, STEPS[3])
    planes = (2, FEATURES * NZ, LANES)
    tables = (forward_y, forward_z, backward_y, backward_z, order)
    sums_shape = struct(64 * TILES, LANES)
    sent_scratch = pltpu.VMEM((2, 64 * TILES, LANES), f32)
    spectra, point, taus, total, *near_tables = pl.pallas_call(
        first_kernel,
        grid=(BINS // 2,),
        out_shape=(
            near(BINS - NEAR, 2, 2, NZ, NY),
            near(*planes),
            near(BINS, 8, LANES),
            near(*planes),
            *[pltpu.VMEM(table.shape, bf16) for table in tables[2:]],
        ),
        in_specs=[constant_block(own.shape)] * 2
        + [constant_block((NZ, NY))] * NEAR
        + [HBM] * 5,
        out_specs=(
            constant_block((BINS - NEAR, 2, 2, NZ, NY)),
            constant_block(planes),
            constant_block((BINS, 8, LANES)),
            constant_block(planes),
            *[constant_block(table.shape) for table in tables[2:]],
        ),
        scratch_shapes=[
            pltpu.VMEM(planes, f32),
            pltpu.VMEM((2, LANES, LANES), f32),
            pltpu.VMEM(forward_y.shape, bf16),
            pltpu.VMEM(forward_z.shape, bf16),
            pltpu.VMEM((2, 2, 2, NZ, NY), f32),
            pltpu.SemaphoreType.DMA((5,)),
        ],
        compiler_params=params(),
        cost_estimate=cost(15),
        name="first",
    )(own, other, *masks, *in_hbm(*tables))

    mine, theirs = pl.pallas_call(
        second_kernel,
        out_shape=(sums_shape, sums_shape),
        in_specs=[VMEM] * 8,
        out_specs=(VMEM, VMEM),
        scratch_shapes=[
            pltpu.VMEM(planes, f32),
            sent_scratch,
            pltpu.VMEM((2, LANES, LANES), f32),
        ],
        compiler_params=params(),
        cost_estimate=cost(4),
        name="second",
    )(far_masks, *in_vmem(spectra, point, taus, total, *near_tables))

    received = by_parity(mine + core_swap(theirs))
    app_dense, sums = pl.pallas_call(
        sums_kernel,
        out_shape=(far(TILES, 4, 8, LANES), near(128, LANES)),
        in_specs=[VMEM] * 3,
        out_specs=(HBM, VMEM),
        scratch_shapes=[pltpu.VMEM((TILES, 4, 8, LANES), f32), pltpu.SemaphoreType.DMA((3,))],
        compiler_params=params(),
        cost_estimate=cost(1),
        name="sums",
    )(received, *in_vmem(dir_dense, res_dense))
    all_sums = lax.all_to_all(sums.reshape(128, 1, LANES), AXES, 0, 0).reshape(128, LANES)

    maps_shape, coils_shape = far(*dir_maps.shape), far(*dir_coils.shape)
    app_maps, fields = pl.pallas_call(
        native_kernel,
        out_shape=(far(*dir_maps.shape), near(48, XS, YB, ZB)),
        in_specs=[HBM] * 3,
        out_specs=(HBM, VMEM),
        scratch_shapes=[
            pltpu.VMEM((TILES, 4, 8, LANES), f32),
            pltpu.VMEM(dir_maps.shape, f32),
            SCRATCH_STACKED,
            SCRATCH_TURNED,
            pltpu.SemaphoreType.DMA((6,)),
        ],
        compiler_params=params(),
        cost_estimate=cost(3),
        name="native",
    )(*in_hbm(app_dense, dir_coils, res_coils))

    outs = pl.pallas_call(
        step_kernel,
        out_shape=(maps_shape, coils_shape, maps_shape, coils_shape),
        in_specs=[VMEM] * 2 + [HBM] * 3,
        out_specs=(HBM,) * 4,
        scratch_shapes=[
            pltpu.VMEM((3,) + dir_maps.shape, f32),
            pltpu.VMEM((2,) + dir_maps.shape, f32),
            pltpu.VMEM((2, 16, XS, YB, ZB), f32),
            pltpu.SemaphoreType.DMA((13,)),
        ],
        compiler_params=params(),
        cost_estimate=cost(2),
        name="step",
    )(all_sums, *in_vmem(fields), *in_hbm(app_maps, dir_maps, res_maps))
    return tuple(jnp.swapaxes(out, -2, -1) for out in outs)


def solution(mesh):
    in_specs = (
        P(None, None, "kz", None),
        P(None, None, None, "kz", None),
        P(None, None, "kz", "ti"),
        P(None, None, None, "kz", "ti"),
        P(None, None, "kz", "ti"),
        P(None, None, None, "kz", "ti"),
        P("ti"),
        P("ti", None, None),
    )
    out_specs = (
        P(None, None, "kz", "ti"),
        P(None, None, None, "kz", "ti"),
        P(None, None, "kz", "ti"),
        P(None, None, None, "kz", "ti"),
    )
    return jax.shard_map(shards, mesh=mesh, in_specs=in_specs, out_specs=out_specs, check_vma=False)
```

```python
import math

import jax
import jax.numpy as jnp
import numpy as np
from jax import lax
from jax.experimental import pallas as pl
from jax.experimental.pallas import tpu as pltpu
from jax.sharding import PartitionSpec as P

regular_weight = 2.0
AXES = ("ti", "kz")
NZ, NY, ZB, YB, XS = 160, 256, 20, 16, 8
HALF_Z, HALF_Y = NZ // 2, NY // 2
LANES = 128
FEATURES = 7
PAIRS = FEATURES * ZB
MAIN = 16
TILES = 18
MSG = TILES * LANES
ITEMS = 9
BINS = 8
NEAR = 5
STEPS = ((0, 0), (0, 1), (0, 3), (1, 0), (3, 0), (1, 1), (1, 3), (2, 0))
WHOLE = 2 * TILES
VMEM_LIMIT = 32 * 1024 * 1024
f32 = jnp.float32
bf16 = jnp.bfloat16


def split_pair(table):
    high = table.astype(np.float32).astype(jnp.bfloat16)
    low = (table - high.astype(np.float64)).astype(np.float32).astype(jnp.bfloat16)
    return high, low


def real_form(matrix):
    return np.block([[matrix.real, matrix.imag], [-matrix.imag, matrix.real]])


def right_table(table):
    high, low = split_pair(table)
    return np.concatenate([high, high, low], axis=0)


def left_table(table):
    high, low = split_pair(table)
    pad = np.zeros((table.shape[0], 32), dtype=jnp.bfloat16)
    return np.concatenate([high, high, low, pad], axis=1)


def z_of_rows():
    rows = np.arange(HALF_Z)
    return (rows % 8) * ZB + 2 * (rows // 8)


def make_tables():
    n, m = np.arange(HALF_Y)[:, None], np.arange(HALF_Y)[None, :]
    y_even = real_form(np.exp(-2j * np.pi * (n * (2 * m) % NY) / NY) / math.sqrt(NY))
    y_odd = real_form(np.exp(-2j * np.pi * (n * (2 * m + 1) % NY) / NY) / math.sqrt(NY))
    spots, freq = z_of_rows()[None, :], np.arange(HALF_Z)[:, None]
    z_even = real_form((np.exp(-2j * np.pi * (freq * spots % NZ) / NZ) / math.sqrt(NZ)).T).T
    z_odd = real_form((np.exp(-2j * np.pi * (freq * (spots + 1) % NZ) / NZ) / math.sqrt(NZ)).T).T
    forward_y = np.stack([right_table(y_even), right_table(y_odd)])
    backward_y = np.stack([right_table(y_even.T), right_table(y_odd.T)])
    forward_z = np.stack([left_table(z_even), left_table(z_odd)])
    backward_z = np.stack([left_table(z_even.T), left_table(z_odd.T)])
    order = np.zeros((NY, NY), dtype=jnp.bfloat16)
    for lane in range(NY):
        order[2 * (lane % HALF_Y) + lane // HALF_Y, lane] = 1
    return forward_y, forward_z, backward_y, backward_z, order


def iota(shape, axis):
    return lax.broadcasted_iota(jnp.int32, shape, axis)


def block_transpose(tiles):
    group = iota((8, LANES), 1) >> 4
    tiles = list(tiles)
    for bit in (1, 2, 4):
        unset = (group & bit) == 0
        for i in range(8):
            if i & bit:
                continue
            a, c = tiles[i], tiles[i | bit]
            tiles[i] = jnp.where(unset, a, pltpu.roll(c, 16 * bit, 1))
            tiles[i | bit] = jnp.where(unset, pltpu.roll(a, LANES - 16 * bit, 1), c)
    return tiles


def inner_transpose(tile):
    group, row = iota((8, LANES), 1) >> 4, iota((8, LANES), 0)
    for bit in (1, 2, 4):
        g, s = (group & bit) != 0, (row & bit) != 0
        down = pltpu.roll(pltpu.roll(tile, bit, 0), LANES - 16 * bit, 1)
        up = pltpu.roll(pltpu.roll(tile, 8 - bit, 0), 16 * bit, 1)
        tile = jnp.where(g == s, tile, jnp.where(s, down, up))
    return tile


def halves(values):
    high = values.astype(bf16)
    return high, (values - high.astype(f32)).astype(bf16)


def times_right(values, table):
    high, low = halves(values)
    return jnp.dot(jnp.concatenate([high, low, high], axis=1), table, preferred_element_type=f32)


def times_left(table, values):
    high, low = halves(values)
    pad = jnp.zeros((32, values.shape[1]), bf16)
    return jnp.dot(table, jnp.concatenate([high, low, high, pad], axis=0), preferred_element_type=f32)


def split_rows(values):
    grouped = values.reshape(ZB // 2, 2, 8, values.shape[1])
    return [grouped[:, parity].reshape(HALF_Z, values.shape[1]) for parity in range(2)]


def join_rows(even, odd):
    parts = [side.reshape(ZB // 2, 1, 8, side.shape[1]) for side in (even, odd)]
    return jnp.concatenate(parts, axis=1).reshape(NZ, even.shape[1])


def plane(ref, f):
    return jnp.concatenate([ref[0, f * NZ : (f + 1) * NZ], ref[1, f * NZ : (f + 1) * NZ]], axis=1)


def pairs_of(g):
    return (g, 4 + (g ^ 1))


def names_of(g):
    return [0, 1, 2] + [3 + 8 * p + 2 * g + e for p in range(2) for e in range(2)]


def dense_tiles(maps, coils, stacked, turned, emit, arrive=None):
    blank = jnp.zeros((8, LANES), f32)
    for g in range(4):
        if arrive is not None:
            arrive(g)
        stacked[g, 136:144] = blank
        for i, name in enumerate(names_of(g)):
            if name < 3:
                if g == 0:
                    rows = jnp.swapaxes(maps[name].reshape(8 * YB, ZB), 0, 1)
                    for other in range(4):
                        stacked[other, i * ZB : (i + 1) * ZB] = rows
            else:
                block = coils[(name - 3) // 8, (name - 3) % 8]
                stacked[g, i * ZB : (i + 1) * ZB] = jnp.swapaxes(block.reshape(8 * YB, ZB), 0, 1)
        turned[g] = jnp.swapaxes(stacked[g, :LANES], 0, 1)
        for j in range(MAIN):
            emit(g, j, turned[g, pl.ds(j, 8, stride=YB), :])
        for v in range(2):
            emit(g, MAIN + v, inner_transpose(stacked[g, LANES + 8 * v : LANES + 8 * v + 8]))


def pack_kernel(
    times, maps_in, coils_in, point_maps, point_coils,
    send_out, dense,
    send, maps, coils, of_maps, of_coils, stamp, stacked, turned, sems,
):
    t = lax.axis_index("ti")
    maps_copies = [
        pltpu.make_async_copy(maps_in, maps, sems.at[9]),
        pltpu.make_async_copy(times, stamp, sems.at[10]),
    ]
    coils_copies = [
        pltpu.make_async_copy(
            coils_in.at[p, pl.ds(2 * g, 2)], coils.at[p, pl.ds(2 * g, 2)], sems.at[11 + 2 * g + p]
        )
        for g in range(4)
        for p in range(2)
    ]
    point_copies = []
    items = []
    for i in range(ITEMS):
        item = jnp.minimum((t >> 1) * 18 + 2 * i + (t & 1), PAIRS - 1)
        f = item // ZB
        z = item - f * ZB
        q = jnp.maximum(f - 3, 0)
        items.append(f)
        point_copies.append(
            pltpu.make_async_copy(point_maps.at[jnp.minimum(f, 2), z], of_maps.at[i], sems.at[19 + i])
        )
        point_copies.append(
            pltpu.make_async_copy(point_coils.at[q >> 1, :, q & 1, z], of_coils.at[i], sems.at[28 + i])
        )
    for copy in point_copies + maps_copies + coils_copies:
        copy.start()
    for copy in point_copies:
        copy.wait()
    for copy in maps_copies:
        copy.wait()
    lane = iota((8, LANES), 1)
    spare = jnp.where(lane == 64, stamp[0], jnp.where(lane == 65, stamp[1], 0.0))

    stores = []

    def emit(g, u, tile):
        dense[g, u] = tile
        if u == TILES - 1:
            tile = jnp.where(lane < 64, tile, spare)
        for m in pairs_of(g):
            send[pl.ds(8 * m * WHOLE + u, 8, stride=WHOLE), :] = tile
        if u == TILES - 1:
            for m in pairs_of(g):
                rows = pl.ds(8 * m * WHOLE, 8 * WHOLE)
                stores.append(pltpu.make_async_copy(send.at[rows], send_out.at[rows], sems.at[len(stores)]))
                stores[-1].start()

    def arrive(g):
        for i in range(ITEMS):
            tile = jnp.where(items[i] < 3, of_maps[i], of_coils[i, g])
            for m in pairs_of(g):
                for half in range(2):
                    first = 8 * m * WHOLE + TILES + 2 * i + half
                    send[pl.ds(first, 8, stride=WHOLE), :] = tile[:, half * LANES : (half + 1) * LANES]
        for copy in coils_copies[2 * g : 2 * g + 2]:
            copy.wait()

    dense_tiles(maps, coils, stacked, turned, emit, arrive)
    for copy in stores:
        copy.wait()


def dense_kernel(maps_in, coils_in, dense, maps, coils, stacked, turned, sems):
    copies = [
        pltpu.make_async_copy(maps_in, maps, sems.at[0]),
        pltpu.make_async_copy(coils_in, coils, sems.at[1]),
    ]
    for copy in copies:
        copy.start()
    for copy in copies:
        copy.wait()

    def emit(g, u, tile):
        dense[g, u] = tile

    dense_tiles(maps, coils, stacked, turned, emit)


def unpack(part, c, point, direction, rest):
    for y in range(4):
        for half in range(2):
            firsts = [WHOLE * (4 * (8 * half + i) + y) for i in range(8)]
            rows = [part[first : first + MAIN, :] for first in firsts]
            pairs = jnp.swapaxes(jnp.concatenate(rows, axis=0), 0, 1)
            direction[half, pl.ds(2 * y + c, LANES, stride=8), :] = pairs
    for v in range(2):
        rest[v, pl.ds(c, 64, stride=2), :] = part[pl.ds(MAIN + v, 64, stride=WHOLE), :]
    for i in range(ITEMS):
        for half in range(2):
            for m in range(8):
                n = 18 * m + 2 * i
                if n < PAIRS:
                    first = 8 * m * WHOLE + TILES + 2 * i + half
                    point[half, pl.ds(8 * n + c, 8, stride=2), :] = part[pl.ds(first, 8, stride=WHOLE), :]


def unpack_rest(direction, rest):
    for v in range(2):
        for half in range(2):
            tiles = [rest[v, 8 * (8 * half + i) : 8 * (8 * half + i) + 8] for i in range(8)]
            for member, tile in enumerate(block_transpose(tiles)):
                n = LANES + 8 * v + member
                if n < PAIRS:
                    direction[half, 8 * n : 8 * n + 8] = tile


def model_terms(tau, point):
    decays = jnp.exp(-tau * plane(point, 2))
    return decays, plane(point, 0) - plane(point, 1) * decays


def forward_bin(tau, point, direction, table_y, table_z, spectrum):
    amplitude = plane(point, 1)
    decays, signal = model_terms(tau, point)
    change = plane(direction, 0) - plane(direction, 1) * decays + amplitude * tau * decays * plane(direction, 2)
    evens, odds = [], []
    for c in range(2):
        re = plane(point, 3 + c) * change + plane(direction, 3 + c) * signal
        im = plane(point, 5 + c) * change + plane(direction, 5 + c) * signal
        re_low, re_high, im_low, im_high = re[:, :HALF_Y], re[:, HALF_Y:], im[:, :HALF_Y], im[:, HALF_Y:]
        evens.append(jnp.concatenate([re_low + re_high, im_low + im_high], axis=1))
        odds.append(jnp.concatenate([re_low - re_high, im_low - im_high], axis=1))
    along_even = times_right(jnp.concatenate(evens, axis=0), table_y[0])
    along_odd = times_right(jnp.concatenate(odds, axis=0), table_y[1])
    for c in range(2):
        rows = slice(c * NZ, (c + 1) * NZ)
        re = jnp.concatenate([along_even[rows, :HALF_Y], along_odd[rows, :HALF_Y]], axis=1)
        im = jnp.concatenate([along_even[rows, HALF_Y:], along_odd[rows, HALF_Y:]], axis=1)
        parts = [
            times_left(table_z[parity], jnp.concatenate(pair, axis=0))
            for parity, pair in enumerate(zip(split_rows(re), split_rows(im)))
        ]
        for part in range(2):
            a, b = (side[part * HALF_Z : (part + 1) * HALF_Z] for side in parts)
            spectrum[c, part, :HALF_Z] = a + b
            spectrum[c, part, HALF_Z:] = a - b
    return decays, signal


def backward_bin(tau, decays, signal, mask, spectrum, point, table_y, table_z, order, total):
    weights = jnp.dot(mask.astype(f32).astype(bf16), order[...], preferred_element_type=f32)
    evens, odds = [], []
    for c in range(2):
        plus, minus = [], []
        for part in range(2):
            values = spectrum[c, part] * weights
            plus.append(values[:HALF_Z] + values[HALF_Z:])
            minus.append(values[:HALF_Z] - values[HALF_Z:])
        for parity, side in enumerate((plus, minus)):
            out = times_left(table_z[parity], jnp.concatenate(side, axis=0))
            re, im = out[:HALF_Z], out[HALF_Z:]
            evens.append(jnp.concatenate([re[:, :HALF_Y], im[:, :HALF_Y]], axis=1))
            odds.append(jnp.concatenate([re[:, HALF_Y:], im[:, HALF_Y:]], axis=1))
    from_even = times_right(jnp.concatenate(evens, axis=0), table_y[0])
    from_odd = times_right(jnp.concatenate(odds, axis=0), table_y[1])
    low, high = from_even + from_odd, from_even - from_odd

    def add(f, values):
        for half in range(2):
            total[half, f * NZ : (f + 1) * NZ] += values[:, half * LANES : (half + 1) * LANES]

    projected = None
    for c in range(2):
        sides = []
        for lanes in (slice(0, HALF_Y), slice(HALF_Y, NY)):
            value = jnp.concatenate([low[:, lanes], high[:, lanes]], axis=1)
            first = 2 * c * HALF_Z
            sides.append(join_rows(value[first : first + HALF_Z], value[first + HALF_Z : first + NZ]))
        re, im = sides
        term = plane(point, 3 + c) * re + plane(point, 5 + c) * im
        projected = term if projected is None else projected + term
        add(3 + c, signal * re)
        add(5 + c, signal * im)
    add(0, projected)
    faded = decays * projected
    add(1, -faded)
    add(2, plane(point, 1) * (tau * faded))


def pack_sums(core, total, sent, rest, mine, theirs):
    for k in range(8):
        place = (k & 1) ^ core
        for half in range(2):
            pairs = jnp.swapaxes(total[half, pl.ds(k, LANES, stride=8), :], 0, 1)
            for i in range(8):
                first = TILES * (4 * (8 * half + i) + (k >> 1))
                sent[place, first : first + MAIN, :] = pairs[YB * i : YB * (i + 1)]
    for v in range(2):
        for half in range(2):
            tiles = []
            for member in range(8):
                n = min(LANES + 8 * v + member, PAIRS - 1)
                tiles.append(total[half, 8 * n : 8 * n + 8])
            for i, tile in enumerate(block_transpose(tiles)):
                rest[v, 8 * (8 * half + i) : 8 * (8 * half + i) + 8] = tile
        for c in range(2):
            rows = pl.ds(MAIN + v, 64, stride=TILES)
            sent[c ^ core, rows, :] = rest[v, pl.ds(c, 64, stride=2), :]
    mine[...] = sent[0]
    theirs[...] = sent[1]


def tables_kernel(after, *refs):
    del after
    sources, targets, sems = refs[:5], refs[5:10], refs[10]
    copies = [pltpu.make_async_copy(a, b, sems.at[i]) for i, (a, b) in enumerate(zip(sources, targets))]
    for copy in copies:
        copy.start()
    for copy in copies:
        copy.wait()


def first_kernel(*refs):
    own, other, *masks = refs[: 2 + NEAR]
    forward_y, forward_z, backward_y, backward_z, order = refs[2 + NEAR : 7 + NEAR]
    spectra, point, taus, total, direction, rest, kept = refs[7 + NEAR :]
    step = pl.program_id(0)
    t, core = lax.axis_index("ti"), lax.axis_index("kz") & 1

    def prepare():
        total[...] = jnp.zeros_like(total)
        unpack(own, core, point, direction, rest)
        unpack(other, 1 - core, point, direction, rest)
        unpack_rest(direction, rest)

    def bin_time(n):
        along_z, along_x = STEPS[n]
        bin_of = (((t >> 2) + along_z) & 3) * 4 + ((t + along_x) & 3)
        block = rest[1, pl.ds(pl.multiple_of(bin_of * 8, 8), 8), :]
        chosen = (iota((8, LANES), 0) == 0) & (iota((8, LANES), 1) == 64 + core)
        tau = jnp.sum(jnp.where(chosen, block, 0.0), axis=(0, 1), keepdims=True)
        taus[n] = jnp.broadcast_to(tau, (8, LANES))
        return tau

    for first in range(0, BINS, 2):

        @pl.when(step == first // 2)
        def _():
            if first == 0:
                prepare()
            done = []
            for n in (first, first + 1):
                tau = bin_time(n)
                spectrum = kept.at[n & 1] if n < NEAR else spectra.at[n - NEAR]
                done.append((n, tau, spectrum, forward_bin(tau, point, direction, forward_y, forward_z, spectrum)))
            for n, tau, spectrum, terms in done:
                if n < NEAR:
                    backward_bin(tau, *terms, masks[n][...], spectrum, point, backward_y, backward_z, order, total)


def second_kernel(mask, spectra, point, taus, total_in, table_y, table_z, order, mine, theirs, total, sent, rest):
    core = lax.axis_index("kz") & 1
    total[...] = total_in[...]
    for n in range(NEAR, BINS):
        tau = taus[n, 0:1, 0:1]
        terms = model_terms(tau, point)
        backward_bin(tau, *terms, mask[n - NEAR], spectra.at[n - NEAR], point, table_y, table_z, order, total)
    pack_sums(core, total, sent, rest, mine, theirs)


def sums_kernel(received, direction, residual, applied_out, out_sums, applied, sems):
    lane = iota((8, LANES), 1)
    sums = [jnp.zeros((8, LANES), f32) for _ in range(4)]
    copies = []
    for u in range(TILES):
        sides = []
        for g in range(4):
            upper, lower = (received[pl.ds(8 * m * TILES + u, 8, stride=TILES), :] for m in pairs_of(g))
            sides.append(upper + lower)
        if u < MAIN:
            maps = sides[0] + sides[1] + sides[2] + sides[3]
        for g in range(4):
            d, r, value = direction[g, u], residual[g, u], sides[g]
            if u < MAIN:
                of_maps = lane < 3 * ZB
                if g == 0:
                    value = jnp.where(of_maps, maps, value)
                else:
                    d, r, value = (jnp.where(of_maps, 0.0, a) for a in (d, r, value))
            elif u == TILES - 1:
                d, r, value = (jnp.where(lane < 64, a, 0.0) for a in (d, r, value))
            q = value + regular_weight * d
            applied[u, g] = q
            for i, (a, b) in enumerate(((r, r), (d, q), (r, q), (q, q))):
                sums[i] = sums[i] + a * b
        if u % 6 == 5:
            part = pl.ds(u - 5, 6)
            copies.append(pltpu.make_async_copy(applied.at[part], applied_out.at[part], sems.at[u // 6]))
            copies[-1].start()
    line = jnp.zeros((1, LANES), f32)
    for i in range(4):
        value = jnp.sum(sums[i], axis=(0, 1), keepdims=True)
        line = jnp.where(iota((1, LANES), 1) == i, value, line)
    out_sums[...] = jnp.broadcast_to(line, (LANES, LANES))
    for copy in copies:
        copy.wait()


def native_kernel(
    dense_in, dir_coils, res_coils, maps_out, fields, dense, maps, stacked, turned, sems
):
    copies = [
        pltpu.make_async_copy(source.at[p], fields.at[pl.ds(first + 8 * p, 8)], sems.at[2 * i + p])
        for i, (source, first) in enumerate(((dir_coils, 16), (res_coils, 32)))
        for p in range(2)
    ]
    copies.append(pltpu.make_async_copy(dense_in, dense, sems.at[5]))
    copies[-1].start()
    for copy in copies[:-1]:
        copy.start()
    copies.pop().wait()
    for g in range(4):
        for j in range(MAIN):
            turned[g, pl.ds(j, 8, stride=YB), :] = dense[j, g]
        stacked[g, :LANES] = jnp.swapaxes(turned[g], 0, 1)
        for v in range(2):
            stacked[g, LANES + 8 * v : LANES + 8 * v + 8] = inner_transpose(dense[MAIN + v, g])
        for i, name in enumerate(names_of(g)):
            if name < 3 and g:
                continue
            block = jnp.swapaxes(stacked[g, i * ZB : (i + 1) * ZB], 0, 1).reshape(XS, YB, ZB)
            if name < 3:
                maps[name] = block
            else:
                fields[name - 3] = block
    copies.append(pltpu.make_async_copy(maps, maps_out, sems.at[4]))
    copies[-1].start()
    for copy in copies:
        copy.wait()


def step_kernel(sums, fields, app_maps, dir_maps, res_maps, *refs):
    outs, (maps, made_maps, made_coils, sems) = refs[:4], refs[4:]
    copies = [
        pltpu.make_async_copy(source, maps.at[i], sems.at[i])
        for i, source in enumerate((app_maps, dir_maps, res_maps))
    ]
    for copy in copies:
        copy.start()
    line = jnp.sum(sums[...], axis=0, keepdims=True)
    lane = iota((1, LANES), 1)
    old, curve, cross, square = (
        jnp.sum(jnp.where(lane == i, line, 0.0), axis=1, keepdims=True) for i in range(4)
    )
    size = old / curve
    new = old - 2.0 * size * cross + size * size * square
    ratio = (new / old).reshape(1, 1, 1)
    size = size.reshape(1, 1, 1)
    stores = []
    for first in range(0, 16, 4):
        for coil in range(first, first + 4):
            fresh = fields[32 + coil] - size * fields[coil]
            made_coils[0, coil] = fresh
            made_coils[1, coil] = fresh + ratio * fields[16 + coil]
        part, rows = first // 8, pl.ds(first % 8, 4)
        for i in range(2):
            stores.append(
                pltpu.make_async_copy(
                    made_coils.at[i, pl.ds(first, 4)], outs[1 + 2 * i].at[part, rows], sems.at[3 + len(stores)]
                )
            )
            stores[-1].start()
    for copy in copies:
        copy.wait()
    for f in range(3):
        fresh = maps[2, f] - size * maps[0, f]
        made_maps[0, f] = fresh
        made_maps[1, f] = fresh + ratio * maps[1, f]
    for i in range(2):
        stores.append(pltpu.make_async_copy(made_maps.at[i], outs[2 * i], sems.at[3 + len(stores)]))
        stores[-1].start()
    for copy in stores:
        copy.wait()


def struct(*shape):
    return jax.ShapeDtypeStruct(shape, f32)


HBM = pl.BlockSpec(memory_space=pltpu.HBM)
VMEM = pl.BlockSpec(memory_space=pltpu.VMEM)
SCRATCH_STACKED = pltpu.VMEM((4, 144, LANES), f32)
SCRATCH_TURNED = pltpu.VMEM((4, LANES, LANES), f32)


def params():
    return pltpu.CompilerParams(vmem_limit_bytes=VMEM_LIMIT)


def cost(micros):
    return pl.CostEstimate(flops=int(micros * 4e8), bytes_accessed=int(micros * 2e6), transcendentals=0)


def constant_block(shape):
    return pl.BlockSpec(shape, lambda s: (0,) * len(shape))


def in_hbm(*values):
    return tuple(pltpu.with_memory_space_constraint(value, pltpu.HBM) for value in values)


def in_vmem(*values):
    return tuple(pltpu.with_memory_space_constraint(value, pltpu.VMEM) for value in values)


def far(*shape):
    return pltpu.HBM(shape, f32)


def near(*shape):
    return pltpu.VMEM(shape, f32)


def core_swap(values):
    return lax.ppermute(values, "kz", [(i, i ^ 1) for i in range(8)])


def by_parity(values):
    groups = [[i for i in range(128) if i & 1 == c] for c in range(2)]
    messages = values.reshape(64, 1, values.shape[0] // 64 * LANES)
    return lax.all_to_all(messages, AXES, 0, 0, axis_index_groups=groups).reshape(values.shape)


def shards(
    point_maps,
    point_coils,
    direction_maps,
    direction_coils,
    residual_maps,
    residual_coils,
    inversion_times,
    sampling_mask,
):
    forward_y, forward_z, backward_y, backward_z, order = (jnp.asarray(table) for table in make_tables())
    dir_maps, dir_coils = jnp.swapaxes(direction_maps, 2, 3), jnp.swapaxes(direction_coils, 3, 4)
    res_maps, res_coils = jnp.swapaxes(residual_maps, 2, 3), jnp.swapaxes(residual_coils, 3, 4)
    pnt_maps = jnp.swapaxes(point_maps, 1, 2)
    pnt_coils = jnp.swapaxes(point_coils, 2, 3).reshape(2, 4, 2, ZB, XS, NY)

    send, dir_dense = pl.pallas_call(
        pack_kernel,
        out_shape=(
            far(64 * WHOLE, LANES),
            near(4, TILES, 8, LANES),
        ),
        in_specs=[HBM] * 5,
        out_specs=(HBM, VMEM),
        scratch_shapes=[
            pltpu.VMEM((64 * WHOLE, LANES), f32),
            pltpu.VMEM(dir_maps.shape, f32),
            pltpu.VMEM(dir_coils.shape, f32),
            pltpu.VMEM((ITEMS, 8, NY), f32),
            pltpu.VMEM((ITEMS, 4, 8, NY), f32),
            pltpu.SMEM((2,), f32),
            SCRATCH_STACKED,
            SCRATCH_TURNED,
            pltpu.SemaphoreType.DMA((37,)),
        ],
        compiler_params=params(),
        cost_estimate=cost(4),
        name="pack",
    )(*in_hbm(inversion_times, dir_maps, dir_coils, pnt_maps, pnt_coils))

    def densify(maps, coils):
        return pl.pallas_call(
            dense_kernel,
            out_shape=near(4, TILES, 8, LANES),
            in_specs=[HBM] * 2,
            out_specs=VMEM,
            scratch_shapes=[
                pltpu.VMEM(maps.shape, f32),
                pltpu.VMEM(coils.shape, f32),
                SCRATCH_STACKED,
                SCRATCH_TURNED,
                pltpu.SemaphoreType.DMA((2,)),
            ],
            compiler_params=params(),
            cost_estimate=cost(3),
            name="dense",
        )(*in_hbm(maps, coils))

    own_mask = lax.dynamic_index_in_dim(sampling_mask, lax.axis_index("kz") & 1, 0, keepdims=False)

    def from_ti(values, move):
        pairs = [((((i >> 2) + move[0]) & 3) * 4 + ((i + move[1]) & 3), i) for i in range(16)]
        return lax.ppermute(values, "ti", pairs)

    masks = [own_mask] + [from_ti(own_mask, move) for move in STEPS[1:NEAR]]
    send, *masks = lax.optimization_barrier((send, *masks))
    own = by_parity(send)
    res_dense = densify(*lax.optimization_barrier((res_maps, res_coils, dir_dense))[:2])
    stack = jnp.stack(masks[1:4])
    own, res_dense, stack = lax.optimization_barrier((own, res_dense, stack))
    other = core_swap(own)
    far_masks = from_ti(stack, STEPS[3])
    planes = (2, FEATURES * NZ, LANES)
    tables = (forward_y, forward_z, backward_y, backward_z, order)
    sums_shape = struct(64 * TILES, LANES)
    sent_scratch = pltpu.VMEM((2, 64 * TILES, LANES), f32)
    near_tables = in_vmem(
        *pl.pallas_call(
            tables_kernel,
            out_shape=[pltpu.VMEM(table.shape, bf16) for table in tables],
            in_specs=[pl.BlockSpec(memory_space=pl.ANY)] + [HBM] * 5,
            out_specs=[VMEM] * 5,
            scratch_shapes=[pltpu.SemaphoreType.DMA((5,))],
            compiler_params=params(),
            cost_estimate=cost(2),
            name="tables",
        )(own, *in_hbm(*tables))
    )
    spectra, point, taus, total = pl.pallas_call(
        first_kernel,
        grid=(BINS // 2,),
        out_shape=(
            near(BINS - NEAR, 2, 2, NZ, NY),
            near(*planes),
            near(BINS, 8, LANES),
            near(*planes),
        ),
        in_specs=[constant_block(own.shape)] * 2
        + [constant_block((NZ, NY))] * NEAR
        + [VMEM] * 5,
        out_specs=(
            constant_block((BINS - NEAR, 2, 2, NZ, NY)),
            constant_block(planes),
            constant_block((BINS, 8, LANES)),
            constant_block(planes),
        ),
        scratch_shapes=[
            pltpu.VMEM(planes, f32),
            pltpu.VMEM((2, LANES, LANES), f32),
            pltpu.VMEM((2, 2, 2, NZ, NY), f32),
        ],
        compiler_params=params(),
        cost_estimate=cost(15),
        name="first",
    )(own, other, *masks, *near_tables)

    mine, theirs = pl.pallas_call(
        second_kernel,
        out_shape=(sums_shape, sums_shape),
        in_specs=[VMEM] * 8,
        out_specs=(VMEM, VMEM),
        scratch_shapes=[
            pltpu.VMEM(planes, f32),
            sent_scratch,
            pltpu.VMEM((2, LANES, LANES), f32),
        ],
        compiler_params=params(),
        cost_estimate=cost(4),
        name="second",
    )(far_masks, *in_vmem(spectra, point, taus, total), *near_tables[2:])

    received = by_parity(mine + core_swap(theirs))
    app_dense, sums = pl.pallas_call(
        sums_kernel,
        out_shape=(far(TILES, 4, 8, LANES), near(128, LANES)),
        in_specs=[VMEM] * 3,
        out_specs=(HBM, VMEM),
        scratch_shapes=[pltpu.VMEM((TILES, 4, 8, LANES), f32), pltpu.SemaphoreType.DMA((3,))],
        compiler_params=params(),
        cost_estimate=cost(1),
        name="sums",
    )(received, *in_vmem(dir_dense, res_dense))
    all_sums = lax.all_to_all(sums.reshape(128, 1, LANES), AXES, 0, 0).reshape(128, LANES)

    maps_shape, coils_shape = far(*dir_maps.shape), far(*dir_coils.shape)
    app_maps, fields = pl.pallas_call(
        native_kernel,
        out_shape=(far(*dir_maps.shape), near(48, XS, YB, ZB)),
        in_specs=[HBM] * 3,
        out_specs=(HBM, VMEM),
        scratch_shapes=[
            pltpu.VMEM((TILES, 4, 8, LANES), f32),
            pltpu.VMEM(dir_maps.shape, f32),
            SCRATCH_STACKED,
            SCRATCH_TURNED,
            pltpu.SemaphoreType.DMA((6,)),
        ],
        compiler_params=params(),
        cost_estimate=cost(3),
        name="native",
    )(*in_hbm(app_dense, dir_coils, res_coils))

    outs = pl.pallas_call(
        step_kernel,
        out_shape=(maps_shape, coils_shape, maps_shape, coils_shape),
        in_specs=[VMEM] * 2 + [HBM] * 3,
        out_specs=(HBM,) * 4,
        scratch_shapes=[
            pltpu.VMEM((3,) + dir_maps.shape, f32),
            pltpu.VMEM((2,) + dir_maps.shape, f32),
            pltpu.VMEM((2, 16, XS, YB, ZB), f32),
            pltpu.SemaphoreType.DMA((13,)),
        ],
        compiler_params=params(),
        cost_estimate=cost(2),
        name="step",
    )(all_sums, *in_vmem(fields), *in_hbm(app_maps, dir_maps, res_maps))
    return tuple(jnp.swapaxes(out, -2, -1) for out in outs)


def solution(mesh):
    in_specs = (
        P(None, None, "kz", None),
        P(None, None, None, "kz", None),
        P(None, None, "kz", "ti"),
        P(None, None, None, "kz", "ti"),
        P(None, None, "kz", "ti"),
        P(None, None, None, "kz", "ti"),
        P("ti"),
        P("ti", None, None),
    )
    out_specs = (
        P(None, None, "kz", "ti"),
        P(None, None, None, "kz", "ti"),
        P(None, None, "kz", "ti"),
        P(None, None, None, "kz", "ti"),
    )
    return jax.shard_map(shards, mesh=mesh, in_specs=in_specs, out_specs=out_specs, check_vma=False)
```

```python
import math

import jax
import jax.numpy as jnp
import numpy as np
from jax import lax
from jax.experimental import pallas as pl
from jax.experimental.pallas import tpu as pltpu
from jax.sharding import PartitionSpec as P

regular_weight = 2.0
AXES = ("ti", "kz")
NZ, NY, ZB, YB, XS = 160, 256, 20, 16, 8
HALF_Z, HALF_Y = NZ // 2, NY // 2
LANES = 128
FEATURES = 7
PAIRS = FEATURES * ZB
MAIN = 16
TILES = 18
MSG = TILES * LANES
ITEMS = 9
BINS = 8
NEAR = 5
STEPS = ((0, 0), (0, 1), (0, 3), (1, 0), (3, 0), (1, 1), (1, 3), (2, 0))
WHOLE = 2 * TILES
VMEM_LIMIT = 32 * 1024 * 1024
f32 = jnp.float32
bf16 = jnp.bfloat16


def split_pair(table):
    high = table.astype(np.float32).astype(jnp.bfloat16)
    low = (table - high.astype(np.float64)).astype(np.float32).astype(jnp.bfloat16)
    return high, low


def real_form(matrix):
    return np.block([[matrix.real, matrix.imag], [-matrix.imag, matrix.real]])


def right_table(table):
    high, low = split_pair(table)
    return np.concatenate([high, high, low], axis=0)


def left_table(table):
    high, low = split_pair(table)
    pad = np.zeros((table.shape[0], 32), dtype=jnp.bfloat16)
    return np.concatenate([high, high, low, pad], axis=1)


def z_of_rows():
    rows = np.arange(HALF_Z)
    return (rows % 8) * ZB + 2 * (rows // 8)


def make_tables():
    n, m = np.arange(HALF_Y)[:, None], np.arange(HALF_Y)[None, :]
    y_even = real_form(np.exp(-2j * np.pi * (n * (2 * m) % NY) / NY) / math.sqrt(NY))
    y_odd = real_form(np.exp(-2j * np.pi * (n * (2 * m + 1) % NY) / NY) / math.sqrt(NY))
    spots, freq = z_of_rows()[None, :], np.arange(HALF_Z)[:, None]
    z_even = real_form((np.exp(-2j * np.pi * (freq * spots % NZ) / NZ) / math.sqrt(NZ)).T).T
    z_odd = real_form((np.exp(-2j * np.pi * (freq * (spots + 1) % NZ) / NZ) / math.sqrt(NZ)).T).T
    forward_y = np.stack([right_table(y_even), right_table(y_odd)])
    backward_y = np.stack([right_table(y_even.T), right_table(y_odd.T)])
    forward_z = np.stack([left_table(z_even), left_table(z_odd)])
    backward_z = np.stack([left_table(z_even.T), left_table(z_odd.T)])
    order = np.zeros((NY, NY), dtype=jnp.bfloat16)
    for lane in range(NY):
        order[2 * (lane % HALF_Y) + lane // HALF_Y, lane] = 1
    return forward_y, forward_z, backward_y, backward_z, order


def iota(shape, axis):
    return lax.broadcasted_iota(jnp.int32, shape, axis)


def block_transpose(tiles):
    group = iota((8, LANES), 1) >> 4
    tiles = list(tiles)
    for bit in (1, 2, 4):
        unset = (group & bit) == 0
        for i in range(8):
            if i & bit:
                continue
            a, c = tiles[i], tiles[i | bit]
            tiles[i] = jnp.where(unset, a, pltpu.roll(c, 16 * bit, 1))
            tiles[i | bit] = jnp.where(unset, pltpu.roll(a, LANES - 16 * bit, 1), c)
    return tiles


def inner_transpose(tile):
    group, row = iota((8, LANES), 1) >> 4, iota((8, LANES), 0)
    for bit in (1, 2, 4):
        g, s = (group & bit) != 0, (row & bit) != 0
        down = pltpu.roll(pltpu.roll(tile, bit, 0), LANES - 16 * bit, 1)
        up = pltpu.roll(pltpu.roll(tile, 8 - bit, 0), 16 * bit, 1)
        tile = jnp.where(g == s, tile, jnp.where(s, down, up))
    return tile


def halves(values):
    high = values.astype(bf16)
    return high, (values - high.astype(f32)).astype(bf16)


def times_right(values, table):
    high, low = halves(values)
    return jnp.dot(jnp.concatenate([high, low, high], axis=1), table, preferred_element_type=f32)


def times_left(table, values):
    high, low = halves(values)
    pad = jnp.zeros((32, values.shape[1]), bf16)
    return jnp.dot(table, jnp.concatenate([high, low, high, pad], axis=0), preferred_element_type=f32)


def split_rows(values):
    grouped = values.reshape(ZB // 2, 2, 8, values.shape[1])
    return [grouped[:, parity].reshape(HALF_Z, values.shape[1]) for parity in range(2)]


def join_rows(even, odd):
    parts = [side.reshape(ZB // 2, 1, 8, side.shape[1]) for side in (even, odd)]
    return jnp.concatenate(parts, axis=1).reshape(NZ, even.shape[1])


def plane(ref, f):
    return jnp.concatenate([ref[0, f * NZ : (f + 1) * NZ], ref[1, f * NZ : (f + 1) * NZ]], axis=1)


def pairs_of(g):
    return (g, 4 + (g ^ 1))


def names_of(g):
    return [0, 1, 2] + [3 + 8 * p + 2 * g + e for p in range(2) for e in range(2)]


def dense_tiles(maps, coils, stacked, turned, emit, arrive=None):
    blank = jnp.zeros((8, LANES), f32)
    for g in range(4):
        if arrive is not None:
            arrive(g)
        stacked[g, 136:144] = blank
        for i, name in enumerate(names_of(g)):
            if name < 3:
                if g == 0:
                    rows = jnp.swapaxes(maps[name].reshape(8 * YB, ZB), 0, 1)
                    for other in range(4):
                        stacked[other, i * ZB : (i + 1) * ZB] = rows
            else:
                block = coils[(name - 3) // 8, (name - 3) % 8]
                stacked[g, i * ZB : (i + 1) * ZB] = jnp.swapaxes(block.reshape(8 * YB, ZB), 0, 1)
        turned[g] = jnp.swapaxes(stacked[g, :LANES], 0, 1)
        for j in range(MAIN):
            emit(g, j, turned[g, pl.ds(j, 8, stride=YB), :])
        for v in range(2):
            emit(g, MAIN + v, inner_transpose(stacked[g, LANES + 8 * v : LANES + 8 * v + 8]))


def pack_kernel(
    times, maps_in, coils_in, point_maps, point_coils,
    send_out, dense,
    send, maps, coils, of_maps, of_coils, stamp, stacked, turned, sems,
):
    t = lax.axis_index("ti")
    maps_copies = [
        pltpu.make_async_copy(maps_in, maps, sems.at[9]),
        pltpu.make_async_copy(times, stamp, sems.at[10]),
    ]
    coils_copies = [
        pltpu.make_async_copy(
            coils_in.at[p, pl.ds(2 * g, 2)], coils.at[p, pl.ds(2 * g, 2)], sems.at[11 + 2 * g + p]
        )
        for g in range(4)
        for p in range(2)
    ]
    point_copies = []
    items = []
    for i in range(ITEMS):
        item = jnp.minimum((t >> 1) * 18 + 2 * i + (t & 1), PAIRS - 1)
        f = item // ZB
        z = item - f * ZB
        q = jnp.maximum(f - 3, 0)
        items.append(f)
        point_copies.append(
            pltpu.make_async_copy(point_maps.at[jnp.minimum(f, 2), z], of_maps.at[i], sems.at[19 + i])
        )
        point_copies.append(
            pltpu.make_async_copy(point_coils.at[q >> 1, :, q & 1, z], of_coils.at[i], sems.at[28 + i])
        )
    for copy in point_copies + maps_copies + coils_copies:
        copy.start()
    for copy in point_copies:
        copy.wait()
    for copy in maps_copies:
        copy.wait()
    lane = iota((8, LANES), 1)
    spare = jnp.where(lane == 64, stamp[0], jnp.where(lane == 65, stamp[1], 0.0))

    stores = []

    def emit(g, u, tile):
        dense[g, u] = tile
        if u == TILES - 1:
            tile = jnp.where(lane < 64, tile, spare)
        for m in pairs_of(g):
            send[pl.ds(8 * m * WHOLE + u, 8, stride=WHOLE), :] = tile
        if u == TILES - 1:
            for m in pairs_of(g):
                rows = pl.ds(8 * m * WHOLE, 8 * WHOLE)
                stores.append(pltpu.make_async_copy(send.at[rows], send_out.at[rows], sems.at[len(stores)]))
                stores[-1].start()

    def arrive(g):
        for i in range(ITEMS):
            tile = jnp.where(items[i] < 3, of_maps[i], of_coils[i, g])
            for m in pairs_of(g):
                for half in range(2):
                    first = 8 * m * WHOLE + TILES + 2 * i + half
                    send[pl.ds(first, 8, stride=WHOLE), :] = tile[:, half * LANES : (half + 1) * LANES]
        for copy in coils_copies[2 * g : 2 * g + 2]:
            copy.wait()

    dense_tiles(maps, coils, stacked, turned, emit, arrive)
    for copy in stores:
        copy.wait()


def dense_kernel(maps_in, coils_in, dense, maps, coils, stacked, turned, sems):
    copies = [
        pltpu.make_async_copy(maps_in, maps, sems.at[0]),
        pltpu.make_async_copy(coils_in, coils, sems.at[1]),
    ]
    for copy in copies:
        copy.start()
    for copy in copies:
        copy.wait()

    def emit(g, u, tile):
        dense[g, u] = tile

    dense_tiles(maps, coils, stacked, turned, emit)


def unpack(part, c, point, direction, rest):
    for y in range(4):
        for half in range(2):
            firsts = [WHOLE * (4 * (8 * half + i) + y) for i in range(8)]
            rows = [part[first : first + MAIN, :] for first in firsts]
            pairs = jnp.swapaxes(jnp.concatenate(rows, axis=0), 0, 1)
            direction[half, pl.ds(2 * y + c, LANES, stride=8), :] = pairs
    for v in range(2):
        rest[v, pl.ds(c, 64, stride=2), :] = part[pl.ds(MAIN + v, 64, stride=WHOLE), :]
    for i in range(ITEMS):
        for half in range(2):
            for m in range(8):
                n = 18 * m + 2 * i
                if n < PAIRS:
                    first = 8 * m * WHOLE + TILES + 2 * i + half
                    point[half, pl.ds(8 * n + c, 8, stride=2), :] = part[pl.ds(first, 8, stride=WHOLE), :]


def unpack_rest(direction, rest):
    for v in range(2):
        for half in range(2):
            tiles = [rest[v, 8 * (8 * half + i) : 8 * (8 * half + i) + 8] for i in range(8)]
            for member, tile in enumerate(block_transpose(tiles)):
                n = LANES + 8 * v + member
                if n < PAIRS:
                    direction[half, 8 * n : 8 * n + 8] = tile


def model_terms(tau, point):
    decays = jnp.exp(-tau * plane(point, 2))
    return decays, plane(point, 0) - plane(point, 1) * decays


def forward_bin(tau, point, direction, table_y, table_z, spectrum):
    amplitude = plane(point, 1)
    decays, signal = model_terms(tau, point)
    change = plane(direction, 0) - plane(direction, 1) * decays + amplitude * tau * decays * plane(direction, 2)
    evens, odds = [], []
    for c in range(2):
        re = plane(point, 3 + c) * change + plane(direction, 3 + c) * signal
        im = plane(point, 5 + c) * change + plane(direction, 5 + c) * signal
        re_low, re_high, im_low, im_high = re[:, :HALF_Y], re[:, HALF_Y:], im[:, :HALF_Y], im[:, HALF_Y:]
        evens.append(jnp.concatenate([re_low + re_high, im_low + im_high], axis=1))
        odds.append(jnp.concatenate([re_low - re_high, im_low - im_high], axis=1))
    along_even = times_right(jnp.concatenate(evens, axis=0), table_y[0])
    along_odd = times_right(jnp.concatenate(odds, axis=0), table_y[1])
    for c in range(2):
        rows = slice(c * NZ, (c + 1) * NZ)
        re = jnp.concatenate([along_even[rows, :HALF_Y], along_odd[rows, :HALF_Y]], axis=1)
        im = jnp.concatenate([along_even[rows, HALF_Y:], along_odd[rows, HALF_Y:]], axis=1)
        parts = [
            times_left(table_z[parity], jnp.concatenate(pair, axis=0))
            for parity, pair in enumerate(zip(split_rows(re), split_rows(im)))
        ]
        for part in range(2):
            a, b = (side[part * HALF_Z : (part + 1) * HALF_Z] for side in parts)
            spectrum[c, part, :HALF_Z] = a + b
            spectrum[c, part, HALF_Z:] = a - b
    return decays, signal


def backward_bin(tau, decays, signal, mask, spectrum, point, table_y, table_z, order, total):
    weights = jnp.dot(mask.astype(f32).astype(bf16), order[...], preferred_element_type=f32)
    evens, odds = [], []
    for c in range(2):
        plus, minus = [], []
        for part in range(2):
            values = spectrum[c, part] * weights
            plus.append(values[:HALF_Z] + values[HALF_Z:])
            minus.append(values[:HALF_Z] - values[HALF_Z:])
        for parity, side in enumerate((plus, minus)):
            out = times_left(table_z[parity], jnp.concatenate(side, axis=0))
            re, im = out[:HALF_Z], out[HALF_Z:]
            evens.append(jnp.concatenate([re[:, :HALF_Y], im[:, :HALF_Y]], axis=1))
            odds.append(jnp.concatenate([re[:, HALF_Y:], im[:, HALF_Y:]], axis=1))
    from_even = times_right(jnp.concatenate(evens, axis=0), table_y[0])
    from_odd = times_right(jnp.concatenate(odds, axis=0), table_y[1])
    low, high = from_even + from_odd, from_even - from_odd

    def add(f, values):
        for half in range(2):
            total[half, f * NZ : (f + 1) * NZ] += values[:, half * LANES : (half + 1) * LANES]

    projected = None
    for c in range(2):
        sides = []
        for lanes in (slice(0, HALF_Y), slice(HALF_Y, NY)):
            value = jnp.concatenate([low[:, lanes], high[:, lanes]], axis=1)
            first = 2 * c * HALF_Z
            sides.append(join_rows(value[first : first + HALF_Z], value[first + HALF_Z : first + NZ]))
        re, im = sides
        term = plane(point, 3 + c) * re + plane(point, 5 + c) * im
        projected = term if projected is None else projected + term
        add(3 + c, signal * re)
        add(5 + c, signal * im)
    add(0, projected)
    faded = decays * projected
    add(1, -faded)
    add(2, plane(point, 1) * (tau * faded))


def pack_sums(core, total, sent, rest, mine, theirs):
    for k in range(8):
        place = (k & 1) ^ core
        for half in range(2):
            pairs = jnp.swapaxes(total[half, pl.ds(k, LANES, stride=8), :], 0, 1)
            for i in range(8):
                first = TILES * (4 * (8 * half + i) + (k >> 1))
                sent[place, first : first + MAIN, :] = pairs[YB * i : YB * (i + 1)]
    for v in range(2):
        for half in range(2):
            tiles = []
            for member in range(8):
                n = min(LANES + 8 * v + member, PAIRS - 1)
                tiles.append(total[half, 8 * n : 8 * n + 8])
            for i, tile in enumerate(block_transpose(tiles)):
                rest[v, 8 * (8 * half + i) : 8 * (8 * half + i) + 8] = tile
        for c in range(2):
            rows = pl.ds(MAIN + v, 64, stride=TILES)
            sent[c ^ core, rows, :] = rest[v, pl.ds(c, 64, stride=2), :]
    mine[...] = sent[0]
    theirs[...] = sent[1]


def tables_kernel(after, *refs):
    del after
    sources, targets, sems = refs[:2], refs[2:4], refs[4]
    copies = [pltpu.make_async_copy(a, b, sems.at[i]) for i, (a, b) in enumerate(zip(sources, targets))]
    for copy in copies:
        copy.start()
    for copy in copies:
        copy.wait()


def first_kernel(*refs):
    own, other, *masks = refs[: 2 + NEAR]
    forward_y, forward_z, *tables_in = refs[2 + NEAR : 7 + NEAR]
    spectra, point, taus, total, *tables, direction, rest, kept, sems = refs[7 + NEAR :]
    backward_y, backward_z, order = tables
    copies = [pltpu.make_async_copy(a, b, sems.at[i]) for i, (a, b) in enumerate(zip(tables_in, tables))]
    step = pl.program_id(0)
    t, core = lax.axis_index("ti"), lax.axis_index("kz") & 1

    def prepare():
        for copy in copies:
            copy.start()
        total[...] = jnp.zeros_like(total)
        unpack(own, core, point, direction, rest)
        unpack(other, 1 - core, point, direction, rest)
        unpack_rest(direction, rest)

    def bin_time(n):
        along_z, along_x = STEPS[n]
        bin_of = (((t >> 2) + along_z) & 3) * 4 + ((t + along_x) & 3)
        block = rest[1, pl.ds(pl.multiple_of(bin_of * 8, 8), 8), :]
        chosen = (iota((8, LANES), 0) == 0) & (iota((8, LANES), 1) == 64 + core)
        tau = jnp.sum(jnp.where(chosen, block, 0.0), axis=(0, 1), keepdims=True)
        taus[n] = jnp.broadcast_to(tau, (8, LANES))
        return tau

    for first in range(0, BINS, 2):

        @pl.when(step == first // 2)
        def _():
            if first == 0:
                prepare()
            done = []
            for n in (first, first + 1):
                tau = bin_time(n)
                spectrum = kept.at[n & 1] if n < NEAR else spectra.at[n - NEAR]
                done.append((n, tau, spectrum, forward_bin(tau, point, direction, forward_y, forward_z, spectrum)))
            if first == 0:
                for copy in copies:
                    copy.wait()
            for n, tau, spectrum, terms in done:
                if n < NEAR:
                    backward_bin(tau, *terms, masks[n][...], spectrum, point, backward_y, backward_z, order, total)


def second_kernel(mask, spectra, point, taus, total_in, table_y, table_z, order, mine, theirs, total, sent, rest):
    core = lax.axis_index("kz") & 1
    total[...] = total_in[...]
    for n in range(NEAR, BINS):
        tau = taus[n, 0:1, 0:1]
        terms = model_terms(tau, point)
        backward_bin(tau, *terms, mask[n - NEAR], spectra.at[n - NEAR], point, table_y, table_z, order, total)
    pack_sums(core, total, sent, rest, mine, theirs)


def sums_kernel(received, direction, residual, applied_out, out_sums, applied, sems):
    lane = iota((8, LANES), 1)
    sums = [jnp.zeros((8, LANES), f32) for _ in range(4)]
    copies = []
    for u in range(TILES):
        sides = []
        for g in range(4):
            upper, lower = (received[pl.ds(8 * m * TILES + u, 8, stride=TILES), :] for m in pairs_of(g))
            sides.append(upper + lower)
        if u < MAIN:
            maps = sides[0] + sides[1] + sides[2] + sides[3]
        for g in range(4):
            d, r, value = direction[g, u], residual[g, u], sides[g]
            if u < MAIN:
                of_maps = lane < 3 * ZB
                if g == 0:
                    value = jnp.where(of_maps, maps, value)
                else:
                    d, r, value = (jnp.where(of_maps, 0.0, a) for a in (d, r, value))
            elif u == TILES - 1:
                d, r, value = (jnp.where(lane < 64, a, 0.0) for a in (d, r, value))
            q = value + regular_weight * d
            applied[u, g] = q
            for i, (a, b) in enumerate(((r, r), (d, q), (r, q), (q, q))):
                sums[i] = sums[i] + a * b
        if u % 6 == 5:
            part = pl.ds(u - 5, 6)
            copies.append(pltpu.make_async_copy(applied.at[part], applied_out.at[part], sems.at[u // 6]))
            copies[-1].start()
    line = jnp.zeros((1, LANES), f32)
    for i in range(4):
        value = jnp.sum(sums[i], axis=(0, 1), keepdims=True)
        line = jnp.where(iota((1, LANES), 1) == i, value, line)
    out_sums[...] = jnp.broadcast_to(line, (LANES, LANES))
    for copy in copies:
        copy.wait()


def native_kernel(
    dense_in, dir_coils, res_coils, maps_out, fields, dense, maps, stacked, turned, sems
):
    copies = [
        pltpu.make_async_copy(source.at[p], fields.at[pl.ds(first + 8 * p, 8)], sems.at[2 * i + p])
        for i, (source, first) in enumerate(((dir_coils, 16), (res_coils, 32)))
        for p in range(2)
    ]
    copies.append(pltpu.make_async_copy(dense_in, dense, sems.at[5]))
    copies[-1].start()
    for copy in copies[:-1]:
        copy.start()
    copies.pop().wait()
    for g in range(4):
        for j in range(MAIN):
            turned[g, pl.ds(j, 8, stride=YB), :] = dense[j, g]
        stacked[g, :LANES] = jnp.swapaxes(turned[g], 0, 1)
        for v in range(2):
            stacked[g, LANES + 8 * v : LANES + 8 * v + 8] = inner_transpose(dense[MAIN + v, g])
        for i, name in enumerate(names_of(g)):
            if name < 3 and g:
                continue
            block = jnp.swapaxes(stacked[g, i * ZB : (i + 1) * ZB], 0, 1).reshape(XS, YB, ZB)
            if name < 3:
                maps[name] = block
            else:
                fields[name - 3] = block
    copies.append(pltpu.make_async_copy(maps, maps_out, sems.at[4]))
    copies[-1].start()
    for copy in copies:
        copy.wait()


def step_kernel(sums, fields, app_maps, dir_maps, res_maps, *refs):
    outs, (maps, made_maps, made_coils, sems) = refs[:4], refs[4:]
    copies = [
        pltpu.make_async_copy(source, maps.at[i], sems.at[i])
        for i, source in enumerate((app_maps, dir_maps, res_maps))
    ]
    for copy in copies:
        copy.start()
    line = jnp.sum(sums[...], axis=0, keepdims=True)
    lane = iota((1, LANES), 1)
    old, curve, cross, square = (
        jnp.sum(jnp.where(lane == i, line, 0.0), axis=1, keepdims=True) for i in range(4)
    )
    size = old / curve
    new = old - 2.0 * size * cross + size * size * square
    ratio = (new / old).reshape(1, 1, 1)
    size = size.reshape(1, 1, 1)
    stores = []
    for first in range(0, 16, 4):
        for coil in range(first, first + 4):
            fresh = fields[32 + coil] - size * fields[coil]
            made_coils[0, coil] = fresh
            made_coils[1, coil] = fresh + ratio * fields[16 + coil]
        part, rows = first // 8, pl.ds(first % 8, 4)
        for i in range(2):
            stores.append(
                pltpu.make_async_copy(
                    made_coils.at[i, pl.ds(first, 4)], outs[1 + 2 * i].at[part, rows], sems.at[3 + len(stores)]
                )
            )
            stores[-1].start()
    for copy in copies:
        copy.wait()
    for f in range(3):
        fresh = maps[2, f] - size * maps[0, f]
        made_maps[0, f] = fresh
        made_maps[1, f] = fresh + ratio * maps[1, f]
    for i in range(2):
        stores.append(pltpu.make_async_copy(made_maps.at[i], outs[2 * i], sems.at[3 + len(stores)]))
        stores[-1].start()
    for copy in stores:
        copy.wait()


def struct(*shape):
    return jax.ShapeDtypeStruct(shape, f32)


HBM = pl.BlockSpec(memory_space=pltpu.HBM)
VMEM = pl.BlockSpec(memory_space=pltpu.VMEM)
SCRATCH_STACKED = pltpu.VMEM((4, 144, LANES), f32)
SCRATCH_TURNED = pltpu.VMEM((4, LANES, LANES), f32)


def params():
    return pltpu.CompilerParams(vmem_limit_bytes=VMEM_LIMIT)


def cost(micros):
    return pl.CostEstimate(flops=int(micros * 4e8), bytes_accessed=int(micros * 2e6), transcendentals=0)


def constant_block(shape):
    return pl.BlockSpec(shape, lambda s: (0,) * len(shape))


def in_hbm(*values):
    return tuple(pltpu.with_memory_space_constraint(value, pltpu.HBM) for value in values)


def in_vmem(*values):
    return tuple(pltpu.with_memory_space_constraint(value, pltpu.VMEM) for value in values)


def far(*shape):
    return pltpu.HBM(shape, f32)


def near(*shape):
    return pltpu.VMEM(shape, f32)


def core_swap(values):
    return lax.ppermute(values, "kz", [(i, i ^ 1) for i in range(8)])


def by_parity(values):
    groups = [[i for i in range(128) if i & 1 == c] for c in range(2)]
    messages = values.reshape(64, 1, values.shape[0] // 64 * LANES)
    return lax.all_to_all(messages, AXES, 0, 0, axis_index_groups=groups).reshape(values.shape)


def shards(
    point_maps,
    point_coils,
    direction_maps,
    direction_coils,
    residual_maps,
    residual_coils,
    inversion_times,
    sampling_mask,
):
    forward_y, forward_z, backward_y, backward_z, order = (jnp.asarray(table) for table in make_tables())
    dir_maps, dir_coils = jnp.swapaxes(direction_maps, 2, 3), jnp.swapaxes(direction_coils, 3, 4)
    res_maps, res_coils = jnp.swapaxes(residual_maps, 2, 3), jnp.swapaxes(residual_coils, 3, 4)
    pnt_maps = jnp.swapaxes(point_maps, 1, 2)
    pnt_coils = jnp.swapaxes(point_coils, 2, 3).reshape(2, 4, 2, ZB, XS, NY)

    send, dir_dense = pl.pallas_call(
        pack_kernel,
        out_shape=(
            far(64 * WHOLE, LANES),
            near(4, TILES, 8, LANES),
        ),
        in_specs=[HBM] * 5,
        out_specs=(HBM, VMEM),
        scratch_shapes=[
            pltpu.VMEM((64 * WHOLE, LANES), f32),
            pltpu.VMEM(dir_maps.shape, f32),
            pltpu.VMEM(dir_coils.shape, f32),
            pltpu.VMEM((ITEMS, 8, NY), f32),
            pltpu.VMEM((ITEMS, 4, 8, NY), f32),
            pltpu.SMEM((2,), f32),
            SCRATCH_STACKED,
            SCRATCH_TURNED,
            pltpu.SemaphoreType.DMA((37,)),
        ],
        compiler_params=params(),
        cost_estimate=cost(4),
        name="pack",
    )(*in_hbm(inversion_times, dir_maps, dir_coils, pnt_maps, pnt_coils))

    def densify(maps, coils):
        return pl.pallas_call(
            dense_kernel,
            out_shape=near(4, TILES, 8, LANES),
            in_specs=[HBM] * 2,
            out_specs=VMEM,
            scratch_shapes=[
                pltpu.VMEM(maps.shape, f32),
                pltpu.VMEM(coils.shape, f32),
                SCRATCH_STACKED,
                SCRATCH_TURNED,
                pltpu.SemaphoreType.DMA((2,)),
            ],
            compiler_params=params(),
            cost_estimate=cost(3),
            name="dense",
        )(*in_hbm(maps, coils))

    own_mask = lax.dynamic_index_in_dim(sampling_mask, lax.axis_index("kz") & 1, 0, keepdims=False)

    def from_ti(values, move):
        pairs = [((((i >> 2) + move[0]) & 3) * 4 + ((i + move[1]) & 3), i) for i in range(16)]
        return lax.ppermute(values, "ti", pairs)

    masks = [own_mask] + [from_ti(own_mask, move) for move in STEPS[1:NEAR]]
    send, *masks = lax.optimization_barrier((send, *masks))
    own = by_parity(send)
    res_dense = densify(*lax.optimization_barrier((res_maps, res_coils, dir_dense))[:2])
    stack = jnp.stack(masks[1:4])
    own, res_dense, stack = lax.optimization_barrier((own, res_dense, stack))
    other = core_swap(own)
    far_masks = from_ti(stack, STEPS[3])
    planes = (2, FEATURES * NZ, LANES)
    tables = (forward_y, forward_z, backward_y, backward_z, order)
    sums_shape = struct(64 * TILES, LANES)
    sent_scratch = pltpu.VMEM((2, 64 * TILES, LANES), f32)
    near_tables = in_vmem(
        *pl.pallas_call(
            tables_kernel,
            out_shape=[pltpu.VMEM(table.shape, bf16) for table in tables[:2]],
            in_specs=[pl.BlockSpec(memory_space=pl.ANY)] + [HBM] * 2,
            out_specs=[VMEM] * 2,
            scratch_shapes=[pltpu.SemaphoreType.DMA((2,))],
            compiler_params=params(),
            cost_estimate=cost(1),
            name="tables",
        )(own, *in_hbm(*tables[:2]))
    )
    spectra, point, taus, total, *back_tables = pl.pallas_call(
        first_kernel,
        grid=(BINS // 2,),
        out_shape=(
            near(BINS - NEAR, 2, 2, NZ, NY),
            near(*planes),
            near(BINS, 8, LANES),
            near(*planes),
            *[pltpu.VMEM(table.shape, bf16) for table in tables[2:]],
        ),
        in_specs=[constant_block(own.shape)] * 2
        + [constant_block((NZ, NY))] * NEAR
        + [VMEM] * 2
        + [HBM] * 3,
        out_specs=(
            constant_block((BINS - NEAR, 2, 2, NZ, NY)),
            constant_block(planes),
            constant_block((BINS, 8, LANES)),
            constant_block(planes),
            *[VMEM] * 3,
        ),
        scratch_shapes=[
            pltpu.VMEM(planes, f32),
            pltpu.VMEM((2, LANES, LANES), f32),
            pltpu.VMEM((2, 2, 2, NZ, NY), f32),
            pltpu.SemaphoreType.DMA((3,)),
        ],
        compiler_params=params(),
        cost_estimate=cost(15),
        name="first",
    )(own, other, *masks, *near_tables, *in_hbm(*tables[2:]))

    mine, theirs = pl.pallas_call(
        second_kernel,
        out_shape=(sums_shape, sums_shape),
        in_specs=[VMEM] * 8,
        out_specs=(VMEM, VMEM),
        scratch_shapes=[
            pltpu.VMEM(planes, f32),
            sent_scratch,
            pltpu.VMEM((2, LANES, LANES), f32),
        ],
        compiler_params=params(),
        cost_estimate=cost(4),
        name="second",
    )(far_masks, *in_vmem(spectra, point, taus, total, *back_tables))

    received = by_parity(mine + core_swap(theirs))
    app_dense, sums = pl.pallas_call(
        sums_kernel,
        out_shape=(far(TILES, 4, 8, LANES), near(128, LANES)),
        in_specs=[VMEM] * 3,
        out_specs=(HBM, VMEM),
        scratch_shapes=[pltpu.VMEM((TILES, 4, 8, LANES), f32), pltpu.SemaphoreType.DMA((3,))],
        compiler_params=params(),
        cost_estimate=cost(1),
        name="sums",
    )(received, *in_vmem(dir_dense, res_dense))
    all_sums = lax.all_to_all(sums.reshape(128, 1, LANES), AXES, 0, 0).reshape(128, LANES)

    maps_shape, coils_shape = far(*dir_maps.shape), far(*dir_coils.shape)
    app_maps, fields = pl.pallas_call(
        native_kernel,
        out_shape=(far(*dir_maps.shape), near(48, XS, YB, ZB)),
        in_specs=[HBM] * 3,
        out_specs=(HBM, VMEM),
        scratch_shapes=[
            pltpu.VMEM((TILES, 4, 8, LANES), f32),
            pltpu.VMEM(dir_maps.shape, f32),
            SCRATCH_STACKED,
            SCRATCH_TURNED,
            pltpu.SemaphoreType.DMA((6,)),
        ],
        compiler_params=params(),
        cost_estimate=cost(3),
        name="native",
    )(*in_hbm(app_dense, dir_coils, res_coils))

    outs = pl.pallas_call(
        step_kernel,
        out_shape=(maps_shape, coils_shape, maps_shape, coils_shape),
        in_specs=[VMEM] * 2 + [HBM] * 3,
        out_specs=(HBM,) * 4,
        scratch_shapes=[
            pltpu.VMEM((3,) + dir_maps.shape, f32),
            pltpu.VMEM((2,) + dir_maps.shape, f32),
            pltpu.VMEM((2, 16, XS, YB, ZB), f32),
            pltpu.SemaphoreType.DMA((13,)),
        ],
        compiler_params=params(),
        cost_estimate=cost(2),
        name="step",
    )(all_sums, *in_vmem(fields), *in_hbm(app_maps, dir_maps, res_maps))
    return tuple(jnp.swapaxes(out, -2, -1) for out in outs)


def solution(mesh):
    in_specs = (
        P(None, None, "kz", None),
        P(None, None, None, "kz", None),
        P(None, None, "kz", "ti"),
        P(None, None, None, "kz", "ti"),
        P(None, None, "kz", "ti"),
        P(None, None, None, "kz", "ti"),
        P("ti"),
        P("ti", None, None),
    )
    out_specs = (
        P(None, None, "kz", "ti"),
        P(None, None, None, "kz", "ti"),
        P(None, None, "kz", "ti"),
        P(None, None, None, "kz", "ti"),
    )
    return jax.shard_map(shards, mesh=mesh, in_specs=in_specs, out_specs=out_specs, check_vma=False)
```
